128 devices in a mesh: gx: 16 (over z, x), gy: 8 (over y, core).
Axes of the slice: x: 4, y: 4, z: 4, core: 2. Of those that a mesh axis runs over, the one named last changes fastest.
Arguments:
- band_phi: float32 [256, 1024, 128], P('gx', 'gy'), may hold values from -8 to 8
- band_seed: float32 [256, 1024, 128], P('gx', 'gy'), may hold values from -6 to 6
- owner_map: int32 [256, 8], P('gx', 'gy'), may hold values from 0 to 15, as said below
- active_list: int32 [256, 8], P('gx', 'gy'), may hold values from 0 to 63, as said below
- brick_phi: float32 [1024, 1024, 128], P('gx', 'gy'), may hold values from -12 to 12
- adjoint_vel: float32 [1024, 1024, 128], P('gx', 'gy'), may hold values from -6 to 6
- upwind_flags: int32 [1024, 1024, 128], P('gx', 'gy'), may hold values from 0 to 7
Outputs:
- adjoint_out: float32 [1024, 1024, 128], P('gx', 'gy')
The draws below stay inside these ranges and needn't reach their ends.
Inputs may be any that keep to these rules, and one draw needn't show every extreme that they name: `owner_map`: among the 16 blocks of one device (aligned rows of one column), no home index appears more than 2 times; in every draw one home index of each column appears exactly 2 times in every device's rows of that column. `active_list`: blocks of one column with the same home index cover distinct slabs.
All inputs are finite; a program needn't handle non-finite values.
Results may differ from the reference program's by a relative error of at most 0.00005.
Values sent between devices are 32-bit elements; how exact they have to be, the bound alone decides.
No kernel may reach another device: no remote copies, remote signals or barrier semaphores. Data moves between devices by JAX's collectives and lax.ppermute only.
A program may use at most 128 MiB of HBM per device.

```python
import jax
import jax.numpy as jnp

CX = 64
CY = 128
BE = 128
OWN_SLOTS = 16
CAP = 2
REINIT = 4
MOM = 2
NXG = 1024
NYG = 1024
BLOCKS = 256
N_GX = 16
N_GY = 8


def block_plan(key):

    def one_column(column_key):
        pick_key, owner_key, slab_key = jax.random.split(column_key, 3)
        busiest = jax.random.randint(pick_key, (), 0, N_GX).astype(jnp.int32)

        def owner_rows(row_key):
            first_key, second_key = jax.random.split(row_key)
            others = (busiest + 1 + jnp.arange((N_GX - 1) * CAP, dtype=jnp.int32) // CAP) % N_GX
            others = jax.random.permutation(first_key, others)[:OWN_SLOTS - CAP].astype(jnp.int32)
            row_homes = jnp.concatenate([jnp.full((CAP,), busiest, jnp.int32), others])
            return jax.random.permutation(second_key, row_homes)
        home_index = jax.vmap(owner_rows)(jax.random.split(owner_key, N_GX)).reshape(N_GX * OWN_SLOTS)
        matches = (home_index[:, None] == jnp.arange(N_GX, dtype=jnp.int32)[None, :]).astype(jnp.int32)
        ranks = jnp.sum((jnp.cumsum(matches, axis=0) - matches) * matches, axis=1)

        def slab_order(order_key):
            rest = jax.random.permutation(order_key, CX - 1).astype(jnp.int32)
            return jnp.concatenate([jnp.full((1,), CX - 1, jnp.int32), rest])
        orders = jax.vmap(slab_order)(jax.random.split(slab_key, N_GX))
        slab_ids = orders[home_index, ranks]
        return (home_index, slab_ids)
    home_index, slab_ids = jax.vmap(one_column)(jax.random.split(key, N_GY))
    return (home_index.T.astype(jnp.int32), slab_ids.T.astype(jnp.int32))


def draw_owner_map(key, part):
    home_index, slab_ids = block_plan(key)
    return home_index


def draw_active_list(key, part):
    home_index, slab_ids = block_plan(key)
    return slab_ids


def touch_ends(array, stream_key, smallest, high):
    index_at = [jax.random.randint(jax.random.fold_in(stream_key, axis), (), 0, length) for axis, length in enumerate(array.shape)]
    main_axis = array.shape.index(max(array.shape))
    next_to = index_at[:main_axis] + [(index_at[main_axis] + 1) % array.shape[main_axis]] + index_at[main_axis + 1:]
    return array.at[tuple(index_at)].set(smallest).at[tuple(next_to)].set(high)


def block_scale(key, shape, shards, least, top_value):
    def one(dim, shards_of):
        draws = jax.random.uniform(jax.random.fold_in(jax.random.fold_in(key, 6), dim), (shards_of,), jnp.float32, least / len(shards), top_value / len(shards))
        return jnp.repeat(jnp.exp(draws), shape[dim] // shards_of).reshape((-1,) + (1,) * (len(shape) - dim - 1))

    level = one(*shards[0])
    for cut in shards[1:]:
        level = level * one(*cut)
    return level


def noise(own_key, shape, deviation, bound, cuts=(), held_as=jnp.bfloat16):
    values = jax.random.normal(own_key, shape, jnp.float32) * deviation
    if len(cuts) > 0:
        values = block_scale(own_key, shape, cuts, -0.22, 0.18) * values
    return jnp.clip(values, min=-bound, max=bound).astype(held_as)


def setup_inputs(seed: int = 0) -> dict:
    key_list = jax.random.split(jax.random.key(seed), 8)
    band_phi = noise(key_list[0], (BLOCKS, NYG, BE), 2.0, 8.0, ((0, 16), (1, 8)), jnp.float32)
    band_seed = noise(key_list[1], (BLOCKS, NYG, BE), 1.0, 6.0, ((0, 16), (1, 8)), jnp.float32)
    owner_map = draw_owner_map(jax.random.fold_in(key_list[7], 71), 0)
    active_list = draw_active_list(jax.random.fold_in(key_list[7], 71), 0)
    brick_phi = noise(key_list[4], (NXG, NYG, BE), 3.0, 12.0, ((0, 16), (1, 8)), jnp.float32)
    adjoint_vel = noise(key_list[5], (NXG, NYG, BE), 1.0, 6.0, ((0, 16), (1, 8)), jnp.float32)
    upwind_flags = touch_ends(jax.random.randint(key_list[6], (NXG, NYG, BE), 0, 8), jax.random.fold_in(key_list[6], 1), 0, 7).astype(jnp.int32)
    return {"band_phi": band_phi, "band_seed": band_seed, "owner_map": owner_map, "active_list": active_list, "brick_phi": brick_phi, "adjoint_vel": adjoint_vel, "upwind_flags": upwind_flags}


REINIT_STEP = 0.4
ADV_RATE = 0.25
DIFFUSION = 0.1
AIR_DENSITY = 0.3
SMEAR_WIDTH = 1.5

def reinit_adjoint(level_rows, seed_rows):
    leading = ((0, 0),) * (level_rows.ndim - 2)
    extended = jnp.pad(level_rows, leading + ((1, 1), (1, 1)), mode='edge')
    grad_y = 0.5 * (extended[..., 2:, 1:-1] - extended[..., :-2, 1:-1])
    grad_z = 0.5 * (extended[..., 1:-1, 2:] - extended[..., 1:-1, :-2])
    normal = jnp.sqrt(grad_y * grad_y + grad_z * grad_z + 1.0)
    smooth_sign = level_rows / jnp.sqrt(level_rows * level_rows + 1.0)
    weight_y = smooth_sign * grad_y / normal
    weight_z = smooth_sign * grad_z / normal
    adjoint = seed_rows
    for repeat in range(REINIT):
        flux_y = jnp.pad(weight_y * adjoint, leading + ((1, 1), (0, 0)))
        flux_z = jnp.pad(weight_z * adjoint, leading + ((0, 0), (1, 1)))
        adjoint = adjoint + REINIT_STEP * (0.5 * (flux_y[..., 2:, :] - flux_y[..., :-2, :]) + 0.5 * (flux_z[..., :, 2:] - flux_z[..., :, :-2]))
    return adjoint

def momentum_update(adjoint_field, padded, upwind_x, upwind_y, upwind_z, advect_rate, forcing):
    lower_x = padded[:-2, 1:-1]
    upper_x = padded[2:, 1:-1]
    lower_y = padded[1:-1, :-2]
    upper_y = padded[1:-1, 2:]
    padded_z = jnp.pad(adjoint_field, ((0, 0), (0, 0), (1, 1)))
    lower_z = padded_z[:, :, :-2]
    upper_z = padded_z[:, :, 2:]
    upwind = jnp.where(upwind_x == 1, lower_x, upper_x) + jnp.where(upwind_y == 1, lower_y, upper_y) + jnp.where(upwind_z == 1, lower_z, upper_z)
    advection = 3.0 * adjoint_field - upwind
    laplace = lower_x + upper_x + lower_y + upper_y + lower_z + upper_z - 6.0 * adjoint_field
    return adjoint_field - advect_rate * advection + DIFFUSION * laplace + forcing

def reference(band_phi, band_seed, owner_map, active_list, brick_phi, adjoint_vel, upwind_flags):
    block_count = band_phi.shape[0]
    depth = band_phi.shape[2]
    levels = band_phi.reshape(block_count, N_GY, CY, depth)
    seeds = band_seed.reshape(block_count, N_GY, CY, depth)
    result = reinit_adjoint(levels, seeds)
    brick_rows = (owner_map * CX + active_list).astype(jnp.int32)
    brick_cols = jnp.broadcast_to(jnp.arange(N_GY, dtype=jnp.int32)[None, :], brick_rows.shape)
    full_shape = (N_GX * CX, N_GY, CY, depth)
    source_field = jnp.zeros(full_shape, jnp.float32).at[brick_rows, brick_cols].set(result)
    level_band = jnp.zeros(full_shape, jnp.float32).at[brick_rows, brick_cols].set(levels)
    covered = jnp.zeros((N_GX * CX, N_GY), jnp.float32).at[brick_rows, brick_cols].set(1.0)
    covered = jnp.broadcast_to(covered[:, :, None, None], full_shape)
    grid_shape = brick_phi.shape
    source_field = source_field.reshape(grid_shape)
    level_band = level_band.reshape(grid_shape)
    covered = covered.reshape(grid_shape)
    level_set = jnp.where(covered > 0.5, level_band, brick_phi)
    heaviside = jnp.tanh(level_set / SMEAR_WIDTH)
    density = AIR_DENSITY + (1.0 - AIR_DENSITY) * 0.5 * (1.0 + heaviside)
    forcing = source_field * (0.5 / SMEAR_WIDTH * (1.0 - heaviside * heaviside))
    advect_rate = ADV_RATE / density
    upwind_x = upwind_flags % 2
    upwind_y = upwind_flags // 2 % 2
    upwind_z = upwind_flags // 4 % 2
    adjoint_field = adjoint_vel
    for repeat in range(MOM):
        padded = jnp.pad(adjoint_field, ((1, 1), (1, 1), (0, 0)))
        adjoint_field = momentum_update(adjoint_field, padded, upwind_x, upwind_y, upwind_z, advect_rate, forcing)
    return adjoint_field
```

```python
import jax
import jax.numpy as jnp
from jax import lax
from jax.experimental import pallas as pl
from jax.experimental.pallas import tpu as pltpu
from jax.sharding import PartitionSpec as P

CAP = 2
REINIT = 4
REINIT_STEP = 0.4
ADV_RATE = 0.25
DIFFUSION = 0.1
AIR_DENSITY = 0.3
SMEAR_WIDTH = 1.5

F32 = jnp.float32
I32 = jnp.int32
MIB = 1 << 20
HBM = pl.BlockSpec(memory_space=pltpu.HBM)
VMEM = pl.BlockSpec(memory_space=pltpu.VMEM)
SMEM = pl.BlockSpec(memory_space=pltpu.SMEM)
EXTRA = 8
PAD = 8
CHUNK = 8
STRIP = 32
UNROLL = 4
REINIT_UNROLL = 2


def params(mib):
    return pltpu.CompilerParams(vmem_limit_bytes=mib * MIB)


def cost(mib, flops):
    return pl.CostEstimate(flops=flops, bytes_accessed=mib * MIB, transcendentals=0)


def homes_and_ranks(owner_ref, count_ref):
    for home in range(count_ref.shape[0]):
        count_ref[home] = 0
    result = []
    for slot in range(owner_ref.shape[1]):
        home = owner_ref[0, slot]
        rank = count_ref[home]
        count_ref[home] = rank + 1
        result.append((home, rank))
    return result


def pack_level_kernel(owner_ref, slab_ref, phi_ref, out_ref, tags, count_ref, sem, tag_sem):
    slots, rows, lanes = phi_ref.shape
    tags[...] = jnp.zeros_like(tags)
    copies = []
    for slot, (home, rank) in enumerate(homes_and_ranks(owner_ref, count_ref)):
        copy = pltpu.make_async_copy(
            phi_ref.at[slot],
            out_ref.at[home, pl.ds(pl.multiple_of(rank * rows, rows), rows)],
            sem.at[slot],
        )
        copy.start()
        copies.append(copy)
        label = (slab_ref[0, slot] + 1).astype(F32)
        tags[home, pl.ds(rank, 1), :] = jnp.full((1, lanes), label, F32)
    copy = pltpu.make_async_copy(tags, out_ref.at[:, pl.ds(CAP * rows, EXTRA)], tag_sem)
    copy.start()
    copies.append(copy)
    for copy in copies:
        copy.wait()


def shift_rows(values, step, row):
    rows = values.shape[0]
    moved = pltpu.roll(values, step % rows, 0)
    return jnp.where(row == (0 if step == 1 else rows - 1), 0.0, moved)


def shift_lanes(values, step, lane):
    lanes = values.shape[1]
    moved = pltpu.roll(values, step % lanes, 1)
    return jnp.where(lane == (0 if step == 1 else lanes - 1), 0.0, moved)


def reinit_kernel(
    owner_ref, phi_ref, seed_ref, out_ref, low_ref, high_ref, hold, count_ref, place_ref, sem
):
    slots, rows, lanes = phi_ref.shape
    for slot, (home, rank) in enumerate(homes_and_ranks(owner_ref, count_ref)):
        place_ref[slot] = home * CAP + rank
    row = lax.broadcasted_iota(I32, (rows, lanes), 0)
    lane = lax.broadcasted_iota(I32, (rows, lanes), 1)
    low_ref[...] = jnp.zeros_like(low_ref)
    high_ref[...] = jnp.zeros_like(high_ref)

    def out_copy(slot):
        place = place_ref[slot]
        return pltpu.make_async_copy(
            hold.at[slot],
            out_ref.at[place // CAP, pl.ds(pl.multiple_of((place % CAP) * rows, rows), rows)],
            sem.at[slot],
        )

    def block(slot):
        phi = phi_ref[slot]
        up_y = jnp.where(row == rows - 1, phi, pltpu.roll(phi, rows - 1, 0))
        low_y = jnp.where(row == 0, phi, pltpu.roll(phi, 1, 0))
        up_z = jnp.where(lane == lanes - 1, phi, pltpu.roll(phi, lanes - 1, 1))
        low_z = jnp.where(lane == 0, phi, pltpu.roll(phi, 1, 1))
        grad_y = 0.5 * (up_y - low_y)
        grad_z = 0.5 * (up_z - low_z)
        normal = jnp.sqrt(grad_y * grad_y + grad_z * grad_z + 1.0)
        sign = phi / jnp.sqrt(phi * phi + 1.0)
        scale = (0.5 * REINIT_STEP) * sign / normal
        weight_y = scale * grad_y
        weight_z = scale * grad_z
        adjoint = seed_ref[slot]
        for _ in range(REINIT):
            flux_y = weight_y * adjoint
            flux_z = weight_z * adjoint
            adjoint = adjoint + (
                (shift_rows(flux_y, -1, row) - shift_rows(flux_y, 1, row))
                + (shift_lanes(flux_z, -1, lane) - shift_lanes(flux_z, 1, lane))
            )
        heaviside = jnp.tanh(phi / SMEAR_WIDTH)
        hold[slot] = adjoint * (0.5 / SMEAR_WIDTH * (1.0 - heaviside * heaviside))

    def body(step, carry):
        for j in range(REINIT_UNROLL):
            block(step * REINIT_UNROLL + j)
        for j in range(REINIT_UNROLL):
            slot = step * REINIT_UNROLL + j
            out_copy(slot).start()
            place = place_ref[slot]
            home, rank = place // CAP, place % CAP
            high_ref[home, pl.ds(rank, 1), :] = hold[slot, rows - 1 : rows, :]
            low_ref[home, pl.ds(CAP + rank, 1), :] = hold[slot, 0:1, :]
        return carry

    lax.fori_loop(0, slots // REINIT_UNROLL, body, 0)
    for slot in range(slots):
        out_copy(slot).wait()


def pack_lines_kernel(below_ref, above_ref, forcing_ref, out_ref, hold, sem):
    hold[...] = below_ref[...] + above_ref[...]
    copy = pltpu.make_async_copy(
        hold, out_ref.at[:, pl.ds(out_ref.shape[1] - EXTRA, EXTRA)], sem
    )
    copy.start()
    copy.wait()


def neighbours(buffer, x, first, rows, lane):
    here = buffer[x + 1, pl.ds(PAD + first, rows), :]
    low_x = buffer[x, pl.ds(PAD + first, rows), :]
    up_x = buffer[x + 2, pl.ds(PAD + first, rows), :]
    low_y = buffer[x + 1, pl.ds(PAD + first - 1, rows), :]
    up_y = buffer[x + 1, pl.ds(PAD + first + 1, rows), :]
    low_z = shift_lanes(here, 1, lane)
    up_z = shift_lanes(here, -1, lane)
    return here, low_x, up_x, low_y, up_y, low_z, up_z


def operator(fields, flags, rate):
    here, low_x, up_x, low_y, up_y, low_z, up_z = fields
    upwind = (
        jnp.where((flags & 1) != 0, low_x, up_x)
        + jnp.where((flags & 2) != 0, low_y, up_y)
        + jnp.where((flags & 4) != 0, low_z, up_z)
    )
    total = (low_x + up_x) + (low_y + up_y) + (low_z + up_z)
    return (1.0 - 6.0 * DIFFUSION) * here + rate * (upwind - 3.0 * here) + DIFFUSION * total


def by_rows(first, last, body):
    def step(i, carry):
        for j in range(UNROLL):
            body(first + i * UNROLL + j)
        return carry

    lax.fori_loop(0, (last - first) // UNROLL, step, 0)


def first_kernel(
    tag_ref, vel_ref, flags, phi_ref, level_ref, xlow_ref, xhigh_ref, ylow_ref, yhigh_ref,
    rate, twice, edge_x_ref, edge_ylow_ref, edge_yhigh_ref, coef_ref, table_ref,
    vel, once, sem_vel, sem_phi,
):
    cells, rows, lanes = flags.shape
    chunks = cells // CHUNK

    def vel_copy(c):
        return pltpu.make_async_copy(
            vel_ref.at[pl.ds(c * CHUNK, CHUNK)],
            vel.at[pl.ds(1 + c * CHUNK, CHUNK), pl.ds(PAD, rows)],
            sem_vel.at[c],
        )

    def phi_copy(x):
        return pltpu.make_async_copy(phi_ref.at[x], rate.at[x], sem_phi.at[x])

    for c in range(chunks):
        vel_copy(c).start()
    for x in range(cells):
        table_ref[x] = -1
    for source in range(tag_ref.shape[0]):
        for rank in range(CAP):
            tag = tag_ref[source, rank]

            @pl.when(tag > 0)
            def _():
                table_ref[tag - 1] = source * CAP + rank

    def start_phi(x, carry):
        slot = table_ref[x]

        @pl.when(slot >= 0)
        def _():
            pltpu.make_async_copy(
                block_of(level_ref, slot, rows), rate.at[x], sem_phi.at[x]
            ).start()

        @pl.when(slot < 0)
        def _():
            phi_copy(x).start()

        return carry

    lax.fori_loop(0, cells, start_phi, 0)

    lane = lax.broadcasted_iota(I32, (STRIP, lanes), 1)
    zeros = jnp.zeros((rows + 2 * PAD, lanes), F32)
    vel[0, pl.ds(PAD, rows), :] = xlow_ref[0]
    vel[cells + 1, pl.ds(PAD, rows), :] = xhigh_ref[0]
    once[0] = zeros
    once[cells + 1] = zeros
    line_zero = jnp.zeros((PAD, lanes), F32)

    def lines(x):
        vel[x + 1, PAD - 1 : PAD, :] = ylow_ref[pl.ds(x, 1), :]
        vel[x + 1, PAD + rows : PAD + rows + 1, :] = yhigh_ref[pl.ds(x, 1), :]
        once[x + 1, 0:PAD, :] = line_zero
        once[x + 1, PAD + rows : PAD + rows + PAD, :] = line_zero
        slot = jnp.full((1, lanes), table_ref[x].astype(F32), F32)
        edge_ylow_ref[pl.ds(cells + x, 1), :] = slot
        edge_yhigh_ref[pl.ds(cells + x, 1), :] = slot

    by_rows(0, cells, lines)

    def update_once(x):
        for first in range(0, rows, STRIP):
            part = pl.ds(first, STRIP)
            heaviside = jnp.tanh(rate[x, part, :] * (1.0 / SMEAR_WIDTH))
            density = (AIR_DENSITY + 0.5 * (1.0 - AIR_DENSITY)) + (0.5 * (1.0 - AIR_DENSITY)) * heaviside
            rate_here = ADV_RATE / density
            rate[x, part, :] = rate_here
            once[x + 1, pl.ds(PAD + first, STRIP), :] = operator(
                neighbours(vel, x, first, STRIP, lane), flags[x, part, :], rate_here
            )

    def update_twice(x):
        for first in range(0, rows, STRIP):
            part = pl.ds(first, STRIP)
            twice[x, part, :] = operator(
                neighbours(once, x, first, STRIP, lane), flags[x, part, :], rate[x, part, :]
            )

    vel_copy(0).wait()
    for c in range(chunks):
        if c + 1 < chunks:
            vel_copy(c + 1).wait()
        for x in range(c * CHUNK, (c + 1) * CHUNK):
            phi_copy(x).wait()
        by_rows(c * CHUNK, (c + 1) * CHUNK, update_once)
    by_rows(0, cells, update_twice)

    edge_x_ref[0] = once[1, pl.ds(PAD, rows), :]
    edge_x_ref[1] = once[cells, pl.ds(PAD, rows), :]
    coef_ref[0] = DIFFUSION + jnp.where((flags[0] & 1) != 0, rate[0], 0.0)
    coef_ref[1] = DIFFUSION + jnp.where((flags[cells - 1] & 1) != 0, 0.0, rate[cells - 1])

    def edge_lines(x):
        edge_ylow_ref[pl.ds(x, 1), :] = once[x + 1, PAD : PAD + 1, :]
        edge_yhigh_ref[pl.ds(x, 1), :] = once[x + 1, PAD + rows - 1 : PAD + rows, :]

    by_rows(0, cells, edge_lines)


def block_of(ref, slot, rows):
    return ref.at[slot // CAP, pl.ds(pl.multiple_of((slot % CAP) * rows, rows), rows)]


def edge_kernel(table_ref, edge_ref, forcing_ref, low_out, high_out):
    rows = low_out.shape[1]
    for side, (x, out) in enumerate(((0, low_out), (table_ref.shape[0] - 1, high_out))):
        slot = table_ref[x]

        @pl.when(slot >= 0)
        def _():
            out[0] = edge_ref[side] + block_of(forcing_ref, slot, rows)[...]

        @pl.when(slot < 0)
        def _():
            out[0] = edge_ref[side]


def last_kernel(
    table_ref, below_ref, above_ref, forcing_ref, rate, flags, twice, ylow_ref, yhigh_ref,
    out_ref, part_ref, source, out, sem_out,
):
    cells, rows, lanes = flags.shape
    chunks = cells // CHUNK
    zeros = jnp.zeros((rows, lanes), F32)
    source[0, pl.ds(PAD, rows), :] = zeros
    source[cells + 1, pl.ds(PAD, rows), :] = zeros

    def fill(x, carry):
        slot = table_ref[x]

        @pl.when(slot >= 0)
        def _():
            source[x + 1, pl.ds(PAD, rows), :] = block_of(forcing_ref, slot, rows)[...]

        @pl.when(slot < 0)
        def _():
            source[x + 1, pl.ds(PAD, rows), :] = zeros

        for side, slots, halo, at in (
            (0, below_ref, ylow_ref, PAD - 1),
            (1, above_ref, yhigh_ref, PAD + rows),
        ):
            line_slot = slots[x]
            safe = jnp.maximum(line_slot, 0)
            line = forcing_ref[safe // CAP, pl.ds(CAP * rows + side * CAP + safe % CAP, 1), :]
            source[x + 1, at : at + 1, :] = halo[pl.ds(x, 1), :] + jnp.where(
                line_slot >= 0, line, 0.0
            )
        return carry

    lane = lax.broadcasted_iota(I32, (STRIP, lanes), 1)

    def update(x):
        for first in range(0, rows, STRIP):
            part = pl.ds(first, STRIP)
            fields = neighbours(source, x, first, STRIP, lane)
            out[x, part, :] = (
                twice[x, part, :] + fields[0] + operator(fields, flags[x, part, :], rate[x, part, :])
            )

    def out_copy(c):
        first = 1 if c == 0 else c * CHUNK
        last = cells - 1 if c == chunks - 1 else (c + 1) * CHUNK
        part = pl.ds(first, last - first)
        return pltpu.make_async_copy(out.at[part], out_ref.at[part], sem_out.at[c])

    lax.fori_loop(0, cells, fill, 0)
    for c in range(chunks):
        by_rows(c * CHUNK, (c + 1) * CHUNK, update)
        out_copy(c).start()
    part_ref[0] = out[0]
    part_ref[1] = out[cells - 1]
    for c in range(chunks):
        out_copy(c).wait()


def close_kernel(part_ref, coef_ref, low_ref, high_ref, whole_ref, out_ref, hold, sem):
    cells = out_ref.shape[0]
    hold[0] = part_ref[0] + coef_ref[0] * low_ref[0]
    hold[1] = part_ref[1] + coef_ref[1] * high_ref[0]
    copies = [
        pltpu.make_async_copy(hold.at[0], out_ref.at[0], sem.at[0]),
        pltpu.make_async_copy(hold.at[1], out_ref.at[cells - 1], sem.at[1]),
    ]
    for copy in copies:
        copy.start()
    for copy in copies:
        copy.wait()


def neighbour_pairs(axis):
    count = lax.axis_size(axis)
    forward = [(i, i + 1) for i in range(count - 1)]
    return forward, [(target, source) for source, target in forward]


def local(band_phi, band_seed, owner_map, active_list, brick_phi, adjoint_vel, upwind_flags):
    gx_count = lax.axis_size("gx")
    slots, rows, lanes = band_phi.shape
    cells = brick_phi.shape[0]
    chunks = cells // CHUNK
    up_x, down_x = neighbour_pairs("gx")
    up_y, down_y = neighbour_pairs("gy")
    shape = jax.ShapeDtypeStruct
    dma = pltpu.SemaphoreType.DMA
    brick = (cells, rows, lanes)
    padded = (cells + 2, rows + 2 * PAD, lanes)
    sent = (gx_count, CAP * rows + EXTRA, lanes)
    owners, slabs = owner_map.T, active_list.T

    level_sent = pl.pallas_call(
        pack_level_kernel,
        out_shape=shape(sent, F32),
        in_specs=[SMEM, SMEM, VMEM],
        out_specs=HBM,
        scratch_shapes=[
            pltpu.VMEM((gx_count, EXTRA, lanes), F32),
            pltpu.SMEM((gx_count,), I32),
            dma((slots,)), dma(()),
        ],
        compiler_params=params(4),
        cost_estimate=cost(2, 1000),
        name="pack_level",
    )(owners, slabs, band_phi)
    level = lax.all_to_all(level_sent, "gx", split_axis=0, concat_axis=0, tiled=True)

    v_xlow = lax.ppermute(adjoint_vel[cells - 1 :], "gx", up_x)
    v_xhigh = lax.ppermute(adjoint_vel[:1], "gx", down_x)
    v_ylow = lax.ppermute(adjoint_vel[:, rows - 1], "gy", up_y)
    v_yhigh = lax.ppermute(adjoint_vel[:, 0], "gy", down_y)

    lines = (gx_count, EXTRA, lanes)
    forcing_sent, low_lines, high_lines = pl.pallas_call(
        reinit_kernel,
        out_shape=(shape(sent, F32), shape(lines, F32), shape(lines, F32)),
        in_specs=[SMEM, VMEM, VMEM],
        out_specs=(HBM, VMEM, VMEM),
        scratch_shapes=[
            pltpu.VMEM((slots, rows, lanes), F32),
            pltpu.SMEM((gx_count,), I32),
            pltpu.SMEM((slots,), I32),
            dma((slots,)),
        ],
        compiler_params=params(8),
        cost_estimate=cost(20, 40_000_000),
        name="reinit",
    )(owners, band_phi, band_seed)
    below_lines = lax.ppermute(high_lines, "gy", up_y)
    above_lines = lax.ppermute(low_lines, "gy", down_y)
    forcing_sent = pl.pallas_call(
        pack_lines_kernel,
        out_shape=shape(sent, F32),
        in_specs=[VMEM, VMEM, HBM],
        out_specs=HBM,
        scratch_shapes=[pltpu.VMEM(lines, F32), dma(())],
        input_output_aliases={2: 0},
        compiler_params=params(4),
        cost_estimate=cost(2, 1000),
        name="pack_lines",
    )(below_lines, above_lines, forcing_sent)
    forcing = lax.all_to_all(forcing_sent, "gx", split_axis=0, concat_axis=0, tiled=True)

    tags = level[:, CAP * rows : CAP * rows + CAP, 0].astype(I32)
    edge_lines = (2 * cells, lanes)
    rate, twice, edge_x, edge_ylow, edge_yhigh, coef, table = pl.pallas_call(
        first_kernel,
        out_shape=(
            shape(brick, F32),
            shape(brick, F32),
            shape((2, rows, lanes), F32),
            shape(edge_lines, F32),
            shape(edge_lines, F32),
            shape((2, rows, lanes), F32),
            shape((cells,), I32),
        ),
        in_specs=[SMEM, HBM, VMEM, HBM, HBM, VMEM, VMEM, VMEM, VMEM],
        out_specs=(VMEM, VMEM, VMEM, VMEM, VMEM, VMEM, SMEM),
        scratch_shapes=[
            pltpu.VMEM(padded, F32),
            pltpu.VMEM(padded, F32),
            dma((chunks,)), dma((cells,)),
        ],
        compiler_params=params(28),
        cost_estimate=cost(30, 60_000_000),
        name="two_updates",
    )(tags, adjoint_vel, upwind_flags, brick_phi, level, v_xlow, v_xhigh, v_ylow, v_yhigh)
    once_ylow = lax.ppermute(edge_yhigh, "gy", up_y)
    once_yhigh = lax.ppermute(edge_ylow, "gy", down_y)
    gy = lax.axis_index("gy")
    below = jnp.where(gy > 0, once_ylow[cells:, 0].astype(I32), -1)
    above = jnp.where(gy < lax.axis_size("gy") - 1, once_yhigh[cells:, 0].astype(I32), -1)

    low_slab, high_slab = pl.pallas_call(
        edge_kernel,
        out_shape=(shape((1, rows, lanes), F32), shape((1, rows, lanes), F32)),
        in_specs=[SMEM, VMEM, VMEM],
        out_specs=(VMEM, VMEM),
        compiler_params=params(8),
        cost_estimate=cost(1, 1000),
        name="edge_slabs",
    )(table, edge_x, forcing)
    from_low = lax.ppermute(high_slab, "gx", up_x)
    from_high = lax.ppermute(low_slab, "gx", down_x)

    out, part = pl.pallas_call(
        last_kernel,
        out_shape=(shape(brick, F32), shape((2, rows, lanes), F32)),
        in_specs=[SMEM, SMEM, SMEM, VMEM, VMEM, VMEM, VMEM, VMEM, VMEM],
        out_specs=(HBM, VMEM),
        scratch_shapes=[
            pltpu.VMEM(padded, F32),
            pltpu.VMEM(brick, F32),
            dma((chunks,)),
        ],
        compiler_params=params(28),
        cost_estimate=cost(30, 60_000_000),
        name="add_forcing",
    )(table, below, above, forcing, rate, upwind_flags, twice, once_ylow, once_yhigh)

    return pl.pallas_call(
        close_kernel,
        out_shape=shape(brick, F32),
        in_specs=[VMEM, VMEM, VMEM, VMEM, HBM],
        out_specs=HBM,
        scratch_shapes=[pltpu.VMEM((2, rows, lanes), F32), dma((2,))],
        input_output_aliases={4: 0},
        compiler_params=params(4),
        cost_estimate=cost(1, 1000),
        name="close_slabs",
    )(part, coef, from_low, from_high, out)


def solution(mesh):
    in_specs = (
        P("gx", "gy", None),
        P("gx", "gy", None),
        P("gx", "gy"),
        P("gx", "gy"),
        P("gx", "gy", None),
        P("gx", "gy", None),
        P("gx", "gy", None),
    )
    out_specs = P("gx", "gy", None)
    return jax.shard_map(local, mesh=mesh, in_specs=in_specs, out_specs=out_specs, check_vma=False)
```

```python
import jax
import jax.numpy as jnp
from jax import lax
from jax.experimental import pallas as pl
from jax.experimental.pallas import tpu as pltpu
from jax.sharding import PartitionSpec as P

CAP = 2
REINIT = 4
REINIT_STEP = 0.4
ADV_RATE = 0.25
DIFFUSION = 0.1
AIR_DENSITY = 0.3
SMEAR_WIDTH = 1.5

F32 = jnp.float32
I32 = jnp.int32
MIB = 1 << 20
HBM = pl.BlockSpec(memory_space=pltpu.HBM)
VMEM = pl.BlockSpec(memory_space=pltpu.VMEM)
SMEM = pl.BlockSpec(memory_space=pltpu.SMEM)
EXTRA = 8
PAD = 8
CHUNK = 8
STRIP = 32
UNROLL = 4
REINIT_UNROLL = 2


VMEM_MIB = 59


def params(mib):
    return pltpu.CompilerParams(vmem_limit_bytes=mib * MIB)


def cost(mib, flops):
    return pl.CostEstimate(flops=flops, bytes_accessed=mib * MIB, transcendentals=0)


def homes_and_ranks(owner_ref, count_ref):
    for home in range(count_ref.shape[0]):
        count_ref[home] = 0
    result = []
    for slot in range(owner_ref.shape[1]):
        home = owner_ref[0, slot]
        rank = count_ref[home]
        count_ref[home] = rank + 1
        result.append((home, rank))
    return result


def pack_level_kernel(
    owner_ref, slab_ref, phi_ref, out_ref, phi, tags, count_ref, load_sem, sem, tag_sem
):
    slots, rows, lanes = phi_ref.shape
    loads = [
        pltpu.make_async_copy(phi_ref.at[slot], phi.at[slot], load_sem.at[slot])
        for slot in range(slots)
    ]
    for load in loads:
        load.start()
    tags[...] = jnp.zeros_like(tags)
    places = homes_and_ranks(owner_ref, count_ref)
    for slot, (home, rank) in enumerate(places):
        label = (slab_ref[0, slot] + 1).astype(F32)
        tags[home, pl.ds(rank, 1), :] = jnp.full((1, lanes), label, F32)
    copies = [pltpu.make_async_copy(tags, out_ref.at[:, pl.ds(CAP * rows, EXTRA)], tag_sem)]
    copies[0].start()
    for slot, (home, rank) in enumerate(places):
        loads[slot].wait()
        copy = pltpu.make_async_copy(
            phi.at[slot],
            out_ref.at[home, pl.ds(pl.multiple_of(rank * rows, rows), rows)],
            sem.at[slot],
        )
        copy.start()
        copies.append(copy)
    for copy in copies:
        copy.wait()


def shift_rows(values, step, row):
    rows = values.shape[0]
    moved = pltpu.roll(values, step % rows, 0)
    return jnp.where(row == (0 if step == 1 else rows - 1), 0.0, moved)


def shift_lanes(values, step, lane):
    lanes = values.shape[1]
    moved = pltpu.roll(values, step % lanes, 1)
    return jnp.where(lane == (0 if step == 1 else lanes - 1), 0.0, moved)


def reinit_kernel(
    owner_ref, phi_hbm, seed_hbm, out_ref, low_ref, high_ref,
    phi_ref, seed_ref, hold, count_ref, place_ref, load_sem, sem,
):
    slots, rows, lanes = phi_ref.shape

    def load(step, which):
        part = pl.ds(step * REINIT_UNROLL, REINIT_UNROLL)
        src, dst = ((phi_hbm, phi_ref), (seed_hbm, seed_ref))[which]
        return pltpu.make_async_copy(src.at[part], dst.at[part], load_sem.at[which, step])

    for step in range(slots // REINIT_UNROLL):
        load(step, 0).start()
        load(step, 1).start()
    for slot, (home, rank) in enumerate(homes_and_ranks(owner_ref, count_ref)):
        place_ref[slot] = home * CAP + rank
    row = lax.broadcasted_iota(I32, (rows, lanes), 0)
    lane = lax.broadcasted_iota(I32, (rows, lanes), 1)
    low_ref[...] = jnp.zeros_like(low_ref)
    high_ref[...] = jnp.zeros_like(high_ref)

    def out_copy(slot):
        place = place_ref[slot]
        return pltpu.make_async_copy(
            hold.at[slot],
            out_ref.at[place // CAP, pl.ds(pl.multiple_of((place % CAP) * rows, rows), rows)],
            sem.at[slot],
        )

    def block(slot):
        phi = phi_ref[slot]
        up_y = jnp.where(row == rows - 1, phi, pltpu.roll(phi, rows - 1, 0))
        low_y = jnp.where(row == 0, phi, pltpu.roll(phi, 1, 0))
        up_z = jnp.where(lane == lanes - 1, phi, pltpu.roll(phi, lanes - 1, 1))
        low_z = jnp.where(lane == 0, phi, pltpu.roll(phi, 1, 1))
        grad_y = 0.5 * (up_y - low_y)
        grad_z = 0.5 * (up_z - low_z)
        normal = jnp.sqrt(grad_y * grad_y + grad_z * grad_z + 1.0)
        sign = phi / jnp.sqrt(phi * phi + 1.0)
        scale = (0.5 * REINIT_STEP) * sign / normal
        weight_y = scale * grad_y
        weight_z = scale * grad_z
        adjoint = seed_ref[slot]
        for _ in range(REINIT):
            flux_y = weight_y * adjoint
            flux_z = weight_z * adjoint
            adjoint = adjoint + (
                (shift_rows(flux_y, -1, row) - shift_rows(flux_y, 1, row))
                + (shift_lanes(flux_z, -1, lane) - shift_lanes(flux_z, 1, lane))
            )
        heaviside = jnp.tanh(phi / SMEAR_WIDTH)
        hold[slot] = adjoint * (0.5 / SMEAR_WIDTH * (1.0 - heaviside * heaviside))

    def body(step, carry):
        load(step, 0).wait()
        load(step, 1).wait()
        for j in range(REINIT_UNROLL):
            block(step * REINIT_UNROLL + j)
        for j in range(REINIT_UNROLL):
            slot = step * REINIT_UNROLL + j
            out_copy(slot).start()
            place = place_ref[slot]
            home, rank = place // CAP, place % CAP
            high_ref[home, pl.ds(rank, 1), :] = hold[slot, rows - 1 : rows, :]
            low_ref[home, pl.ds(CAP + rank, 1), :] = hold[slot, 0:1, :]
        return carry

    lax.fori_loop(0, slots // REINIT_UNROLL, body, 0)
    for slot in range(slots):
        out_copy(slot).wait()


def pack_lines_kernel(below_ref, above_ref, forcing_ref, out_ref, hold, sem):
    hold[...] = below_ref[...] + above_ref[...]
    copy = pltpu.make_async_copy(
        hold, out_ref.at[:, pl.ds(out_ref.shape[1] - EXTRA, EXTRA)], sem
    )
    copy.start()
    copy.wait()


def neighbours(buffer, x, first, rows, lane):
    here = buffer[x + 1, pl.ds(PAD + first, rows), :]
    low_x = buffer[x, pl.ds(PAD + first, rows), :]
    up_x = buffer[x + 2, pl.ds(PAD + first, rows), :]
    low_y = buffer[x + 1, pl.ds(PAD + first - 1, rows), :]
    up_y = buffer[x + 1, pl.ds(PAD + first + 1, rows), :]
    low_z = shift_lanes(here, 1, lane)
    up_z = shift_lanes(here, -1, lane)
    return here, low_x, up_x, low_y, up_y, low_z, up_z


def operator(fields, flags, rate):
    here, low_x, up_x, low_y, up_y, low_z, up_z = fields
    upwind = (
        jnp.where((flags & 1) != 0, low_x, up_x)
        + jnp.where((flags & 2) != 0, low_y, up_y)
        + jnp.where((flags & 4) != 0, low_z, up_z)
    )
    total = (low_x + up_x) + (low_y + up_y) + (low_z + up_z)
    return (1.0 - 6.0 * DIFFUSION) * here + rate * (upwind - 3.0 * here) + DIFFUSION * total


def by_rows(first, last, body):
    def step(i, carry):
        for j in range(UNROLL):
            body(first + i * UNROLL + j)
        return carry

    lax.fori_loop(0, (last - first) // UNROLL, step, 0)


def chunk_copy(src, dst, sem, c):
    part = pl.ds(c * CHUNK, CHUNK)
    return pltpu.make_async_copy(src.at[part], dst.at[part], sem.at[c])


def first_kernel(
    tag_ref, vel_ref, flags_ref, phi_ref, level_ref, xlow_ref, xhigh_ref, ylow_ref, yhigh_ref,
    rate_out, twice_out, edge_x_ref, edge_ylow_ref, edge_yhigh_ref, coef_ref, table_ref,
    vel, once, flags, rate, twice, sem_vel, sem_flags, sem_phi, sem_rate, sem_twice,
):
    cells, rows, lanes = flags.shape
    chunks = cells // CHUNK

    def vel_copy(c):
        return pltpu.make_async_copy(
            vel_ref.at[pl.ds(c * CHUNK, CHUNK)],
            vel.at[pl.ds(1 + c * CHUNK, CHUNK), pl.ds(PAD, rows)],
            sem_vel.at[c],
        )

    def phi_copy(x):
        return pltpu.make_async_copy(phi_ref.at[x], rate.at[x], sem_phi.at[x])

    def flags_copy(c):
        return chunk_copy(flags_ref, flags, sem_flags, c)

    def rate_copy(c):
        return chunk_copy(rate, rate_out, sem_rate, c)

    def twice_copy(c):
        return chunk_copy(twice, twice_out, sem_twice, c)

    for c in range(chunks):
        vel_copy(c).start()
        flags_copy(c).start()
    for x in range(cells):
        table_ref[x] = -1
    for source in range(tag_ref.shape[0]):
        for rank in range(CAP):
            tag = tag_ref[source, rank]

            @pl.when(tag > 0)
            def _():
                table_ref[tag - 1] = source * CAP + rank

    def start_phi(x, carry):
        slot = table_ref[x]

        @pl.when(slot >= 0)
        def _():
            pltpu.make_async_copy(
                block_of(level_ref, slot, rows), rate.at[x], sem_phi.at[x]
            ).start()

        @pl.when(slot < 0)
        def _():
            phi_copy(x).start()

        return carry

    lax.fori_loop(0, cells, start_phi, 0)

    lane = lax.broadcasted_iota(I32, (STRIP, lanes), 1)
    zeros = jnp.zeros((rows + 2 * PAD, lanes), F32)
    vel[0, pl.ds(PAD, rows), :] = xlow_ref[0]
    vel[cells + 1, pl.ds(PAD, rows), :] = xhigh_ref[0]
    once[0] = zeros
    once[cells + 1] = zeros
    line_zero = jnp.zeros((PAD, lanes), F32)

    def lines(x):
        vel[x + 1, PAD - 1 : PAD, :] = ylow_ref[pl.ds(x, 1), :]
        vel[x + 1, PAD + rows : PAD + rows + 1, :] = yhigh_ref[pl.ds(x, 1), :]
        once[x + 1, 0:PAD, :] = line_zero
        once[x + 1, PAD + rows : PAD + rows + PAD, :] = line_zero
        slot = jnp.full((1, lanes), table_ref[x].astype(F32), F32)
        edge_ylow_ref[pl.ds(cells + x, 1), :] = slot
        edge_yhigh_ref[pl.ds(cells + x, 1), :] = slot

    by_rows(0, cells, lines)

    def update_once(x):
        for first in range(0, rows, STRIP):
            part = pl.ds(first, STRIP)
            heaviside = jnp.tanh(rate[x, part, :] * (1.0 / SMEAR_WIDTH))
            density = (AIR_DENSITY + 0.5 * (1.0 - AIR_DENSITY)) + (0.5 * (1.0 - AIR_DENSITY)) * heaviside
            rate_here = ADV_RATE / density
            rate[x, part, :] = rate_here
            once[x + 1, pl.ds(PAD + first, STRIP), :] = operator(
                neighbours(vel, x, first, STRIP, lane), flags[x, part, :], rate_here
            )

    def update_twice(x):
        for first in range(0, rows, STRIP):
            part = pl.ds(first, STRIP)
            twice[x, part, :] = operator(
                neighbours(once, x, first, STRIP, lane), flags[x, part, :], rate[x, part, :]
            )

    vel_copy(0).wait()
    for c in range(chunks):
        if c + 1 < chunks:
            vel_copy(c + 1).wait()
        flags_copy(c).wait()
        for x in range(c * CHUNK, (c + 1) * CHUNK):
            phi_copy(x).wait()
        by_rows(c * CHUNK, (c + 1) * CHUNK, update_once)
        rate_copy(c).start()

    edge_x_ref[0] = once[1, pl.ds(PAD, rows), :]
    edge_x_ref[1] = once[cells, pl.ds(PAD, rows), :]
    coef_ref[0] = DIFFUSION + jnp.where((flags[0] & 1) != 0, rate[0], 0.0)
    coef_ref[1] = DIFFUSION + jnp.where((flags[cells - 1] & 1) != 0, 0.0, rate[cells - 1])

    def edge_lines(x):
        edge_ylow_ref[pl.ds(x, 1), :] = once[x + 1, PAD : PAD + 1, :]
        edge_yhigh_ref[pl.ds(x, 1), :] = once[x + 1, PAD + rows - 1 : PAD + rows, :]

    by_rows(0, cells, edge_lines)
    for c in range(chunks):
        by_rows(c * CHUNK, (c + 1) * CHUNK, update_twice)
        twice_copy(c).start()
    for c in range(chunks):
        rate_copy(c).wait()
        twice_copy(c).wait()


def block_of(ref, slot, rows):
    return ref.at[slot // CAP, pl.ds(pl.multiple_of((slot % CAP) * rows, rows), rows)]


def edge_kernel(table_ref, edge_ref, forcing_ref, low_out, high_out):
    rows = low_out.shape[1]
    for side, (x, out) in enumerate(((0, low_out), (table_ref.shape[0] - 1, high_out))):
        slot = table_ref[x]

        @pl.when(slot >= 0)
        def _():
            out[0] = edge_ref[side] + block_of(forcing_ref, slot, rows)[...]

        @pl.when(slot < 0)
        def _():
            out[0] = edge_ref[side]


def last_kernel(
    table_ref, below_ref, above_ref, forcing_ref, rate_ref, flags_ref, twice_ref, ylow_ref, yhigh_ref,
    out_ref, part_ref, source, rate, flags, twice, sem_rate, sem_flags, sem_twice, sem_out,
):
    cells, rows, lanes = flags.shape
    chunks = cells // CHUNK
    loads = ((rate_ref, rate, sem_rate), (flags_ref, flags, sem_flags), (twice_ref, twice, sem_twice))
    for c in range(chunks):
        for load in loads:
            chunk_copy(*load, c).start()
    zeros = jnp.zeros((rows, lanes), F32)
    source[0, pl.ds(PAD, rows), :] = zeros
    source[cells + 1, pl.ds(PAD, rows), :] = zeros

    def fill(x, carry):
        slot = table_ref[x]

        @pl.when(slot >= 0)
        def _():
            source[x + 1, pl.ds(PAD, rows), :] = block_of(forcing_ref, slot, rows)[...]

        @pl.when(slot < 0)
        def _():
            source[x + 1, pl.ds(PAD, rows), :] = zeros

        for side, slots, halo, at in (
            (0, below_ref, ylow_ref, PAD - 1),
            (1, above_ref, yhigh_ref, PAD + rows),
        ):
            line_slot = slots[x]
            safe = jnp.maximum(line_slot, 0)
            line = forcing_ref[safe // CAP, pl.ds(CAP * rows + side * CAP + safe % CAP, 1), :]
            source[x + 1, at : at + 1, :] = halo[pl.ds(x, 1), :] + jnp.where(
                line_slot >= 0, line, 0.0
            )
        return carry

    lane = lax.broadcasted_iota(I32, (STRIP, lanes), 1)

    def update(x):
        for first in range(0, rows, STRIP):
            part = pl.ds(first, STRIP)
            fields = neighbours(source, x, first, STRIP, lane)
            twice[x, part, :] = (
                twice[x, part, :] + fields[0] + operator(fields, flags[x, part, :], rate[x, part, :])
            )

    def out_copy(c):
        first = 1 if c == 0 else c * CHUNK
        last = cells - 1 if c == chunks - 1 else (c + 1) * CHUNK
        part = pl.ds(first, last - first)
        return pltpu.make_async_copy(twice.at[part], out_ref.at[part], sem_out.at[c])

    lax.fori_loop(0, cells, fill, 0)
    for c in range(chunks):
        for load in loads:
            chunk_copy(*load, c).wait()
        by_rows(c * CHUNK, (c + 1) * CHUNK, update)
        out_copy(c).start()
    part_ref[0] = twice[0]
    part_ref[1] = twice[cells - 1]
    for c in range(chunks):
        out_copy(c).wait()


def close_kernel(part_ref, coef_ref, low_ref, high_ref, whole_ref, out_ref, hold, sem):
    cells = out_ref.shape[0]
    hold[0] = part_ref[0] + coef_ref[0] * low_ref[0]
    hold[1] = part_ref[1] + coef_ref[1] * high_ref[0]
    copies = [
        pltpu.make_async_copy(hold.at[0], out_ref.at[0], sem.at[0]),
        pltpu.make_async_copy(hold.at[1], out_ref.at[cells - 1], sem.at[1]),
    ]
    for copy in copies:
        copy.start()
    for copy in copies:
        copy.wait()


def neighbour_pairs(axis):
    count = lax.axis_size(axis)
    forward = [(i, i + 1) for i in range(count - 1)]
    return forward, [(target, source) for source, target in forward]


def local(band_phi, band_seed, owner_map, active_list, brick_phi, adjoint_vel, upwind_flags):
    gx_count = lax.axis_size("gx")
    slots, rows, lanes = band_phi.shape
    cells = brick_phi.shape[0]
    chunks = cells // CHUNK
    up_x, down_x = neighbour_pairs("gx")
    up_y, down_y = neighbour_pairs("gy")
    shape = jax.ShapeDtypeStruct
    dma = pltpu.SemaphoreType.DMA
    brick = (cells, rows, lanes)
    padded = (cells + 2, rows + 2 * PAD, lanes)
    sent = (gx_count, CAP * rows + EXTRA, lanes)
    owners, slabs = owner_map.T, active_list.T

    level_sent = pl.pallas_call(
        pack_level_kernel,
        out_shape=shape(sent, F32),
        in_specs=[SMEM, SMEM, HBM],
        out_specs=HBM,
        scratch_shapes=[
            pltpu.VMEM((slots, rows, lanes), F32),
            pltpu.VMEM((gx_count, EXTRA, lanes), F32),
            pltpu.SMEM((gx_count,), I32),
            dma((slots,)), dma((slots,)), dma(()),
        ],
        compiler_params=params(VMEM_MIB),
        cost_estimate=cost(2, 1000),
        name="pack_level",
    )(owners, slabs, band_phi)
    level = lax.all_to_all(level_sent, "gx", split_axis=0, concat_axis=0, tiled=True)

    v_xlow = lax.ppermute(adjoint_vel[cells - 1 :], "gx", up_x)
    v_xhigh = lax.ppermute(adjoint_vel[:1], "gx", down_x)
    v_ylow = lax.ppermute(adjoint_vel[:, rows - 1], "gy", up_y)
    v_yhigh = lax.ppermute(adjoint_vel[:, 0], "gy", down_y)

    lines = (gx_count, EXTRA, lanes)
    forcing_sent, low_lines, high_lines = pl.pallas_call(
        reinit_kernel,
        out_shape=(shape(sent, F32), shape(lines, F32), shape(lines, F32)),
        in_specs=[SMEM, HBM, HBM],
        out_specs=(HBM, VMEM, VMEM),
        scratch_shapes=[
            pltpu.VMEM((slots, rows, lanes), F32),
            pltpu.VMEM((slots, rows, lanes), F32),
            pltpu.VMEM((slots, rows, lanes), F32),
            pltpu.SMEM((gx_count,), I32),
            pltpu.SMEM((slots,), I32),
            dma((2, slots // REINIT_UNROLL)), dma((slots,)),
        ],
        compiler_params=params(VMEM_MIB),
        cost_estimate=cost(20, 40_000_000),
        name="reinit",
    )(owners, band_phi, band_seed)
    below_lines = lax.ppermute(high_lines, "gy", up_y)
    above_lines = lax.ppermute(low_lines, "gy", down_y)
    halos = (v_xlow, v_xhigh, v_ylow, v_yhigh)
    halos, below_lines, above_lines = lax.optimization_barrier((halos, below_lines, above_lines))
    v_xlow, v_xhigh, v_ylow, v_yhigh = halos
    forcing_sent = pl.pallas_call(
        pack_lines_kernel,
        out_shape=shape(sent, F32),
        in_specs=[VMEM, VMEM, HBM],
        out_specs=HBM,
        scratch_shapes=[pltpu.VMEM(lines, F32), dma(())],
        input_output_aliases={2: 0},
        compiler_params=params(VMEM_MIB),
        cost_estimate=cost(2, 1000),
        name="pack_lines",
    )(below_lines, above_lines, forcing_sent)
    forcing = lax.all_to_all(forcing_sent, "gx", split_axis=0, concat_axis=0, tiled=True)

    tags = level[:, CAP * rows : CAP * rows + CAP, 0].astype(I32)
    edge_lines = (2 * cells, lanes)
    rate, twice, edge_x, edge_ylow, edge_yhigh, coef, table = pl.pallas_call(
        first_kernel,
        out_shape=(
            shape(brick, F32),
            shape(brick, F32),
            shape((2, rows, lanes), F32),
            shape(edge_lines, F32),
            shape(edge_lines, F32),
            shape((2, rows, lanes), F32),
            shape((cells,), I32),
        ),
        in_specs=[SMEM, HBM, HBM, HBM, HBM, VMEM, VMEM, VMEM, VMEM],
        out_specs=(HBM, HBM, VMEM, VMEM, VMEM, VMEM, SMEM),
        scratch_shapes=[
            pltpu.VMEM(padded, F32),
            pltpu.VMEM(padded, F32),
            pltpu.VMEM(brick, I32),
            pltpu.VMEM(brick, F32),
            pltpu.VMEM(brick, F32),
            dma((chunks,)), dma((chunks,)), dma((cells,)), dma((chunks,)), dma((chunks,)),
        ],
        compiler_params=params(VMEM_MIB),
        cost_estimate=cost(30, 60_000_000),
        name="two_updates",
    )(tags, adjoint_vel, upwind_flags, brick_phi, level, v_xlow, v_xhigh, v_ylow, v_yhigh)
    once_ylow = lax.ppermute(edge_yhigh, "gy", up_y)
    once_yhigh = lax.ppermute(edge_ylow, "gy", down_y)
    gy = lax.axis_index("gy")
    below = jnp.where(gy > 0, once_ylow[cells:, 0].astype(I32), -1)
    above = jnp.where(gy < lax.axis_size("gy") - 1, once_yhigh[cells:, 0].astype(I32), -1)

    low_slab, high_slab = pl.pallas_call(
        edge_kernel,
        out_shape=(shape((1, rows, lanes), F32), shape((1, rows, lanes), F32)),
        in_specs=[SMEM, VMEM, VMEM],
        out_specs=(VMEM, VMEM),
        compiler_params=params(VMEM_MIB),
        cost_estimate=cost(1, 1000),
        name="edge_slabs",
    )(table, edge_x, forcing)
    from_low = lax.ppermute(high_slab, "gx", up_x)
    from_high = lax.ppermute(low_slab, "gx", down_x)

    out, part = pl.pallas_call(
        last_kernel,
        out_shape=(shape(brick, F32), shape((2, rows, lanes), F32)),
        in_specs=[SMEM, SMEM, SMEM, VMEM, HBM, HBM, HBM, VMEM, VMEM],
        out_specs=(HBM, VMEM),
        scratch_shapes=[
            pltpu.VMEM(padded, F32),
            pltpu.VMEM(brick, F32),
            pltpu.VMEM(brick, I32),
            pltpu.VMEM(brick, F32),
            dma((chunks,)), dma((chunks,)), dma((chunks,)), dma((chunks,)),
        ],
        compiler_params=params(VMEM_MIB),
        cost_estimate=cost(30, 60_000_000),
        name="add_forcing",
    )(table, below, above, forcing, rate, upwind_flags, twice, once_ylow, once_yhigh)

    return pl.pallas_call(
        close_kernel,
        out_shape=shape(brick, F32),
        in_specs=[VMEM, VMEM, VMEM, VMEM, HBM],
        out_specs=HBM,
        scratch_shapes=[pltpu.VMEM((2, rows, lanes), F32), dma((2,))],
        input_output_aliases={4: 0},
        compiler_params=params(VMEM_MIB),
        cost_estimate=cost(1, 1000),
        name="close_slabs",
    )(part, coef, from_low, from_high, out)


def solution(mesh):
    in_specs = (
        P("gx", "gy", None),
        P("gx", "gy", None),
        P("gx", "gy"),
        P("gx", "gy"),
        P("gx", "gy", None),
        P("gx", "gy", None),
        P("gx", "gy", None),
    )
    out_specs = P("gx", "gy", None)
    return jax.shard_map(local, mesh=mesh, in_specs=in_specs, out_specs=out_specs, check_vma=False)
```

```python
import jax
import jax.numpy as jnp
from jax import lax
from jax.experimental import pallas as pl
from jax.experimental.pallas import tpu as pltpu
from jax.sharding import PartitionSpec as P

CAP = 2
REINIT = 4
REINIT_STEP = 0.4
ADV_RATE = 0.25
DIFFUSION = 0.1
AIR_DENSITY = 0.3
SMEAR_WIDTH = 1.5

F32 = jnp.float32
I32 = jnp.int32
MIB = 1 << 20
HBM = pl.BlockSpec(memory_space=pltpu.HBM)
VMEM = pl.BlockSpec(memory_space=pltpu.VMEM)
SMEM = pl.BlockSpec(memory_space=pltpu.SMEM)
EXTRA = 8
PAD = 8
CHUNK = 8
STRIP = 32
UNROLL = 4
REINIT_UNROLL = 2


BIG = 55
MEDIUM = 52
ROOMY = 50
SMALL = 4


def params(mib):
    return pltpu.CompilerParams(vmem_limit_bytes=mib * MIB)


def cost(mib, flops):
    return pl.CostEstimate(flops=flops, bytes_accessed=mib * MIB, transcendentals=0)


def homes_and_ranks(owner_ref, count_ref):
    for home in range(count_ref.shape[0]):
        count_ref[home] = 0
    result = []
    for slot in range(owner_ref.shape[1]):
        home = owner_ref[0, slot]
        rank = count_ref[home]
        count_ref[home] = rank + 1
        result.append((home, rank))
    return result


def pack_level_kernel(
    owner_ref, slab_ref, phi_ref, out_ref, phi, tags, count_ref, load_sem, sem, tag_sem
):
    slots, rows, lanes = phi_ref.shape
    loads = [
        pltpu.make_async_copy(phi_ref.at[slot], phi.at[slot], load_sem.at[slot])
        for slot in range(slots)
    ]
    for load in loads:
        load.start()
    tags[...] = jnp.zeros_like(tags)
    places = homes_and_ranks(owner_ref, count_ref)
    for slot, (home, rank) in enumerate(places):
        label = (slab_ref[0, slot] + 1).astype(F32)
        tags[home, pl.ds(rank, 1), :] = jnp.full((1, lanes), label, F32)
    copies = [pltpu.make_async_copy(tags, out_ref.at[:, pl.ds(CAP * rows, EXTRA)], tag_sem)]
    copies[0].start()
    for slot, (home, rank) in enumerate(places):
        loads[slot].wait()
        copy = pltpu.make_async_copy(
            phi.at[slot],
            out_ref.at[home, pl.ds(pl.multiple_of(rank * rows, rows), rows)],
            sem.at[slot],
        )
        copy.start()
        copies.append(copy)
    for copy in copies:
        copy.wait()


def shift_rows(values, step, row):
    rows = values.shape[0]
    moved = pltpu.roll(values, step % rows, 0)
    return jnp.where(row == (0 if step == 1 else rows - 1), 0.0, moved)


def shift_lanes(values, step, lane):
    lanes = values.shape[1]
    moved = pltpu.roll(values, step % lanes, 1)
    return jnp.where(lane == (0 if step == 1 else lanes - 1), 0.0, moved)


def reinit_kernel(
    owner_ref, phi_hbm, seed_hbm, vel_hbm, out_ref, low_ref, high_ref, xlow_ref, xhigh_ref,
    phi_ref, seed_ref, hold, vel_low, vel_high, count_ref, place_ref, load_sem, vel_sem, sem,
):
    slots, rows, lanes = phi_ref.shape

    def load(step, which):
        part = pl.ds(step * REINIT_UNROLL, REINIT_UNROLL)
        src, dst = ((phi_hbm, phi_ref), (seed_hbm, seed_ref))[which]
        return pltpu.make_async_copy(src.at[part], dst.at[part], load_sem.at[which, step])

    for step in range(slots // REINIT_UNROLL):
        load(step, 0).start()
        load(step, 1).start()
    cells = vel_hbm.shape[0]
    vel_copies = [
        pltpu.make_async_copy(vel_hbm.at[pl.ds(0, 1)], xlow_ref, vel_sem.at[0]),
        pltpu.make_async_copy(vel_hbm.at[pl.ds(cells - 1, 1)], xhigh_ref, vel_sem.at[1]),
        pltpu.make_async_copy(vel_hbm.at[:, pl.ds(0, 8)], vel_low, vel_sem.at[2]),
        pltpu.make_async_copy(vel_hbm.at[:, pl.ds(rows - 8, 8)], vel_high, vel_sem.at[3]),
    ]
    for copy in vel_copies:
        copy.start()
    for slot, (home, rank) in enumerate(homes_and_ranks(owner_ref, count_ref)):
        place_ref[slot] = home * CAP + rank
    row = lax.broadcasted_iota(I32, (rows, lanes), 0)
    lane = lax.broadcasted_iota(I32, (rows, lanes), 1)
    low_ref[...] = jnp.zeros_like(low_ref)
    high_ref[...] = jnp.zeros_like(high_ref)

    def out_copy(slot):
        place = place_ref[slot]
        return pltpu.make_async_copy(
            hold.at[slot],
            out_ref.at[place // CAP, pl.ds(pl.multiple_of((place % CAP) * rows, rows), rows)],
            sem.at[slot],
        )

    def block(slot):
        phi = phi_ref[slot]
        up_y = jnp.where(row == rows - 1, phi, pltpu.roll(phi, rows - 1, 0))
        low_y = jnp.where(row == 0, phi, pltpu.roll(phi, 1, 0))
        up_z = jnp.where(lane == lanes - 1, phi, pltpu.roll(phi, lanes - 1, 1))
        low_z = jnp.where(lane == 0, phi, pltpu.roll(phi, 1, 1))
        grad_y = 0.5 * (up_y - low_y)
        grad_z = 0.5 * (up_z - low_z)
        normal = jnp.sqrt(grad_y * grad_y + grad_z * grad_z + 1.0)
        sign = phi / jnp.sqrt(phi * phi + 1.0)
        scale = (0.5 * REINIT_STEP) * sign / normal
        weight_y = scale * grad_y
        weight_z = scale * grad_z
        adjoint = seed_ref[slot]
        for _ in range(REINIT):
            flux_y = weight_y * adjoint
            flux_z = weight_z * adjoint
            adjoint = adjoint + (
                (shift_rows(flux_y, -1, row) - shift_rows(flux_y, 1, row))
                + (shift_lanes(flux_z, -1, lane) - shift_lanes(flux_z, 1, lane))
            )
        heaviside = jnp.tanh(phi / SMEAR_WIDTH)
        hold[slot] = adjoint * (0.5 / SMEAR_WIDTH * (1.0 - heaviside * heaviside))

    def body(step, carry):
        load(step, 0).wait()
        load(step, 1).wait()
        for j in range(REINIT_UNROLL):
            block(step * REINIT_UNROLL + j)
        for j in range(REINIT_UNROLL):
            slot = step * REINIT_UNROLL + j
            out_copy(slot).start()
            place = place_ref[slot]
            first = (place // CAP) * EXTRA + place % CAP
            high_ref[pl.ds(first, 1), :] = hold[slot, rows - 1 : rows, :]
            low_ref[pl.ds(first + CAP, 1), :] = hold[slot, 0:1, :]
        return carry

    lax.fori_loop(0, slots // REINIT_UNROLL, body, 0)
    for copy in vel_copies:
        copy.wait()
    behind = low_ref.shape[0] - cells
    for x in range(cells):
        low_ref[behind + x : behind + x + 1, :] = vel_low[x, 0:1, :]
        high_ref[behind + x : behind + x + 1, :] = vel_high[x, 7:8, :]
    for slot in range(slots):
        out_copy(slot).wait()


def pack_lines_kernel(below_ref, above_ref, forcing_ref, out_ref, hold, sem):
    for home in range(hold.shape[0]):
        part = pl.ds(home * EXTRA, EXTRA)
        hold[home] = below_ref[part, :] + above_ref[part, :]
    copy = pltpu.make_async_copy(
        hold, out_ref.at[:, pl.ds(out_ref.shape[1] - EXTRA, EXTRA)], sem
    )
    copy.start()
    copy.wait()


def neighbours(buffer, x, first, rows, lane):
    here = buffer[x + 1, pl.ds(PAD + first, rows), :]
    low_x = buffer[x, pl.ds(PAD + first, rows), :]
    up_x = buffer[x + 2, pl.ds(PAD + first, rows), :]
    low_y = buffer[x + 1, pl.ds(PAD + first - 1, rows), :]
    up_y = buffer[x + 1, pl.ds(PAD + first + 1, rows), :]
    low_z = shift_lanes(here, 1, lane)
    up_z = shift_lanes(here, -1, lane)
    return here, low_x, up_x, low_y, up_y, low_z, up_z


def operator(fields, flags, rate):
    here, low_x, up_x, low_y, up_y, low_z, up_z = fields
    upwind = (
        jnp.where((flags & 1) != 0, low_x, up_x)
        + jnp.where((flags & 2) != 0, low_y, up_y)
        + jnp.where((flags & 4) != 0, low_z, up_z)
    )
    total = (low_x + up_x) + (low_y + up_y) + (low_z + up_z)
    return (1.0 - 6.0 * DIFFUSION) * here + rate * (upwind - 3.0 * here) + DIFFUSION * total


def by_rows(first, last, body):
    def step(i, carry):
        for j in range(UNROLL):
            body(first + i * UNROLL + j)
        return carry

    lax.fori_loop(0, (last - first) // UNROLL, step, 0)


def chunk_copy(src, dst, sem, c):
    part = pl.ds(c * CHUNK, CHUNK)
    return pltpu.make_async_copy(src.at[part], dst.at[part], sem.at[c])


def first_kernel(
    tag_ref, vel_ref, flags_ref, phi_ref, level_ref, xlow_ref, xhigh_ref, ylow_ref, yhigh_ref,
    rate_out, twice_out, edge_x_ref, edge_ylow_ref, edge_yhigh_ref, coef_ref, table_ref,
    vel, once, flags, rate, twice, sem_vel, sem_flags, sem_phi, sem_rate, sem_twice,
):
    cells, rows, lanes = flags.shape
    chunks = cells // CHUNK

    def vel_copy(c):
        return pltpu.make_async_copy(
            vel_ref.at[pl.ds(c * CHUNK, CHUNK)],
            vel.at[pl.ds(1 + c * CHUNK, CHUNK), pl.ds(PAD, rows)],
            sem_vel.at[c],
        )

    def phi_copy(x):
        return pltpu.make_async_copy(phi_ref.at[x], rate.at[x], sem_phi.at[x])

    def flags_copy(c):
        return chunk_copy(flags_ref, flags, sem_flags, c)

    def rate_copy(c):
        return chunk_copy(rate, rate_out, sem_rate, c)

    def twice_copy(c):
        return chunk_copy(twice, twice_out, sem_twice, c)

    for c in range(chunks):
        vel_copy(c).start()
        flags_copy(c).start()
    for x in range(cells):
        table_ref[x] = -1
    for source in range(tag_ref.shape[0]):
        for rank in range(CAP):
            tag = tag_ref[source, rank]

            @pl.when(tag > 0)
            def _():
                table_ref[tag - 1] = source * CAP + rank

    def start_phi(x, carry):
        slot = table_ref[x]

        @pl.when(slot >= 0)
        def _():
            pltpu.make_async_copy(
                block_of(level_ref, slot, rows), rate.at[x], sem_phi.at[x]
            ).start()

        @pl.when(slot < 0)
        def _():
            phi_copy(x).start()

        return carry

    lax.fori_loop(0, cells, start_phi, 0)

    lane = lax.broadcasted_iota(I32, (STRIP, lanes), 1)
    zeros = jnp.zeros((rows + 2 * PAD, lanes), F32)
    vel[0, pl.ds(PAD, rows), :] = xlow_ref[0]
    vel[cells + 1, pl.ds(PAD, rows), :] = xhigh_ref[0]
    once[0] = zeros
    once[cells + 1] = zeros
    line_zero = jnp.zeros((PAD, lanes), F32)

    behind = ylow_ref.shape[0] - cells

    def lines(x):
        vel[x + 1, PAD - 1 : PAD, :] = ylow_ref[pl.ds(behind + x, 1), :]
        vel[x + 1, PAD + rows : PAD + rows + 1, :] = yhigh_ref[pl.ds(behind + x, 1), :]
        once[x + 1, 0:PAD, :] = line_zero
        once[x + 1, PAD + rows : PAD + rows + PAD, :] = line_zero
        slot = jnp.full((1, lanes), table_ref[x].astype(F32), F32)
        edge_ylow_ref[pl.ds(cells + x, 1), :] = slot
        edge_yhigh_ref[pl.ds(cells + x, 1), :] = slot

    by_rows(0, cells, lines)

    def update_once(x):
        for first in range(0, rows, STRIP):
            part = pl.ds(first, STRIP)
            heaviside = jnp.tanh(rate[x, part, :] * (1.0 / SMEAR_WIDTH))
            density = (AIR_DENSITY + 0.5 * (1.0 - AIR_DENSITY)) + (0.5 * (1.0 - AIR_DENSITY)) * heaviside
            rate_here = ADV_RATE / density
            rate[x, part, :] = rate_here
            once[x + 1, pl.ds(PAD + first, STRIP), :] = operator(
                neighbours(vel, x, first, STRIP, lane), flags[x, part, :], rate_here
            )

    def update_twice(x):
        for first in range(0, rows, STRIP):
            part = pl.ds(first, STRIP)
            twice[x, part, :] = operator(
                neighbours(once, x, first, STRIP, lane), flags[x, part, :], rate[x, part, :]
            )

    vel_copy(0).wait()
    for c in range(chunks):
        if c + 1 < chunks:
            vel_copy(c + 1).wait()
        flags_copy(c).wait()
        for x in range(c * CHUNK, (c + 1) * CHUNK):
            phi_copy(x).wait()
        by_rows(c * CHUNK, (c + 1) * CHUNK, update_once)
        rate_copy(c).start()

    edge_x_ref[0] = once[1, pl.ds(PAD, rows), :]
    edge_x_ref[1] = once[cells, pl.ds(PAD, rows), :]
    coef_ref[0] = DIFFUSION + jnp.where((flags[0] & 1) != 0, rate[0], 0.0)
    coef_ref[1] = DIFFUSION + jnp.where((flags[cells - 1] & 1) != 0, 0.0, rate[cells - 1])

    def edge_lines(x):
        edge_ylow_ref[pl.ds(x, 1), :] = once[x + 1, PAD : PAD + 1, :]
        edge_yhigh_ref[pl.ds(x, 1), :] = once[x + 1, PAD + rows - 1 : PAD + rows, :]

    by_rows(0, cells, edge_lines)
    for c in range(chunks):
        by_rows(c * CHUNK, (c + 1) * CHUNK, update_twice)
        twice_copy(c).start()
    for c in range(chunks):
        rate_copy(c).wait()
        twice_copy(c).wait()


def block_of(ref, slot, rows):
    return ref.at[slot // CAP, pl.ds(pl.multiple_of((slot % CAP) * rows, rows), rows)]


def edge_kernel(table_ref, edge_ref, forcing_ref, low_out, high_out):
    rows = low_out.shape[1]
    for side, (x, out) in enumerate(((0, low_out), (table_ref.shape[0] - 1, high_out))):
        slot = table_ref[x]

        @pl.when(slot >= 0)
        def _():
            out[0] = edge_ref[side] + block_of(forcing_ref, slot, rows)[...]

        @pl.when(slot < 0)
        def _():
            out[0] = edge_ref[side]


def last_kernel(
    table_ref, below_ref, above_ref, forcing_ref, rate_ref, flags_ref, twice_ref, ylow_ref, yhigh_ref,
    out_ref, part_ref, source, rate, flags, twice, sem_rate, sem_flags, sem_twice, sem_out,
):
    cells, rows, lanes = flags.shape
    chunks = cells // CHUNK
    loads = ((rate_ref, rate, sem_rate), (flags_ref, flags, sem_flags), (twice_ref, twice, sem_twice))
    for c in range(chunks):
        for load in loads:
            chunk_copy(*load, c).start()
    zeros = jnp.zeros((rows, lanes), F32)
    source[0, pl.ds(PAD, rows), :] = zeros
    source[cells + 1, pl.ds(PAD, rows), :] = zeros

    def fill(x):
        slot = table_ref[x]
        safe = jnp.maximum(slot, 0)
        source[x + 1, pl.ds(PAD, rows), :] = jnp.where(
            slot >= 0, block_of(forcing_ref, safe, rows)[...], 0.0
        )
        for side, slots, halo, at in (
            (0, below_ref, ylow_ref, PAD - 1),
            (1, above_ref, yhigh_ref, PAD + rows),
        ):
            line_slot = slots[x]
            safe = jnp.maximum(line_slot, 0)
            line = forcing_ref[safe // CAP, pl.ds(CAP * rows + side * CAP + safe % CAP, 1), :]
            source[x + 1, at : at + 1, :] = halo[pl.ds(x, 1), :] + jnp.where(
                line_slot >= 0, line, 0.0
            )

    lane = lax.broadcasted_iota(I32, (STRIP, lanes), 1)

    def update(x):
        for first in range(0, rows, STRIP):
            part = pl.ds(first, STRIP)
            fields = neighbours(source, x, first, STRIP, lane)
            twice[x, part, :] = (
                twice[x, part, :] + fields[0] + operator(fields, flags[x, part, :], rate[x, part, :])
            )

    def out_copy(c):
        first = 1 if c == 0 else c * CHUNK
        last = cells - 1 if c == chunks - 1 else (c + 1) * CHUNK
        part = pl.ds(first, last - first)
        return pltpu.make_async_copy(twice.at[part], out_ref.at[part], sem_out.at[c])

    by_rows(0, cells, fill)
    for c in range(chunks):
        for load in loads:
            chunk_copy(*load, c).wait()
        by_rows(c * CHUNK, (c + 1) * CHUNK, update)
        out_copy(c).start()
    part_ref[0] = twice[0]
    part_ref[1] = twice[cells - 1]
    for c in range(chunks):
        out_copy(c).wait()


def close_kernel(part_ref, coef_ref, low_ref, high_ref, whole_ref, out_ref, hold, sem):
    cells = out_ref.shape[0]
    hold[0] = part_ref[0] + coef_ref[0] * low_ref[0]
    hold[1] = part_ref[1] + coef_ref[1] * high_ref[0]
    copies = [
        pltpu.make_async_copy(hold.at[0], out_ref.at[0], sem.at[0]),
        pltpu.make_async_copy(hold.at[1], out_ref.at[cells - 1], sem.at[1]),
    ]
    for copy in copies:
        copy.start()
    for copy in copies:
        copy.wait()


def neighbour_pairs(axis):
    count = lax.axis_size(axis)
    forward = [(i, i + 1) for i in range(count - 1)]
    return forward, [(target, source) for source, target in forward]


def local(band_phi, band_seed, owner_map, active_list, brick_phi, adjoint_vel, upwind_flags):
    gx_count = lax.axis_size("gx")
    slots, rows, lanes = band_phi.shape
    cells = brick_phi.shape[0]
    chunks = cells // CHUNK
    up_x, down_x = neighbour_pairs("gx")
    up_y, down_y = neighbour_pairs("gy")
    shape = jax.ShapeDtypeStruct
    dma = pltpu.SemaphoreType.DMA
    brick = (cells, rows, lanes)
    padded = (cells + 2, rows + 2 * PAD, lanes)
    sent = (gx_count, CAP * rows + EXTRA, lanes)
    owners, slabs = owner_map.T, active_list.T

    level_sent = pl.pallas_call(
        pack_level_kernel,
        out_shape=shape(sent, F32),
        in_specs=[SMEM, SMEM, HBM],
        out_specs=HBM,
        scratch_shapes=[
            pltpu.VMEM((slots, rows, lanes), F32),
            pltpu.VMEM((gx_count, EXTRA, lanes), F32),
            pltpu.SMEM((gx_count,), I32),
            dma((slots,)), dma((slots,)), dma(()),
        ],
        compiler_params=params(BIG),
        cost_estimate=cost(2, 1000),
        name="pack_level",
    )(owners, slabs, band_phi)
    level = lax.all_to_all(level_sent, "gx", split_axis=0, concat_axis=0, tiled=True)

    lines = (gx_count * EXTRA + cells, lanes)
    slab = (1, rows, lanes)
    forcing_sent, low_lines, high_lines, v_first, v_last = pl.pallas_call(
        reinit_kernel,
        out_shape=(
            shape(sent, F32), shape(lines, F32), shape(lines, F32), shape(slab, F32), shape(slab, F32)
        ),
        in_specs=[SMEM, HBM, HBM, HBM],
        out_specs=(HBM, VMEM, VMEM, VMEM, VMEM),
        scratch_shapes=[
            pltpu.VMEM((slots, rows, lanes), F32),
            pltpu.VMEM((slots, rows, lanes), F32),
            pltpu.VMEM((slots, rows, lanes), F32),
            pltpu.VMEM((cells, 8, lanes), F32),
            pltpu.VMEM((cells, 8, lanes), F32),
            pltpu.SMEM((gx_count,), I32),
            pltpu.SMEM((slots,), I32),
            dma((2, slots // REINIT_UNROLL)), dma((4,)), dma((slots,)),
        ],
        compiler_params=params(BIG),
        cost_estimate=cost(20, 40_000_000),
        name="reinit",
    )(owners, band_phi, band_seed, adjoint_vel)
    below_lines = lax.ppermute(high_lines, "gy", up_y)
    above_lines = lax.ppermute(low_lines, "gy", down_y)
    v_xlow = lax.ppermute(v_last, "gx", up_x)
    v_xhigh = lax.ppermute(v_first, "gx", down_x)
    v_xlow, v_xhigh, below_lines, above_lines = lax.optimization_barrier(
        (v_xlow, v_xhigh, below_lines, above_lines)
    )
    forcing_sent = pl.pallas_call(
        pack_lines_kernel,
        out_shape=shape(sent, F32),
        in_specs=[VMEM, VMEM, HBM],
        out_specs=HBM,
        scratch_shapes=[pltpu.VMEM((gx_count, EXTRA, lanes), F32), dma(())],
        input_output_aliases={2: 0},
        compiler_params=params(MEDIUM),
        cost_estimate=cost(2, 1000),
        name="pack_lines",
    )(below_lines, above_lines, forcing_sent)
    forcing = lax.all_to_all(forcing_sent, "gx", split_axis=0, concat_axis=0, tiled=True)

    tags = level[:, CAP * rows : CAP * rows + CAP, 0].astype(I32)
    edge_lines = (2 * cells, lanes)
    rate, twice, edge_x, edge_ylow, edge_yhigh, coef, table = pl.pallas_call(
        first_kernel,
        out_shape=(
            shape(brick, F32),
            shape(brick, F32),
            shape((2, rows, lanes), F32),
            shape(edge_lines, F32),
            shape(edge_lines, F32),
            shape((2, rows, lanes), F32),
            shape((cells,), I32),
        ),
        in_specs=[SMEM, HBM, HBM, HBM, HBM, VMEM, VMEM, VMEM, VMEM],
        out_specs=(HBM, HBM, VMEM, VMEM, VMEM, VMEM, SMEM),
        scratch_shapes=[
            pltpu.VMEM(padded, F32),
            pltpu.VMEM(padded, F32),
            pltpu.VMEM(brick, I32),
            pltpu.VMEM(brick, F32),
            pltpu.VMEM(brick, F32),
            dma((chunks,)), dma((chunks,)), dma((cells,)), dma((chunks,)), dma((chunks,)),
        ],
        compiler_params=params(ROOMY),
        cost_estimate=cost(30, 60_000_000),
        name="two_updates",
    )(tags, adjoint_vel, upwind_flags, brick_phi, level, v_xlow, v_xhigh, below_lines, above_lines)
    once_ylow = lax.ppermute(edge_yhigh, "gy", up_y)
    once_yhigh = lax.ppermute(edge_ylow, "gy", down_y)
    gy = lax.axis_index("gy")
    below = jnp.where(gy > 0, once_ylow[cells:, 0].astype(I32), -1)
    above = jnp.where(gy < lax.axis_size("gy") - 1, once_yhigh[cells:, 0].astype(I32), -1)

    edge_x, below, above = lax.optimization_barrier((edge_x, below, above))

    low_slab, high_slab = pl.pallas_call(
        edge_kernel,
        out_shape=(shape((1, rows, lanes), F32), shape((1, rows, lanes), F32)),
        in_specs=[SMEM, VMEM, VMEM],
        out_specs=(VMEM, VMEM),
        compiler_params=params(SMALL),
        cost_estimate=cost(1, 1000),
        name="edge_slabs",
    )(table, edge_x, forcing)
    from_low = lax.ppermute(high_slab, "gx", up_x)
    from_high = lax.ppermute(low_slab, "gx", down_x)

    out, part = pl.pallas_call(
        last_kernel,
        out_shape=(shape(brick, F32), shape((2, rows, lanes), F32)),
        in_specs=[SMEM, SMEM, SMEM, VMEM, HBM, HBM, HBM, VMEM, VMEM],
        out_specs=(HBM, VMEM),
        scratch_shapes=[
            pltpu.VMEM(padded, F32),
            pltpu.VMEM(brick, F32),
            pltpu.VMEM(brick, I32),
            pltpu.VMEM(brick, F32),
            dma((chunks,)), dma((chunks,)), dma((chunks,)), dma((chunks,)),
        ],
        compiler_params=params(ROOMY),
        cost_estimate=cost(30, 60_000_000),
        name="add_forcing",
    )(table, below, above, forcing, rate, upwind_flags, twice, once_ylow, once_yhigh)

    return pl.pallas_call(
        close_kernel,
        out_shape=shape(brick, F32),
        in_specs=[VMEM, VMEM, VMEM, VMEM, HBM],
        out_specs=HBM,
        scratch_shapes=[pltpu.VMEM((2, rows, lanes), F32), dma((2,))],
        input_output_aliases={4: 0},
        compiler_params=params(SMALL),
        cost_estimate=cost(1, 1000),
        name="close_slabs",
    )(part, coef, from_low, from_high, out)


def solution(mesh):
    in_specs = (
        P("gx", "gy", None),
        P("gx", "gy", None),
        P("gx", "gy"),
        P("gx", "gy"),
        P("gx", "gy", None),
        P("gx", "gy", None),
        P("gx", "gy", None),
    )
    out_specs = P("gx", "gy", None)
    return jax.shard_map(local, mesh=mesh, in_specs=in_specs, out_specs=out_specs, check_vma=False)
```

```python
import jax
import jax.numpy as jnp
from jax import lax
from jax.experimental import pallas as pl
from jax.experimental.pallas import tpu as pltpu
from jax.sharding import PartitionSpec as P

CAP = 2
REINIT = 4
REINIT_STEP = 0.4
ADV_RATE = 0.25
DIFFUSION = 0.1
AIR_DENSITY = 0.3
SMEAR_WIDTH = 1.5

F32 = jnp.float32
I32 = jnp.int32
MIB = 1 << 20
HBM = pl.BlockSpec(memory_space=pltpu.HBM)
VMEM = pl.BlockSpec(memory_space=pltpu.VMEM)
SMEM = pl.BlockSpec(memory_space=pltpu.SMEM)
EXTRA = 8
PAD = 8
CHUNK = 8
STRIP = 32
UNROLL = 4
REINIT_UNROLL = 2


BIG = 55
MEDIUM = 52
ROOMY = 50
SMALL = 4


def params(mib):
    return pltpu.CompilerParams(vmem_limit_bytes=mib * MIB)


def cost(mib, flops):
    return pl.CostEstimate(flops=flops, bytes_accessed=mib * MIB, transcendentals=0)


def by_rows(first, last, body):
    def step(i, carry):
        for j in range(UNROLL):
            body(first + i * UNROLL + j)
        return carry

    lax.fori_loop(0, (last - first) // UNROLL, step, 0)


def homes_and_ranks(owner_ref, count_ref):
    for home in range(count_ref.shape[0]):
        count_ref[home] = 0
    result = []
    for slot in range(owner_ref.shape[1]):
        home = owner_ref[0, slot]
        rank = count_ref[home]
        count_ref[home] = rank + 1
        result.append((home, rank))
    return result


def pack_level_kernel(
    owner_ref, slab_ref, phi_ref, out_ref, phi, tags, count_ref, load_sem, sem, tag_sem
):
    slots, rows, lanes = phi_ref.shape
    loads = [
        pltpu.make_async_copy(phi_ref.at[slot], phi.at[slot], load_sem.at[slot])
        for slot in range(slots)
    ]
    for load in loads:
        load.start()
    tags[...] = jnp.zeros_like(tags)
    places = homes_and_ranks(owner_ref, count_ref)
    for slot, (home, rank) in enumerate(places):
        label = (slab_ref[0, slot] + 1).astype(F32)
        tags[home, pl.ds(rank, 1), :] = jnp.full((1, lanes), label, F32)
    copies = [pltpu.make_async_copy(tags, out_ref.at[:, pl.ds(CAP * rows, EXTRA)], tag_sem)]
    copies[0].start()
    for slot, (home, rank) in enumerate(places):
        loads[slot].wait()
        copy = pltpu.make_async_copy(
            phi.at[slot],
            out_ref.at[home, pl.ds(pl.multiple_of(rank * rows, rows), rows)],
            sem.at[slot],
        )
        copy.start()
        copies.append(copy)
    for copy in copies:
        copy.wait()


def shift_rows(values, step, row):
    rows = values.shape[0]
    moved = pltpu.roll(values, step % rows, 0)
    return jnp.where(row == (0 if step == 1 else rows - 1), 0.0, moved)


def shift_lanes(values, step, lane):
    lanes = values.shape[1]
    moved = pltpu.roll(values, step % lanes, 1)
    return jnp.where(lane == (0 if step == 1 else lanes - 1), 0.0, moved)


def reinit_kernel(
    owner_ref, phi_hbm, seed_hbm, vel_hbm, out_ref, low_ref, high_ref,
    phi_ref, seed_ref, hold, vel_low, vel_high, count_ref, place_ref, load_sem, vel_sem, sem,
):
    slots, rows, lanes = phi_ref.shape

    def load(step, which):
        part = pl.ds(step * REINIT_UNROLL, REINIT_UNROLL)
        src, dst = ((phi_hbm, phi_ref), (seed_hbm, seed_ref))[which]
        return pltpu.make_async_copy(src.at[part], dst.at[part], load_sem.at[which, step])

    for step in range(slots // REINIT_UNROLL):
        load(step, 0).start()
        load(step, 1).start()
    cells = vel_hbm.shape[0]
    vel_copies = [
        pltpu.make_async_copy(vel_hbm.at[:, pl.ds(0, 8)], vel_low, vel_sem.at[0]),
        pltpu.make_async_copy(vel_hbm.at[:, pl.ds(rows - 8, 8)], vel_high, vel_sem.at[1]),
    ]
    for copy in vel_copies:
        copy.start()
    for slot, (home, rank) in enumerate(homes_and_ranks(owner_ref, count_ref)):
        place_ref[slot] = home * CAP + rank
    row = lax.broadcasted_iota(I32, (rows, lanes), 0)
    lane = lax.broadcasted_iota(I32, (rows, lanes), 1)
    low_ref[...] = jnp.zeros_like(low_ref)
    high_ref[...] = jnp.zeros_like(high_ref)

    def out_copy(slot):
        place = place_ref[slot]
        return pltpu.make_async_copy(
            hold.at[slot],
            out_ref.at[place // CAP, pl.ds(pl.multiple_of((place % CAP) * rows, rows), rows)],
            sem.at[slot],
        )

    def block(slot):
        phi = phi_ref[slot]
        up_y = jnp.where(row == rows - 1, phi, pltpu.roll(phi, rows - 1, 0))
        low_y = jnp.where(row == 0, phi, pltpu.roll(phi, 1, 0))
        up_z = jnp.where(lane == lanes - 1, phi, pltpu.roll(phi, lanes - 1, 1))
        low_z = jnp.where(lane == 0, phi, pltpu.roll(phi, 1, 1))
        grad_y = 0.5 * (up_y - low_y)
        grad_z = 0.5 * (up_z - low_z)
        normal = jnp.sqrt(grad_y * grad_y + grad_z * grad_z + 1.0)
        sign = phi / jnp.sqrt(phi * phi + 1.0)
        scale = (0.5 * REINIT_STEP) * sign / normal
        weight_y = scale * grad_y
        weight_z = scale * grad_z
        adjoint = seed_ref[slot]
        for _ in range(REINIT):
            flux_y = weight_y * adjoint
            flux_z = weight_z * adjoint
            adjoint = adjoint + (
                (shift_rows(flux_y, -1, row) - shift_rows(flux_y, 1, row))
                + (shift_lanes(flux_z, -1, lane) - shift_lanes(flux_z, 1, lane))
            )
        heaviside = jnp.tanh(phi / SMEAR_WIDTH)
        hold[slot] = adjoint * (0.5 / SMEAR_WIDTH * (1.0 - heaviside * heaviside))

    def body(step, carry):
        load(step, 0).wait()
        load(step, 1).wait()
        for j in range(REINIT_UNROLL):
            block(step * REINIT_UNROLL + j)
        for j in range(REINIT_UNROLL):
            slot = step * REINIT_UNROLL + j
            out_copy(slot).start()
            place = place_ref[slot]
            first = (place // CAP) * EXTRA + place % CAP
            high_ref[pl.ds(first, 1), :] = hold[slot, rows - 1 : rows, :]
            low_ref[pl.ds(first + CAP, 1), :] = hold[slot, 0:1, :]
        return carry

    lax.fori_loop(0, slots // REINIT_UNROLL, body, 0)
    for copy in vel_copies:
        copy.wait()
    behind = low_ref.shape[0] - cells

    def vel_lines(x):
        low_ref[pl.ds(behind + x, 1), :] = vel_low[x, 0:1, :]
        high_ref[pl.ds(behind + x, 1), :] = vel_high[x, 7:8, :]

    by_rows(0, cells, vel_lines)
    for slot in range(slots):
        out_copy(slot).wait()


def pack_lines_kernel(below_ref, above_ref, forcing_ref, out_ref, hold, sem):
    for home in range(hold.shape[0]):
        part = pl.ds(home * EXTRA, EXTRA)
        hold[home] = below_ref[part, :] + above_ref[part, :]
    copy = pltpu.make_async_copy(
        hold, out_ref.at[:, pl.ds(out_ref.shape[1] - EXTRA, EXTRA)], sem
    )
    copy.start()
    copy.wait()


def neighbours(buffer, x, first, rows, lane):
    here = buffer[x + 1, pl.ds(PAD + first, rows), :]
    low_x = buffer[x, pl.ds(PAD + first, rows), :]
    up_x = buffer[x + 2, pl.ds(PAD + first, rows), :]
    low_y = buffer[x + 1, pl.ds(PAD + first - 1, rows), :]
    up_y = buffer[x + 1, pl.ds(PAD + first + 1, rows), :]
    low_z = shift_lanes(here, 1, lane)
    up_z = shift_lanes(here, -1, lane)
    return here, low_x, up_x, low_y, up_y, low_z, up_z


def operator(fields, flags, rate):
    here, low_x, up_x, low_y, up_y, low_z, up_z = fields
    upwind = (
        jnp.where((flags & 1) != 0, low_x, up_x)
        + jnp.where((flags & 2) != 0, low_y, up_y)
        + jnp.where((flags & 4) != 0, low_z, up_z)
    )
    total = (low_x + up_x) + (low_y + up_y) + (low_z + up_z)
    return (1.0 - 6.0 * DIFFUSION) * here + rate * (upwind - 3.0 * here) + DIFFUSION * total


def chunk_copy(src, dst, sem, c):
    part = pl.ds(c * CHUNK, CHUNK)
    return pltpu.make_async_copy(src.at[part], dst.at[part], sem.at[c])


def first_kernel(
    vel_ref, flags_ref, phi_ref, level_ref, xlow_ref, xhigh_ref, ylow_ref, yhigh_ref,
    code_out, twice_out, edge_x_ref, edge_ylow_ref, edge_yhigh_ref, coef_ref, table_ref,
    vel, once, flags, rate, code, twice, tags, sem_tags, sem_vel, sem_flags, sem_phi, sem_code, sem_twice,
):
    cells, rows, lanes = flags.shape
    chunks = cells // CHUNK

    def vel_copy(c):
        return pltpu.make_async_copy(
            vel_ref.at[pl.ds(c * CHUNK, CHUNK)],
            vel.at[pl.ds(1 + c * CHUNK, CHUNK), pl.ds(PAD, rows)],
            sem_vel.at[c],
        )

    def flags_copy(c):
        return chunk_copy(flags_ref, flags, sem_flags, c)

    def code_copy(c):
        return chunk_copy(code, code_out, sem_code, c)

    def twice_copy(c):
        return chunk_copy(twice, twice_out, sem_twice, c)

    tag_copy = pltpu.make_async_copy(level_ref.at[:, pl.ds(CAP * rows, EXTRA)], tags, sem_tags)
    tag_copy.start()

    def start_loads(c, carry):
        vel_copy(c).start()
        flags_copy(c).start()
        return carry

    lax.fori_loop(0, chunks, start_loads, 0)
    for x in range(cells):
        table_ref[x] = -1
    tag_copy.wait()
    for source in range(tags.shape[0]):
        for rank in range(CAP):
            tag = tags[source, rank, 0].astype(I32)

            @pl.when(tag > 0)
            def _():
                table_ref[tag - 1] = source * CAP + rank

    def start(c, carry):
        for j in range(CHUNK):
            x = c * CHUNK + j
            slot = table_ref[x]

            @pl.when(slot >= 0)
            def _():
                pltpu.make_async_copy(
                    block_of(level_ref, slot, rows), rate.at[x], sem_phi.at[c]
                ).start()

            @pl.when(slot < 0)
            def _():
                pltpu.make_async_copy(phi_ref.at[x], rate.at[x], sem_phi.at[c]).start()

        return carry

    lax.fori_loop(0, chunks, start, 0)

    lane = lax.broadcasted_iota(I32, (STRIP, lanes), 1)
    zeros = jnp.zeros((rows + 2 * PAD, lanes), F32)
    vel[0, pl.ds(PAD, rows), :] = xlow_ref[0]
    vel[cells + 1, pl.ds(PAD, rows), :] = xhigh_ref[0]
    once[0] = zeros
    once[cells + 1] = zeros
    line_zero = jnp.zeros((PAD, lanes), F32)

    behind = ylow_ref.shape[0] - cells

    def lines(x):
        vel[x + 1, PAD - 1 : PAD, :] = ylow_ref[pl.ds(behind + x, 1), :]
        vel[x + 1, PAD + rows : PAD + rows + 1, :] = yhigh_ref[pl.ds(behind + x, 1), :]
        once[x + 1, 0:PAD, :] = line_zero
        once[x + 1, PAD + rows : PAD + rows + PAD, :] = line_zero
        slot = jnp.full((1, lanes), table_ref[x].astype(F32), F32)
        edge_ylow_ref[pl.ds(cells + x, 1), :] = slot
        edge_yhigh_ref[pl.ds(cells + x, 1), :] = slot

    by_rows(0, cells, lines)

    def update_once(x):
        for first in range(0, rows, STRIP):
            part = pl.ds(first, STRIP)
            heaviside = jnp.tanh(rate[x, part, :] * (1.0 / SMEAR_WIDTH))
            density = (AIR_DENSITY + 0.5 * (1.0 - AIR_DENSITY)) + (0.5 * (1.0 - AIR_DENSITY)) * heaviside
            rate_here = ADV_RATE / density
            bits = flags[x, part, :]
            rate[x, part, :] = rate_here
            code[x, part, :] = bits.astype(F32) + rate_here
            once[x + 1, pl.ds(PAD + first, STRIP), :] = operator(
                neighbours(vel, x, first, STRIP, lane), bits, rate_here
            )

    def update_twice(x):
        for first in range(0, rows, STRIP):
            part = pl.ds(first, STRIP)
            twice[x, part, :] = operator(
                neighbours(once, x, first, STRIP, lane), flags[x, part, :], rate[x, part, :]
            )

    vel_copy(0).wait()

    def first_pass(c, carry):
        @pl.when(c + 1 < chunks)
        def _():
            vel_copy(c + 1).wait()

        flags_copy(c).wait()
        chunk_copy(phi_ref, rate, sem_phi, c).wait()
        for j in range(CHUNK):
            update_once(c * CHUNK + j)
        code_copy(c).start()
        return carry

    lax.fori_loop(0, chunks, first_pass, 0)
    edge_x_ref[0] = once[1, pl.ds(PAD, rows), :]
    edge_x_ref[1] = once[cells, pl.ds(PAD, rows), :]
    coef_ref[0] = DIFFUSION + jnp.where((flags[0] & 1) != 0, rate[0], 0.0)
    coef_ref[1] = DIFFUSION + jnp.where((flags[cells - 1] & 1) != 0, 0.0, rate[cells - 1])

    def edge_lines(x):
        edge_ylow_ref[pl.ds(x, 1), :] = once[x + 1, PAD : PAD + 1, :]
        edge_yhigh_ref[pl.ds(x, 1), :] = once[x + 1, PAD + rows - 1 : PAD + rows, :]

    by_rows(0, cells, edge_lines)

    def second_pass(c, carry):
        for j in range(CHUNK):
            update_twice(c * CHUNK + j)
        twice_copy(c).start()
        return carry

    lax.fori_loop(0, chunks, second_pass, 0)
    for c in range(chunks):
        code_copy(c).wait()
        twice_copy(c).wait()


def block_of(ref, slot, rows):
    return ref.at[slot // CAP, pl.ds(pl.multiple_of((slot % CAP) * rows, rows), rows)]


def edge_kernel(table_ref, edge_ref, forcing_ref, low_out, high_out):
    rows = low_out.shape[1]
    for side, (x, out) in enumerate(((0, low_out), (table_ref.shape[0] - 1, high_out))):
        slot = table_ref[x]

        @pl.when(slot >= 0)
        def _():
            out[0] = edge_ref[side] + block_of(forcing_ref, slot, rows)[...]

        @pl.when(slot < 0)
        def _():
            out[0] = edge_ref[side]


def last_kernel(
    table_ref, below_ref, above_ref, forcing_ref, code_ref, twice_ref, ylow_ref, yhigh_ref,
    out_ref, part_ref, source, code, twice, sem_code, sem_twice, sem_out,
):
    cells, rows, lanes = code.shape
    chunks = cells // CHUNK
    loads = ((code_ref, code, sem_code), (twice_ref, twice, sem_twice))

    def start(c, carry):
        for load in loads:
            chunk_copy(*load, c).start()
        return carry

    lax.fori_loop(0, chunks, start, 0)
    zeros = jnp.zeros((rows, lanes), F32)
    source[0, pl.ds(PAD, rows), :] = zeros
    source[cells + 1, pl.ds(PAD, rows), :] = zeros

    def fill(x):
        slot = table_ref[x]
        safe = jnp.maximum(slot, 0)
        source[x + 1, pl.ds(PAD, rows), :] = jnp.where(
            slot >= 0, block_of(forcing_ref, safe, rows)[...], 0.0
        )
        for side, slots, halo, at in (
            (0, below_ref, ylow_ref, PAD - 1),
            (1, above_ref, yhigh_ref, PAD + rows),
        ):
            line_slot = slots[x]
            safe = jnp.maximum(line_slot, 0)
            line = forcing_ref[safe // CAP, pl.ds(CAP * rows + side * CAP + safe % CAP, 1), :]
            source[x + 1, at : at + 1, :] = halo[pl.ds(x, 1), :] + jnp.where(
                line_slot >= 0, line, 0.0
            )

    lane = lax.broadcasted_iota(I32, (STRIP, lanes), 1)

    def update(x):
        for first in range(0, rows, STRIP):
            part = pl.ds(first, STRIP)
            fields = neighbours(source, x, first, STRIP, lane)
            both = code[x, part, :]
            bits = both.astype(I32)
            twice[x, part, :] = (
                twice[x, part, :] + fields[0] + operator(fields, bits, both - bits.astype(F32))
            )

    by_rows(0, cells, fill)

    def work(c, carry):
        for load in loads:
            chunk_copy(*load, c).wait()
        for j in range(CHUNK):
            update(c * CHUNK + j)
        chunk_copy(twice, out_ref, sem_out, c).start()
        return carry

    lax.fori_loop(0, chunks, work, 0)
    part_ref[0] = twice[0]
    part_ref[1] = twice[cells - 1]
    for c in range(chunks):
        chunk_copy(twice, out_ref, sem_out, c).wait()


def close_kernel(part_ref, coef_ref, low_ref, high_ref, whole_ref, out_ref, hold, sem):
    cells = out_ref.shape[0]
    hold[0] = part_ref[0] + coef_ref[0] * low_ref[0]
    hold[1] = part_ref[1] + coef_ref[1] * high_ref[0]
    copies = [
        pltpu.make_async_copy(hold.at[0], out_ref.at[0], sem.at[0]),
        pltpu.make_async_copy(hold.at[1], out_ref.at[cells - 1], sem.at[1]),
    ]
    for copy in copies:
        copy.start()
    for copy in copies:
        copy.wait()


def neighbour_pairs(axis):
    count = lax.axis_size(axis)
    forward = [(i, i + 1) for i in range(count - 1)]
    return forward, [(target, source) for source, target in forward]


def local(band_phi, band_seed, owner_map, active_list, brick_phi, adjoint_vel, upwind_flags):
    gx_count = lax.axis_size("gx")
    slots, rows, lanes = band_phi.shape
    cells = brick_phi.shape[0]
    chunks = cells // CHUNK
    up_x, down_x = neighbour_pairs("gx")
    up_y, down_y = neighbour_pairs("gy")
    shape = jax.ShapeDtypeStruct
    dma = pltpu.SemaphoreType.DMA
    brick = (cells, rows, lanes)
    padded = (cells + 2, rows + 2 * PAD, lanes)
    sent = (gx_count, CAP * rows + EXTRA, lanes)
    owners, slabs = owner_map.T, active_list.T

    level_sent = pl.pallas_call(
        pack_level_kernel,
        out_shape=shape(sent, F32),
        in_specs=[SMEM, SMEM, HBM],
        out_specs=HBM,
        scratch_shapes=[
            pltpu.VMEM((slots, rows, lanes), F32),
            pltpu.VMEM((gx_count, EXTRA, lanes), F32),
            pltpu.SMEM((gx_count,), I32),
            dma((slots,)), dma((slots,)), dma(()),
        ],
        compiler_params=params(BIG),
        cost_estimate=cost(2, 1000),
        name="pack_level",
    )(owners, slabs, band_phi)
    level = lax.all_to_all(level_sent, "gx", split_axis=0, concat_axis=0, tiled=True)

    lines = (gx_count * EXTRA + cells, lanes)
    v_xlow = lax.ppermute(adjoint_vel[cells - 1 :], "gx", up_x)
    v_xhigh = lax.ppermute(adjoint_vel[:1], "gx", down_x)
    forcing_sent, low_lines, high_lines = pl.pallas_call(
        reinit_kernel,
        out_shape=(shape(sent, F32), shape(lines, F32), shape(lines, F32)),
        in_specs=[SMEM, HBM, HBM, HBM],
        out_specs=(HBM, VMEM, VMEM),
        scratch_shapes=[
            pltpu.VMEM((slots, rows, lanes), F32),
            pltpu.VMEM((slots, rows, lanes), F32),
            pltpu.VMEM((slots, rows, lanes), F32),
            pltpu.VMEM((cells, 8, lanes), F32),
            pltpu.VMEM((cells, 8, lanes), F32),
            pltpu.SMEM((gx_count,), I32),
            pltpu.SMEM((slots,), I32),
            dma((2, slots // REINIT_UNROLL)), dma((2,)), dma((slots,)),
        ],
        compiler_params=params(BIG),
        cost_estimate=cost(20, 40_000_000),
        name="reinit",
    )(owners, band_phi, band_seed, adjoint_vel)
    below_lines = lax.ppermute(high_lines, "gy", up_y)
    above_lines = lax.ppermute(low_lines, "gy", down_y)
    v_xlow, v_xhigh, below_lines, above_lines = lax.optimization_barrier(
        (v_xlow, v_xhigh, below_lines, above_lines)
    )
    forcing_sent = pl.pallas_call(
        pack_lines_kernel,
        out_shape=shape(sent, F32),
        in_specs=[VMEM, VMEM, HBM],
        out_specs=HBM,
        scratch_shapes=[pltpu.VMEM((gx_count, EXTRA, lanes), F32), dma(())],
        input_output_aliases={2: 0},
        compiler_params=params(MEDIUM),
        cost_estimate=cost(2, 1000),
        name="pack_lines",
    )(below_lines, above_lines, forcing_sent)
    forcing = lax.all_to_all(forcing_sent, "gx", split_axis=0, concat_axis=0, tiled=True)

    edge_lines = (2 * cells, lanes)
    code, twice, edge_x, edge_ylow, edge_yhigh, coef, table = pl.pallas_call(
        first_kernel,
        out_shape=(
            shape(brick, F32),
            shape(brick, F32),
            shape((2, rows, lanes), F32),
            shape(edge_lines, F32),
            shape(edge_lines, F32),
            shape((2, rows, lanes), F32),
            shape((cells,), I32),
        ),
        in_specs=[HBM, HBM, HBM, HBM, VMEM, VMEM, VMEM, VMEM],
        out_specs=(HBM, HBM, VMEM, VMEM, VMEM, VMEM, SMEM),
        scratch_shapes=[
            pltpu.VMEM(padded, F32),
            pltpu.VMEM(padded, F32),
            pltpu.VMEM(brick, I32),
            pltpu.VMEM(brick, F32),
            pltpu.VMEM(brick, F32),
            pltpu.VMEM(brick, F32),
            pltpu.SMEM((gx_count, EXTRA, lanes), F32),
            dma(()),
            dma((chunks,)), dma((chunks,)), dma((chunks,)), dma((chunks,)), dma((chunks,)),
        ],
        compiler_params=params(ROOMY),
        cost_estimate=cost(30, 60_000_000),
        name="two_updates",
    )(adjoint_vel, upwind_flags, brick_phi, level, v_xlow, v_xhigh, below_lines, above_lines)
    once_ylow = lax.ppermute(edge_yhigh, "gy", up_y)
    once_yhigh = lax.ppermute(edge_ylow, "gy", down_y)
    gy = lax.axis_index("gy")
    below = jnp.where(gy > 0, once_ylow[cells:, 0].astype(I32), -1)
    above = jnp.where(gy < lax.axis_size("gy") - 1, once_yhigh[cells:, 0].astype(I32), -1)

    edge_x, below, above = lax.optimization_barrier((edge_x, below, above))

    low_slab, high_slab = pl.pallas_call(
        edge_kernel,
        out_shape=(shape((1, rows, lanes), F32), shape((1, rows, lanes), F32)),
        in_specs=[SMEM, VMEM, VMEM],
        out_specs=(VMEM, VMEM),
        compiler_params=params(SMALL),
        cost_estimate=cost(1, 1000),
        name="edge_slabs",
    )(table, edge_x, forcing)
    from_low = lax.ppermute(high_slab, "gx", up_x)
    from_high = lax.ppermute(low_slab, "gx", down_x)

    out, part = pl.pallas_call(
        last_kernel,
        out_shape=(shape(brick, F32), shape((2, rows, lanes), F32)),
        in_specs=[SMEM, SMEM, SMEM, VMEM, HBM, HBM, VMEM, VMEM],
        out_specs=(HBM, VMEM),
        scratch_shapes=[
            pltpu.VMEM(padded, F32),
            pltpu.VMEM(brick, F32),
            pltpu.VMEM(brick, F32),
            dma((chunks,)), dma((chunks,)), dma((chunks,)),
        ],
        compiler_params=params(ROOMY),
        cost_estimate=cost(30, 60_000_000),
        name="add_forcing",
    )(table, below, above, forcing, code, twice, once_ylow, once_yhigh)

    return pl.pallas_call(
        close_kernel,
        out_shape=shape(brick, F32),
        in_specs=[VMEM, VMEM, VMEM, VMEM, HBM],
        out_specs=HBM,
        scratch_shapes=[pltpu.VMEM((2, rows, lanes), F32), dma((2,))],
        input_output_aliases={4: 0},
        compiler_params=params(SMALL),
        cost_estimate=cost(1, 1000),
        name="close_slabs",
    )(part, coef, from_low, from_high, out)


def solution(mesh):
    in_specs = (
        P("gx", "gy", None),
        P("gx", "gy", None),
        P("gx", "gy"),
        P("gx", "gy"),
        P("gx", "gy", None),
        P("gx", "gy", None),
        P("gx", "gy", None),
    )
    out_specs = P("gx", "gy", None)
    return jax.shard_map(local, mesh=mesh, in_specs=in_specs, out_specs=out_specs, check_vma=False)
```

```python
import jax
import jax.numpy as jnp
from jax import lax
from jax.experimental import pallas as pl
from jax.experimental.pallas import tpu as pltpu
from jax.sharding import PartitionSpec as P

CAP = 2
REINIT = 4
REINIT_STEP = 0.4
ADV_RATE = 0.25
DIFFUSION = 0.1
AIR_DENSITY = 0.3
SMEAR_WIDTH = 1.5

F32 = jnp.float32
I32 = jnp.int32
MIB = 1 << 20
HBM = pl.BlockSpec(memory_space=pltpu.HBM)
VMEM = pl.BlockSpec(memory_space=pltpu.VMEM)
SMEM = pl.BlockSpec(memory_space=pltpu.SMEM)
EXTRA = 8
PAD = 8
CHUNK = 8
STRIP = 32
UNROLL = 4
REINIT_UNROLL = 2


BIG = 62
MEDIUM = 52
ROOMY = 50
SMALL = 4


def params(mib):
    return pltpu.CompilerParams(vmem_limit_bytes=mib * MIB)


def cost(mib, flops):
    return pl.CostEstimate(flops=flops, bytes_accessed=mib * MIB, transcendentals=0)


def by_rows(first, last, body):
    def step(i, carry):
        for j in range(UNROLL):
            body(first + i * UNROLL + j)
        return carry

    lax.fori_loop(0, (last - first) // UNROLL, step, 0)


def homes_and_ranks(owner_ref, count_ref):
    for home in range(count_ref.shape[0]):
        count_ref[home] = 0
    result = []
    for slot in range(owner_ref.shape[1]):
        home = owner_ref[0, slot]
        rank = count_ref[home]
        count_ref[home] = rank + 1
        result.append((home, rank))
    return result


def pack_level_kernel(
    owner_hbm, slab_hbm, phi_ref, out_ref, owner_ref, slab_ref, phi, tags, count_ref, load_sem, sem, tag_sem
):
    slots, rows, lanes = phi_ref.shape
    loads = [
        pltpu.make_async_copy(phi_ref.at[slot], phi.at[slot], load_sem.at[slot])
        for slot in range(slots)
    ]
    scalars = [
        pltpu.make_async_copy(owner_hbm, owner_ref, load_sem.at[slots]),
        pltpu.make_async_copy(slab_hbm, slab_ref, load_sem.at[slots + 1]),
    ]
    for load in scalars + loads:
        load.start()
    tags[...] = jnp.zeros_like(tags)
    for load in scalars:
        load.wait()
    places = homes_and_ranks(owner_ref, count_ref)
    for slot, (home, rank) in enumerate(places):
        label = (slab_ref[0, slot] + 1).astype(F32)
        tags[home, pl.ds(rank, 1), :] = jnp.full((1, lanes), label, F32)
    copies = [pltpu.make_async_copy(tags, out_ref.at[:, pl.ds(CAP * rows, EXTRA)], tag_sem)]
    copies[0].start()
    for slot, (home, rank) in enumerate(places):
        loads[slot].wait()
        copy = pltpu.make_async_copy(
            phi.at[slot],
            out_ref.at[home, pl.ds(pl.multiple_of(rank * rows, rows), rows)],
            sem.at[slot],
        )
        copy.start()
        copies.append(copy)
    for copy in copies:
        copy.wait()


def shift_rows(values, step, row):
    rows = values.shape[0]
    moved = pltpu.roll(values, step % rows, 0)
    return jnp.where(row == (0 if step == 1 else rows - 1), 0.0, moved)


def shift_lanes(values, step, lane):
    lanes = values.shape[1]
    moved = pltpu.roll(values, step % lanes, 1)
    return jnp.where(lane == (0 if step == 1 else lanes - 1), 0.0, moved)


def reinit_kernel(
    owner_ref, phi_hbm, seed_hbm, vel_hbm, out_ref, low_ref, high_ref,
    phi_ref, seed_ref, hold, vel_low, vel_high, count_ref, place_ref, load_sem, vel_sem, sem,
):
    slots, rows, lanes = phi_ref.shape

    def load(step, which):
        part = pl.ds(step * REINIT_UNROLL, REINIT_UNROLL)
        src, dst = ((phi_hbm, phi_ref), (seed_hbm, seed_ref))[which]
        return pltpu.make_async_copy(src.at[part], dst.at[part], load_sem.at[which, step])

    for step in range(slots // REINIT_UNROLL):
        load(step, 0).start()
        load(step, 1).start()
    cells = vel_hbm.shape[0]
    vel_copies = [
        pltpu.make_async_copy(vel_hbm.at[:, pl.ds(0, 8)], vel_low, vel_sem.at[0]),
        pltpu.make_async_copy(vel_hbm.at[:, pl.ds(rows - 8, 8)], vel_high, vel_sem.at[1]),
    ]
    for copy in vel_copies:
        copy.start()
    for slot, (home, rank) in enumerate(homes_and_ranks(owner_ref, count_ref)):
        place_ref[slot] = home * CAP + rank
    row = lax.broadcasted_iota(I32, (rows, lanes), 0)
    lane = lax.broadcasted_iota(I32, (rows, lanes), 1)
    low_ref[...] = jnp.zeros_like(low_ref)
    high_ref[...] = jnp.zeros_like(high_ref)

    def out_copy(slot):
        place = place_ref[slot]
        return pltpu.make_async_copy(
            hold.at[slot],
            out_ref.at[place // CAP, pl.ds(pl.multiple_of((place % CAP) * rows, rows), rows)],
            sem.at[slot],
        )

    def block(slot):
        phi = phi_ref[slot]
        up_y = jnp.where(row == rows - 1, phi, pltpu.roll(phi, rows - 1, 0))
        low_y = jnp.where(row == 0, phi, pltpu.roll(phi, 1, 0))
        up_z = jnp.where(lane == lanes - 1, phi, pltpu.roll(phi, lanes - 1, 1))
        low_z = jnp.where(lane == 0, phi, pltpu.roll(phi, 1, 1))
        grad_y = 0.5 * (up_y - low_y)
        grad_z = 0.5 * (up_z - low_z)
        normal = jnp.sqrt(grad_y * grad_y + grad_z * grad_z + 1.0)
        sign = phi / jnp.sqrt(phi * phi + 1.0)
        scale = (0.5 * REINIT_STEP) * sign / normal
        weight_y = scale * grad_y
        weight_z = scale * grad_z
        adjoint = seed_ref[slot]
        for _ in range(REINIT):
            flux_y = weight_y * adjoint
            flux_z = weight_z * adjoint
            adjoint = adjoint + (
                (shift_rows(flux_y, -1, row) - shift_rows(flux_y, 1, row))
                + (shift_lanes(flux_z, -1, lane) - shift_lanes(flux_z, 1, lane))
            )
        heaviside = jnp.tanh(phi / SMEAR_WIDTH)
        hold[slot] = adjoint * (0.5 / SMEAR_WIDTH * (1.0 - heaviside * heaviside))

    def body(step, carry):
        load(step, 0).wait()
        load(step, 1).wait()
        for j in range(REINIT_UNROLL):
            block(step * REINIT_UNROLL + j)
        for j in range(REINIT_UNROLL):
            slot = step * REINIT_UNROLL + j
            out_copy(slot).start()
            place = place_ref[slot]
            first = (place // CAP) * EXTRA + place % CAP
            high_ref[pl.ds(first, 1), :] = hold[slot, rows - 1 : rows, :]
            low_ref[pl.ds(first + CAP, 1), :] = hold[slot, 0:1, :]
        return carry

    lax.fori_loop(0, slots // REINIT_UNROLL, body, 0)
    for copy in vel_copies:
        copy.wait()
    behind = low_ref.shape[0] - cells

    def vel_lines(x):
        low_ref[pl.ds(behind + x, 1), :] = vel_low[x, 0:1, :]
        high_ref[pl.ds(behind + x, 1), :] = vel_high[x, 7:8, :]

    by_rows(0, cells, vel_lines)
    for slot in range(slots):
        out_copy(slot).wait()


def pack_lines_kernel(below_ref, above_ref, forcing_ref, out_ref, hold, sem):
    for home in range(hold.shape[0]):
        part = pl.ds(home * EXTRA, EXTRA)
        hold[home] = below_ref[part, :] + above_ref[part, :]
    copy = pltpu.make_async_copy(
        hold, out_ref.at[:, pl.ds(out_ref.shape[1] - EXTRA, EXTRA)], sem
    )
    copy.start()
    copy.wait()


def neighbours(buffer, x, first, rows, lane):
    here = buffer[x + 1, pl.ds(PAD + first, rows), :]
    low_x = buffer[x, pl.ds(PAD + first, rows), :]
    up_x = buffer[x + 2, pl.ds(PAD + first, rows), :]
    low_y = buffer[x + 1, pl.ds(PAD + first - 1, rows), :]
    up_y = buffer[x + 1, pl.ds(PAD + first + 1, rows), :]
    low_z = shift_lanes(here, 1, lane)
    up_z = shift_lanes(here, -1, lane)
    return here, low_x, up_x, low_y, up_y, low_z, up_z


def operator(fields, flags, rate):
    here, low_x, up_x, low_y, up_y, low_z, up_z = fields
    upwind = (
        jnp.where((flags & 1) != 0, low_x, up_x)
        + jnp.where((flags & 2) != 0, low_y, up_y)
        + jnp.where((flags & 4) != 0, low_z, up_z)
    )
    total = (low_x + up_x) + (low_y + up_y) + (low_z + up_z)
    return (1.0 - 6.0 * DIFFUSION) * here + rate * (upwind - 3.0 * here) + DIFFUSION * total


def chunk_copy(src, dst, sem, c):
    part = pl.ds(c * CHUNK, CHUNK)
    return pltpu.make_async_copy(src.at[part], dst.at[part], sem.at[c])


def first_kernel(
    vel_ref, flags_ref, phi_ref, level_ref, xlow_ref, xhigh_ref, ylow_ref, yhigh_ref,
    code_out, twice_out, edge_x_ref, edge_ylow_ref, edge_yhigh_ref, coef_ref, table_ref,
    vel, once, flags, rate, code, twice, tags, sem_tags, sem_vel, sem_flags, sem_phi, sem_code, sem_twice,
):
    cells, rows, lanes = flags.shape
    chunks = cells // CHUNK

    def vel_copy(c):
        return pltpu.make_async_copy(
            vel_ref.at[pl.ds(c * CHUNK, CHUNK)],
            vel.at[pl.ds(1 + c * CHUNK, CHUNK), pl.ds(PAD, rows)],
            sem_vel.at[c],
        )

    def flags_copy(c):
        return chunk_copy(flags_ref, flags, sem_flags, c)

    def code_copy(c):
        return chunk_copy(code, code_out, sem_code, c)

    def twice_copy(c):
        return chunk_copy(twice, twice_out, sem_twice, c)

    tag_copy = pltpu.make_async_copy(level_ref.at[:, pl.ds(CAP * rows, EXTRA)], tags, sem_tags)
    tag_copy.start()

    def start_loads(c, carry):
        vel_copy(c).start()
        flags_copy(c).start()
        return carry

    lax.fori_loop(0, chunks, start_loads, 0)
    for x in range(cells):
        table_ref[x] = -1
    tag_copy.wait()
    for source in range(tags.shape[0]):
        for rank in range(CAP):
            tag = tags[source, rank, 0].astype(I32)

            @pl.when(tag > 0)
            def _():
                table_ref[tag - 1] = source * CAP + rank

    def start(c, carry):
        for j in range(CHUNK):
            x = c * CHUNK + j
            slot = table_ref[x]

            @pl.when(slot >= 0)
            def _():
                pltpu.make_async_copy(
                    block_of(level_ref, slot, rows), rate.at[x], sem_phi.at[c]
                ).start()

            @pl.when(slot < 0)
            def _():
                pltpu.make_async_copy(phi_ref.at[x], rate.at[x], sem_phi.at[c]).start()

        return carry

    lax.fori_loop(0, chunks, start, 0)

    lane = lax.broadcasted_iota(I32, (STRIP, lanes), 1)
    zeros = jnp.zeros((rows + 2 * PAD, lanes), F32)
    vel[0, pl.ds(PAD, rows), :] = xlow_ref[0]
    vel[cells + 1, pl.ds(PAD, rows), :] = xhigh_ref[0]
    once[0] = zeros
    once[cells + 1] = zeros
    line_zero = jnp.zeros((PAD, lanes), F32)

    behind = ylow_ref.shape[0] - cells

    def lines(x):
        vel[x + 1, PAD - 1 : PAD, :] = ylow_ref[pl.ds(behind + x, 1), :]
        vel[x + 1, PAD + rows : PAD + rows + 1, :] = yhigh_ref[pl.ds(behind + x, 1), :]
        once[x + 1, 0:PAD, :] = line_zero
        once[x + 1, PAD + rows : PAD + rows + PAD, :] = line_zero
        slot = jnp.full((1, lanes), table_ref[x].astype(F32), F32)
        edge_ylow_ref[pl.ds(cells + x, 1), :] = slot
        edge_yhigh_ref[pl.ds(cells + x, 1), :] = slot

    by_rows(0, cells, lines)

    def update_once(x):
        for first in range(0, rows, STRIP):
            part = pl.ds(first, STRIP)
            heaviside = jnp.tanh(rate[x, part, :] * (1.0 / SMEAR_WIDTH))
            density = (AIR_DENSITY + 0.5 * (1.0 - AIR_DENSITY)) + (0.5 * (1.0 - AIR_DENSITY)) * heaviside
            rate_here = ADV_RATE / density
            bits = flags[x, part, :]
            rate[x, part, :] = rate_here
            code[x, part, :] = bits.astype(F32) + rate_here
            once[x + 1, pl.ds(PAD + first, STRIP), :] = operator(
                neighbours(vel, x, first, STRIP, lane), bits, rate_here
            )

    def update_twice(x):
        for first in range(0, rows, STRIP):
            part = pl.ds(first, STRIP)
            twice[x, part, :] = operator(
                neighbours(once, x, first, STRIP, lane), flags[x, part, :], rate[x, part, :]
            )

    def second_pass(c):
        for j in range(CHUNK):
            update_twice(c * CHUNK + j)
        twice_copy(c).start()

    vel_copy(0).wait()

    def first_pass(c, carry):
        @pl.when(c + 1 < chunks)
        def _():
            vel_copy(c + 1).wait()

        flags_copy(c).wait()
        chunk_copy(phi_ref, rate, sem_phi, c).wait()
        for j in range(CHUNK):
            update_once(c * CHUNK + j)
        code_copy(c).start()

        @pl.when(c > 0)
        def _():
            second_pass(c - 1)

        return carry

    lax.fori_loop(0, chunks, first_pass, 0)
    second_pass(chunks - 1)
    edge_x_ref[0] = once[1, pl.ds(PAD, rows), :]
    edge_x_ref[1] = once[cells, pl.ds(PAD, rows), :]
    coef_ref[0] = DIFFUSION + jnp.where((flags[0] & 1) != 0, rate[0], 0.0)
    coef_ref[1] = DIFFUSION + jnp.where((flags[cells - 1] & 1) != 0, 0.0, rate[cells - 1])

    def edge_lines(x):
        edge_ylow_ref[pl.ds(x, 1), :] = once[x + 1, PAD : PAD + 1, :]
        edge_yhigh_ref[pl.ds(x, 1), :] = once[x + 1, PAD + rows - 1 : PAD + rows, :]

    by_rows(0, cells, edge_lines)

    for c in range(chunks):
        code_copy(c).wait()
        twice_copy(c).wait()


def block_of(ref, slot, rows):
    return ref.at[slot // CAP, pl.ds(pl.multiple_of((slot % CAP) * rows, rows), rows)]


def edge_kernel(table_ref, edge_ref, forcing_ref, low_out, high_out):
    rows = low_out.shape[1]
    for side, (x, out) in enumerate(((0, low_out), (table_ref.shape[0] - 1, high_out))):
        slot = table_ref[x]

        @pl.when(slot >= 0)
        def _():
            out[0] = edge_ref[side] + block_of(forcing_ref, slot, rows)[...]

        @pl.when(slot < 0)
        def _():
            out[0] = edge_ref[side]


def last_kernel(
    table_ref, below_ref, above_ref, forcing_ref, code_ref, twice_ref, ylow_ref, yhigh_ref,
    out_ref, part_ref, source, code, twice, sem_code, sem_twice, sem_out,
):
    cells, rows, lanes = code.shape
    chunks = cells // CHUNK
    loads = ((code_ref, code, sem_code), (twice_ref, twice, sem_twice))

    def start(c, carry):
        for load in loads:
            chunk_copy(*load, c).start()
        return carry

    lax.fori_loop(0, chunks, start, 0)
    zeros = jnp.zeros((rows, lanes), F32)
    source[0, pl.ds(PAD, rows), :] = zeros
    source[cells + 1, pl.ds(PAD, rows), :] = zeros

    def fill(x):
        slot = table_ref[x]
        safe = jnp.maximum(slot, 0)
        source[x + 1, pl.ds(PAD, rows), :] = jnp.where(
            slot >= 0, block_of(forcing_ref, safe, rows)[...], 0.0
        )
        for side, slots, halo, at in (
            (0, below_ref, ylow_ref, PAD - 1),
            (1, above_ref, yhigh_ref, PAD + rows),
        ):
            line_slot = slots[x]
            safe = jnp.maximum(line_slot, 0)
            line = forcing_ref[safe // CAP, pl.ds(CAP * rows + side * CAP + safe % CAP, 1), :]
            source[x + 1, at : at + 1, :] = halo[pl.ds(x, 1), :] + jnp.where(
                line_slot >= 0, line, 0.0
            )

    lane = lax.broadcasted_iota(I32, (STRIP, lanes), 1)

    def update(x):
        for first in range(0, rows, STRIP):
            part = pl.ds(first, STRIP)
            fields = neighbours(source, x, first, STRIP, lane)
            both = code[x, part, :]
            bits = both.astype(I32)
            twice[x, part, :] = (
                twice[x, part, :] + fields[0] + operator(fields, bits, both - bits.astype(F32))
            )

    by_rows(0, cells, fill)

    def work(c, carry):
        for load in loads:
            chunk_copy(*load, c).wait()
        for j in range(CHUNK):
            update(c * CHUNK + j)
        chunk_copy(twice, out_ref, sem_out, c).start()
        return carry

    lax.fori_loop(0, chunks, work, 0)
    part_ref[0] = twice[0]
    part_ref[1] = twice[cells - 1]
    for c in range(chunks):
        chunk_copy(twice, out_ref, sem_out, c).wait()


def close_kernel(part_ref, coef_ref, low_ref, high_ref, whole_ref, out_ref, hold, sem):
    cells = out_ref.shape[0]
    hold[0] = part_ref[0] + coef_ref[0] * low_ref[0]
    hold[1] = part_ref[1] + coef_ref[1] * high_ref[0]
    copies = [
        pltpu.make_async_copy(hold.at[0], out_ref.at[0], sem.at[0]),
        pltpu.make_async_copy(hold.at[1], out_ref.at[cells - 1], sem.at[1]),
    ]
    for copy in copies:
        copy.start()
    for copy in copies:
        copy.wait()


def neighbour_pairs(axis):
    count = lax.axis_size(axis)
    forward = [(i, i + 1) for i in range(count - 1)]
    return forward, [(target, source) for source, target in forward]


def local(band_phi, band_seed, owner_map, active_list, brick_phi, adjoint_vel, upwind_flags):
    gx_count = lax.axis_size("gx")
    slots, rows, lanes = band_phi.shape
    cells = brick_phi.shape[0]
    chunks = cells // CHUNK
    up_x, down_x = neighbour_pairs("gx")
    up_y, down_y = neighbour_pairs("gy")
    shape = jax.ShapeDtypeStruct
    dma = pltpu.SemaphoreType.DMA
    brick = (cells, rows, lanes)
    padded = (cells + 2, rows + 2 * PAD, lanes)
    sent = (gx_count, CAP * rows + EXTRA, lanes)
    owners, slabs = owner_map.T, active_list.T

    level_sent = pl.pallas_call(
        pack_level_kernel,
        out_shape=shape(sent, F32),
        in_specs=[HBM, HBM, HBM],
        out_specs=HBM,
        scratch_shapes=[
            pltpu.SMEM((1, slots), I32),
            pltpu.SMEM((1, slots), I32),
            pltpu.VMEM((slots, rows, lanes), F32),
            pltpu.VMEM((gx_count, EXTRA, lanes), F32),
            pltpu.SMEM((gx_count,), I32),
            dma((slots + 2,)), dma((slots,)), dma(()),
        ],
        compiler_params=params(BIG),
        cost_estimate=cost(2, 1000),
        name="pack_level",
    )(owners, slabs, band_phi)
    level = lax.all_to_all(level_sent, "gx", split_axis=0, concat_axis=0, tiled=True)

    lines = (gx_count * EXTRA + cells, lanes)
    v_xlow = lax.ppermute(adjoint_vel[cells - 1 :], "gx", up_x)
    v_xhigh = lax.ppermute(adjoint_vel[:1], "gx", down_x)
    forcing_sent, low_lines, high_lines = pl.pallas_call(
        reinit_kernel,
        out_shape=(shape(sent, F32), shape(lines, F32), shape(lines, F32)),
        in_specs=[SMEM, HBM, HBM, HBM],
        out_specs=(HBM, VMEM, VMEM),
        scratch_shapes=[
            pltpu.VMEM((slots, rows, lanes), F32),
            pltpu.VMEM((slots, rows, lanes), F32),
            pltpu.VMEM((slots, rows, lanes), F32),
            pltpu.VMEM((cells, 8, lanes), F32),
            pltpu.VMEM((cells, 8, lanes), F32),
            pltpu.SMEM((gx_count,), I32),
            pltpu.SMEM((slots,), I32),
            dma((2, slots // REINIT_UNROLL)), dma((2,)), dma((slots,)),
        ],
        compiler_params=params(BIG),
        cost_estimate=cost(20, 40_000_000),
        name="reinit",
    )(owners, band_phi, band_seed, adjoint_vel)
    below_lines = lax.ppermute(high_lines, "gy", up_y)
    above_lines = lax.ppermute(low_lines, "gy", down_y)
    v_xlow, v_xhigh, below_lines, above_lines = lax.optimization_barrier(
        (v_xlow, v_xhigh, below_lines, above_lines)
    )
    forcing_sent = pl.pallas_call(
        pack_lines_kernel,
        out_shape=shape(sent, F32),
        in_specs=[VMEM, VMEM, HBM],
        out_specs=HBM,
        scratch_shapes=[pltpu.VMEM((gx_count, EXTRA, lanes), F32), dma(())],
        input_output_aliases={2: 0},
        compiler_params=params(MEDIUM),
        cost_estimate=cost(2, 1000),
        name="pack_lines",
    )(below_lines, above_lines, forcing_sent)
    forcing = lax.all_to_all(forcing_sent, "gx", split_axis=0, concat_axis=0, tiled=True)

    edge_lines = (2 * cells, lanes)
    code, twice, edge_x, edge_ylow, edge_yhigh, coef, table = pl.pallas_call(
        first_kernel,
        out_shape=(
            shape(brick, F32),
            shape(brick, F32),
            shape((2, rows, lanes), F32),
            shape(edge_lines, F32),
            shape(edge_lines, F32),
            shape((2, rows, lanes), F32),
            shape((cells,), I32),
        ),
        in_specs=[HBM, HBM, HBM, HBM, VMEM, VMEM, VMEM, VMEM],
        out_specs=(HBM, HBM, VMEM, VMEM, VMEM, VMEM, SMEM),
        scratch_shapes=[
            pltpu.VMEM(padded, F32),
            pltpu.VMEM(padded, F32),
            pltpu.VMEM(brick, I32),
            pltpu.VMEM(brick, F32),
            pltpu.VMEM(brick, F32),
            pltpu.VMEM(brick, F32),
            pltpu.SMEM((gx_count, EXTRA, lanes), F32),
            dma(()),
            dma((chunks,)), dma((chunks,)), dma((chunks,)), dma((chunks,)), dma((chunks,)),
        ],
        compiler_params=params(ROOMY),
        cost_estimate=cost(30, 60_000_000),
        name="two_updates",
    )(adjoint_vel, upwind_flags, brick_phi, level, v_xlow, v_xhigh, below_lines, above_lines)
    once_ylow = lax.ppermute(edge_yhigh, "gy", up_y)
    once_yhigh = lax.ppermute(edge_ylow, "gy", down_y)
    gy = lax.axis_index("gy")
    below = jnp.where(gy > 0, once_ylow[cells:, 0].astype(I32), -1)
    above = jnp.where(gy < lax.axis_size("gy") - 1, once_yhigh[cells:, 0].astype(I32), -1)

    edge_x, below, above = lax.optimization_barrier((edge_x, below, above))

    low_slab, high_slab = pl.pallas_call(
        edge_kernel,
        out_shape=(shape((1, rows, lanes), F32), shape((1, rows, lanes), F32)),
        in_specs=[SMEM, VMEM, VMEM],
        out_specs=(VMEM, VMEM),
        compiler_params=params(SMALL),
        cost_estimate=cost(1, 1000),
        name="edge_slabs",
    )(table, edge_x, forcing)
    from_low = lax.ppermute(high_slab, "gx", up_x)
    from_high = lax.ppermute(low_slab, "gx", down_x)

    out, part = pl.pallas_call(
        last_kernel,
        out_shape=(shape(brick, F32), shape((2, rows, lanes), F32)),
        in_specs=[SMEM, SMEM, SMEM, VMEM, HBM, HBM, VMEM, VMEM],
        out_specs=(HBM, VMEM),
        scratch_shapes=[
            pltpu.VMEM(padded, F32),
            pltpu.VMEM(brick, F32),
            pltpu.VMEM(brick, F32),
            dma((chunks,)), dma((chunks,)), dma((chunks,)),
        ],
        compiler_params=params(ROOMY),
        cost_estimate=cost(30, 60_000_000),
        name="add_forcing",
    )(table, below, above, forcing, code, twice, once_ylow, once_yhigh)

    return pl.pallas_call(
        close_kernel,
        out_shape=shape(brick, F32),
        in_specs=[VMEM, VMEM, VMEM, VMEM, HBM],
        out_specs=HBM,
        scratch_shapes=[pltpu.VMEM((2, rows, lanes), F32), dma((2,))],
        input_output_aliases={4: 0},
        compiler_params=params(SMALL),
        cost_estimate=cost(1, 1000),
        name="close_slabs",
    )(part, coef, from_low, from_high, out)


def solution(mesh):
    in_specs = (
        P("gx", "gy", None),
        P("gx", "gy", None),
        P("gx", "gy"),
        P("gx", "gy"),
        P("gx", "gy", None),
        P("gx", "gy", None),
        P("gx", "gy", None),
    )
    out_specs = P("gx", "gy", None)
    return jax.shard_map(local, mesh=mesh, in_specs=in_specs, out_specs=out_specs, check_vma=False)
```

```python
import jax
import jax.numpy as jnp
from jax import lax
from jax.experimental import pallas as pl
from jax.experimental.pallas import tpu as pltpu
from jax.sharding import PartitionSpec as P

CAP = 2
REINIT = 4
REINIT_STEP = 0.4
ADV_RATE = 0.25
DIFFUSION = 0.1
AIR_DENSITY = 0.3
SMEAR_WIDTH = 1.5

F32 = jnp.float32
I32 = jnp.int32
MIB = 1 << 20
HBM = pl.BlockSpec(memory_space=pltpu.HBM)
VMEM = pl.BlockSpec(memory_space=pltpu.VMEM)
SMEM = pl.BlockSpec(memory_space=pltpu.SMEM)
EXTRA = 8
PAD = 8
CHUNK = 8
STRIP = 32
UNROLL = 4
REINIT_UNROLL = 2


BIG = 62
MEDIUM = 52
ROOMY = 50
SMALL = 4


def params(mib):
    return pltpu.CompilerParams(vmem_limit_bytes=mib * MIB)


def cost(mib, flops):
    return pl.CostEstimate(flops=flops, bytes_accessed=mib * MIB, transcendentals=0)


def by_rows(first, last, body):
    def step(i, carry):
        for j in range(UNROLL):
            body(first + i * UNROLL + j)
        return carry

    lax.fori_loop(0, (last - first) // UNROLL, step, 0)


def homes_and_ranks(owner_ref, count_ref):
    for home in range(count_ref.shape[0]):
        count_ref[home] = 0
    result = []
    for slot in range(owner_ref.shape[1]):
        home = owner_ref[0, slot]
        rank = count_ref[home]
        count_ref[home] = rank + 1
        result.append((home, rank))
    return result


def pack_level_kernel(
    owner_hbm, slab_hbm, phi_ref, out_ref, owner_ref, slab_ref, phi, tags, count_ref, load_sem, sem, tag_sem
):
    slots, rows, lanes = phi_ref.shape
    loads = [
        pltpu.make_async_copy(phi_ref.at[slot], phi.at[slot], load_sem.at[slot])
        for slot in range(slots)
    ]
    scalars = [
        pltpu.make_async_copy(owner_hbm, owner_ref, load_sem.at[slots]),
        pltpu.make_async_copy(slab_hbm, slab_ref, load_sem.at[slots + 1]),
    ]
    for load in scalars + loads:
        load.start()
    tags[...] = jnp.zeros_like(tags)
    for load in scalars:
        load.wait()
    places = homes_and_ranks(owner_ref, count_ref)
    for slot, (home, rank) in enumerate(places):
        label = (slab_ref[0, slot] + 1).astype(F32)
        tags[home, pl.ds(rank, 1), :] = jnp.full((1, lanes), label, F32)
    copies = [pltpu.make_async_copy(tags, out_ref.at[:, pl.ds(CAP * rows, EXTRA)], tag_sem)]
    copies[0].start()
    for slot, (home, rank) in enumerate(places):
        loads[slot].wait()
        copy = pltpu.make_async_copy(
            phi.at[slot],
            out_ref.at[home, pl.ds(pl.multiple_of(rank * rows, rows), rows)],
            sem.at[slot],
        )
        copy.start()
        copies.append(copy)
    for copy in copies:
        copy.wait()


def shift_rows(values, step, row):
    rows = values.shape[0]
    moved = pltpu.roll(values, step % rows, 0)
    return jnp.where(row == (0 if step == 1 else rows - 1), 0.0, moved)


def shift_lanes(values, step, lane):
    lanes = values.shape[1]
    moved = pltpu.roll(values, step % lanes, 1)
    return jnp.where(lane == (0 if step == 1 else lanes - 1), 0.0, moved)


def reinit_kernel(
    owner_ref, phi_hbm, seed_hbm, vel_hbm, out_ref, low_ref, high_ref,
    phi_ref, seed_ref, hold, vel_low, vel_high, count_ref, place_ref, load_sem, vel_sem, sem,
):
    slots, rows, lanes = phi_ref.shape

    def load(step, which):
        part = pl.ds(step * REINIT_UNROLL, REINIT_UNROLL)
        src, dst = ((phi_hbm, phi_ref), (seed_hbm, seed_ref))[which]
        return pltpu.make_async_copy(src.at[part], dst.at[part], load_sem.at[which, step])

    for step in range(slots // REINIT_UNROLL):
        load(step, 0).start()
        load(step, 1).start()
    cells = vel_hbm.shape[0]
    vel_copies = [
        pltpu.make_async_copy(vel_hbm.at[:, pl.ds(0, 8)], vel_low, vel_sem.at[0]),
        pltpu.make_async_copy(vel_hbm.at[:, pl.ds(rows - 8, 8)], vel_high, vel_sem.at[1]),
    ]
    for copy in vel_copies:
        copy.start()
    for slot, (home, rank) in enumerate(homes_and_ranks(owner_ref, count_ref)):
        place_ref[slot] = home * CAP + rank
    row = lax.broadcasted_iota(I32, (rows, lanes), 0)
    lane = lax.broadcasted_iota(I32, (rows, lanes), 1)
    low_ref[...] = jnp.zeros_like(low_ref)
    high_ref[...] = jnp.zeros_like(high_ref)

    def out_copy(slot):
        place = place_ref[slot]
        return pltpu.make_async_copy(
            hold.at[slot],
            out_ref.at[place // CAP, pl.ds(pl.multiple_of((place % CAP) * rows, rows), rows)],
            sem.at[slot],
        )

    def block(slot):
        phi = phi_ref[slot]
        up_y = jnp.where(row == rows - 1, phi, pltpu.roll(phi, rows - 1, 0))
        low_y = jnp.where(row == 0, phi, pltpu.roll(phi, 1, 0))
        up_z = jnp.where(lane == lanes - 1, phi, pltpu.roll(phi, lanes - 1, 1))
        low_z = jnp.where(lane == 0, phi, pltpu.roll(phi, 1, 1))
        grad_y = 0.5 * (up_y - low_y)
        grad_z = 0.5 * (up_z - low_z)
        normal = jnp.sqrt(grad_y * grad_y + grad_z * grad_z + 1.0)
        sign = phi / jnp.sqrt(phi * phi + 1.0)
        scale = (0.5 * REINIT_STEP) * sign / normal
        weight_y = scale * grad_y
        weight_z = scale * grad_z
        adjoint = seed_ref[slot]
        for _ in range(REINIT):
            flux_y = weight_y * adjoint
            flux_z = weight_z * adjoint
            adjoint = adjoint + (
                (shift_rows(flux_y, -1, row) - shift_rows(flux_y, 1, row))
                + (shift_lanes(flux_z, -1, lane) - shift_lanes(flux_z, 1, lane))
            )
        heaviside = jnp.tanh(phi / SMEAR_WIDTH)
        hold[slot] = adjoint * (0.5 / SMEAR_WIDTH * (1.0 - heaviside * heaviside))

    def body(step, carry):
        load(step, 0).wait()
        load(step, 1).wait()
        for j in range(REINIT_UNROLL):
            block(step * REINIT_UNROLL + j)
        for j in range(REINIT_UNROLL):
            slot = step * REINIT_UNROLL + j
            out_copy(slot).start()
            place = place_ref[slot]
            first = (place // CAP) * EXTRA + place % CAP
            high_ref[pl.ds(first, 1), :] = hold[slot, rows - 1 : rows, :]
            low_ref[pl.ds(first + CAP, 1), :] = hold[slot, 0:1, :]
        return carry

    lax.fori_loop(0, slots // REINIT_UNROLL, body, 0)
    for copy in vel_copies:
        copy.wait()
    behind = low_ref.shape[0] - cells

    def vel_lines(x):
        low_ref[pl.ds(behind + x, 1), :] = vel_low[x, 0:1, :]
        high_ref[pl.ds(behind + x, 1), :] = vel_high[x, 7:8, :]

    by_rows(0, cells, vel_lines)
    for slot in range(slots):
        out_copy(slot).wait()


def pack_lines_kernel(below_ref, above_ref, forcing_ref, out_ref, hold, sem):
    for home in range(hold.shape[0]):
        part = pl.ds(home * EXTRA, EXTRA)
        hold[home] = below_ref[part, :] + above_ref[part, :]
    copy = pltpu.make_async_copy(
        hold, out_ref.at[:, pl.ds(out_ref.shape[1] - EXTRA, EXTRA)], sem
    )
    copy.start()
    copy.wait()


def neighbours(buffer, x, first, rows, lane):
    here = buffer[x + 1, pl.ds(PAD + first, rows), :]
    low_x = buffer[x, pl.ds(PAD + first, rows), :]
    up_x = buffer[x + 2, pl.ds(PAD + first, rows), :]
    low_y = buffer[x + 1, pl.ds(PAD + first - 1, rows), :]
    up_y = buffer[x + 1, pl.ds(PAD + first + 1, rows), :]
    low_z = shift_lanes(here, 1, lane)
    up_z = shift_lanes(here, -1, lane)
    return here, low_x, up_x, low_y, up_y, low_z, up_z


def operator(fields, flags, rate):
    here, low_x, up_x, low_y, up_y, low_z, up_z = fields
    upwind = (
        jnp.where((flags & 1) != 0, low_x, up_x)
        + jnp.where((flags & 2) != 0, low_y, up_y)
        + jnp.where((flags & 4) != 0, low_z, up_z)
    )
    total = (low_x + up_x) + (low_y + up_y) + (low_z + up_z)
    return (1.0 - 6.0 * DIFFUSION) * here + rate * (upwind - 3.0 * here) + DIFFUSION * total


def chunk_copy(src, dst, sem, c):
    part = pl.ds(c * CHUNK, CHUNK)
    return pltpu.make_async_copy(src.at[part], dst.at[part], sem.at[c])


def first_kernel(
    vel_ref, flags_ref, phi_ref, level_ref, xlow_ref, xhigh_ref, ylow_ref, yhigh_ref,
    code_out, twice_out, edge_x_ref, edge_ylow_ref, edge_yhigh_ref, coef_ref, table_ref,
    vel, once, flags, rate, code, twice, tags, sem_tags, sem_vel, sem_flags, sem_phi, sem_code, sem_twice,
):
    cells, rows, lanes = flags.shape
    chunks = cells // CHUNK

    def vel_copy(c):
        return pltpu.make_async_copy(
            vel_ref.at[pl.ds(c * CHUNK, CHUNK)],
            vel.at[pl.ds(1 + c * CHUNK, CHUNK), pl.ds(PAD, rows)],
            sem_vel.at[c],
        )

    def flags_copy(c):
        return chunk_copy(flags_ref, flags, sem_flags, c)

    def code_copy(c):
        return chunk_copy(code, code_out, sem_code, c)

    def twice_copy(c):
        return chunk_copy(twice, twice_out, sem_twice, c)

    tag_copy = pltpu.make_async_copy(level_ref.at[:, pl.ds(CAP * rows, EXTRA)], tags, sem_tags)
    tag_copy.start()

    def start_loads(c, carry):
        vel_copy(c).start()
        flags_copy(c).start()
        return carry

    lax.fori_loop(0, chunks, start_loads, 0)
    for x in range(cells):
        table_ref[x] = -1
    tag_copy.wait()
    for source in range(tags.shape[0]):
        for rank in range(CAP):
            tag = tags[source, rank, 0].astype(I32)

            @pl.when(tag > 0)
            def _():
                table_ref[tag - 1] = source * CAP + rank

    def start(c, carry):
        for j in range(CHUNK):
            x = c * CHUNK + j
            slot = table_ref[x]

            @pl.when(slot >= 0)
            def _():
                pltpu.make_async_copy(
                    block_of(level_ref, slot, rows), rate.at[x], sem_phi.at[c]
                ).start()

            @pl.when(slot < 0)
            def _():
                pltpu.make_async_copy(phi_ref.at[x], rate.at[x], sem_phi.at[c]).start()

        return carry

    lax.fori_loop(0, chunks, start, 0)

    lane = lax.broadcasted_iota(I32, (STRIP, lanes), 1)
    zeros = jnp.zeros((rows + 2 * PAD, lanes), F32)
    vel[0, pl.ds(PAD, rows), :] = xlow_ref[0]
    vel[cells + 1, pl.ds(PAD, rows), :] = xhigh_ref[0]
    once[0] = zeros
    once[cells + 1] = zeros
    line_zero = jnp.zeros((PAD, lanes), F32)

    behind = ylow_ref.shape[0] - cells

    def lines(x):
        vel[x + 1, PAD - 1 : PAD, :] = ylow_ref[pl.ds(behind + x, 1), :]
        vel[x + 1, PAD + rows : PAD + rows + 1, :] = yhigh_ref[pl.ds(behind + x, 1), :]
        once[x + 1, 0:PAD, :] = line_zero
        once[x + 1, PAD + rows : PAD + rows + PAD, :] = line_zero
        slot = jnp.full((1, lanes), table_ref[x].astype(F32), F32)
        edge_ylow_ref[pl.ds(cells + x, 1), :] = slot
        edge_yhigh_ref[pl.ds(cells + x, 1), :] = slot

    by_rows(0, cells, lines)

    def update_once(x):
        for first in range(0, rows, STRIP):
            part = pl.ds(first, STRIP)
            heaviside = jnp.tanh(rate[x, part, :] * (1.0 / SMEAR_WIDTH))
            density = (AIR_DENSITY + 0.5 * (1.0 - AIR_DENSITY)) + (0.5 * (1.0 - AIR_DENSITY)) * heaviside
            rate_here = ADV_RATE / density
            bits = flags[x, part, :]
            rate[x, part, :] = rate_here
            code[x, part, :] = bits.astype(F32) + rate_here
            once[x + 1, pl.ds(PAD + first, STRIP), :] = operator(
                neighbours(vel, x, first, STRIP, lane), bits, rate_here
            )

    def update_twice(x):
        for first in range(0, rows, STRIP):
            part = pl.ds(first, STRIP)
            twice[x, part, :] = operator(
                neighbours(once, x, first, STRIP, lane), flags[x, part, :], rate[x, part, :]
            )

    def second_pass(c):
        for j in range(CHUNK):
            update_twice(c * CHUNK + j)
        twice_copy(c).start()

    vel_copy(0).wait()

    def first_pass(c, carry):
        @pl.when(c + 1 < chunks)
        def _():
            vel_copy(c + 1).wait()

        flags_copy(c).wait()
        chunk_copy(phi_ref, rate, sem_phi, c).wait()
        for j in range(CHUNK):
            update_once(c * CHUNK + j)
        code_copy(c).start()

        @pl.when(c > 0)
        def _():
            second_pass(c - 1)

        return carry

    lax.fori_loop(0, chunks, first_pass, 0)
    second_pass(chunks - 1)
    edge_x_ref[0] = once[1, pl.ds(PAD, rows), :]
    edge_x_ref[1] = once[cells, pl.ds(PAD, rows), :]
    coef_ref[0] = DIFFUSION + jnp.where((flags[0] & 1) != 0, rate[0], 0.0)
    coef_ref[1] = DIFFUSION + jnp.where((flags[cells - 1] & 1) != 0, 0.0, rate[cells - 1])

    def edge_lines(x):
        edge_ylow_ref[pl.ds(x, 1), :] = once[x + 1, PAD : PAD + 1, :]
        edge_yhigh_ref[pl.ds(x, 1), :] = once[x + 1, PAD + rows - 1 : PAD + rows, :]

    by_rows(0, cells, edge_lines)

    for c in range(chunks):
        code_copy(c).wait()
        twice_copy(c).wait()


def block_of(ref, slot, rows):
    return ref.at[slot // CAP, pl.ds(pl.multiple_of((slot % CAP) * rows, rows), rows)]


def edge_kernel(odd_ref, table_ref, edge_ref, forcing_ref, first_out, second_out):
    rows = first_out.shape[1]
    odd = odd_ref[0]
    for side, x in enumerate((0, table_ref.shape[0] - 1)):
        slot = table_ref[x]
        safe = jnp.maximum(slot, 0)
        slab = edge_ref[side] + jnp.where(
            slot >= 0, block_of(forcing_ref, safe, rows)[...], 0.0
        )

        @pl.when(odd != side)
        def _():
            first_out[0] = slab

        @pl.when(odd == side)
        def _():
            second_out[0] = slab


def last_kernel(
    table_ref, below_ref, above_ref, forcing_ref, code_ref, twice_ref, ylow_ref, yhigh_ref,
    out_ref, part_ref, source, code, twice, sem_code, sem_twice, sem_out,
):
    cells, rows, lanes = code.shape
    chunks = cells // CHUNK
    loads = ((code_ref, code, sem_code), (twice_ref, twice, sem_twice))

    def start(c, carry):
        for load in loads:
            chunk_copy(*load, c).start()
        return carry

    lax.fori_loop(0, chunks, start, 0)
    zeros = jnp.zeros((rows, lanes), F32)
    source[0, pl.ds(PAD, rows), :] = zeros
    source[cells + 1, pl.ds(PAD, rows), :] = zeros

    def fill(x):
        slot = table_ref[x]
        safe = jnp.maximum(slot, 0)
        source[x + 1, pl.ds(PAD, rows), :] = jnp.where(
            slot >= 0, block_of(forcing_ref, safe, rows)[...], 0.0
        )
        for side, slots, halo, at in (
            (0, below_ref, ylow_ref, PAD - 1),
            (1, above_ref, yhigh_ref, PAD + rows),
        ):
            line_slot = slots[x]
            safe = jnp.maximum(line_slot, 0)
            line = forcing_ref[safe // CAP, pl.ds(CAP * rows + side * CAP + safe % CAP, 1), :]
            source[x + 1, at : at + 1, :] = halo[pl.ds(x, 1), :] + jnp.where(
                line_slot >= 0, line, 0.0
            )

    lane = lax.broadcasted_iota(I32, (STRIP, lanes), 1)

    def update(x):
        for first in range(0, rows, STRIP):
            part = pl.ds(first, STRIP)
            fields = neighbours(source, x, first, STRIP, lane)
            both = code[x, part, :]
            bits = both.astype(I32)
            twice[x, part, :] = (
                twice[x, part, :] + fields[0] + operator(fields, bits, both - bits.astype(F32))
            )

    by_rows(0, cells, fill)

    def work(c, carry):
        for load in loads:
            chunk_copy(*load, c).wait()
        for j in range(CHUNK):
            update(c * CHUNK + j)
        chunk_copy(twice, out_ref, sem_out, c).start()
        return carry

    lax.fori_loop(0, chunks, work, 0)
    part_ref[0] = twice[0]
    part_ref[1] = twice[cells - 1]
    for c in range(chunks):
        chunk_copy(twice, out_ref, sem_out, c).wait()


def close_kernel(odd_ref, part_ref, coef_ref, first_ref, second_ref, whole_ref, out_ref, hold, sem):
    cells = out_ref.shape[0]
    odd = odd_ref[0] == 1
    hold[0] = part_ref[0] + coef_ref[0] * jnp.where(odd, first_ref[0], second_ref[0])
    hold[1] = part_ref[1] + coef_ref[1] * jnp.where(odd, second_ref[0], first_ref[0])
    copies = [
        pltpu.make_async_copy(hold.at[0], out_ref.at[0], sem.at[0]),
        pltpu.make_async_copy(hold.at[1], out_ref.at[cells - 1], sem.at[1]),
    ]
    for copy in copies:
        copy.start()
    for copy in copies:
        copy.wait()


def neighbour_pairs(axis):
    count = lax.axis_size(axis)
    forward = [(i, i + 1) for i in range(count - 1)]
    return forward, [(target, source) for source, target in forward]


def swaps(axis, first):
    low = range(first, lax.axis_size(axis) - 1, 2)
    return [(i, i + 1) for i in low] + [(i + 1, i) for i in low]


def local(band_phi, band_seed, owner_map, active_list, brick_phi, adjoint_vel, upwind_flags):
    gx_count = lax.axis_size("gx")
    slots, rows, lanes = band_phi.shape
    cells = brick_phi.shape[0]
    chunks = cells // CHUNK
    up_x, down_x = neighbour_pairs("gx")
    up_y, down_y = neighbour_pairs("gy")
    shape = jax.ShapeDtypeStruct
    dma = pltpu.SemaphoreType.DMA
    brick = (cells, rows, lanes)
    padded = (cells + 2, rows + 2 * PAD, lanes)
    sent = (gx_count, CAP * rows + EXTRA, lanes)
    owners, slabs = owner_map.T, active_list.T

    level_sent = pl.pallas_call(
        pack_level_kernel,
        out_shape=shape(sent, F32),
        in_specs=[HBM, HBM, HBM],
        out_specs=HBM,
        scratch_shapes=[
            pltpu.SMEM((1, slots), I32),
            pltpu.SMEM((1, slots), I32),
            pltpu.VMEM((slots, rows, lanes), F32),
            pltpu.VMEM((gx_count, EXTRA, lanes), F32),
            pltpu.SMEM((gx_count,), I32),
            dma((slots + 2,)), dma((slots,)), dma(()),
        ],
        compiler_params=params(BIG),
        cost_estimate=cost(2, 1000),
        name="pack_level",
    )(owners, slabs, band_phi)
    level = lax.all_to_all(level_sent, "gx", split_axis=0, concat_axis=0, tiled=True)

    lines = (gx_count * EXTRA + cells, lanes)
    v_xlow = lax.ppermute(adjoint_vel[cells - 1 :], "gx", up_x)
    v_xhigh = lax.ppermute(adjoint_vel[:1], "gx", down_x)
    forcing_sent, low_lines, high_lines = pl.pallas_call(
        reinit_kernel,
        out_shape=(shape(sent, F32), shape(lines, F32), shape(lines, F32)),
        in_specs=[SMEM, HBM, HBM, HBM],
        out_specs=(HBM, VMEM, VMEM),
        scratch_shapes=[
            pltpu.VMEM((slots, rows, lanes), F32),
            pltpu.VMEM((slots, rows, lanes), F32),
            pltpu.VMEM((slots, rows, lanes), F32),
            pltpu.VMEM((cells, 8, lanes), F32),
            pltpu.VMEM((cells, 8, lanes), F32),
            pltpu.SMEM((gx_count,), I32),
            pltpu.SMEM((slots,), I32),
            dma((2, slots // REINIT_UNROLL)), dma((2,)), dma((slots,)),
        ],
        compiler_params=params(BIG),
        cost_estimate=cost(20, 40_000_000),
        name="reinit",
    )(owners, band_phi, band_seed, adjoint_vel)
    below_lines = lax.ppermute(high_lines, "gy", up_y)
    above_lines = lax.ppermute(low_lines, "gy", down_y)
    v_xlow, v_xhigh, below_lines, above_lines = lax.optimization_barrier(
        (v_xlow, v_xhigh, below_lines, above_lines)
    )
    forcing_sent = pl.pallas_call(
        pack_lines_kernel,
        out_shape=shape(sent, F32),
        in_specs=[VMEM, VMEM, HBM],
        out_specs=HBM,
        scratch_shapes=[pltpu.VMEM((gx_count, EXTRA, lanes), F32), dma(())],
        input_output_aliases={2: 0},
        compiler_params=params(MEDIUM),
        cost_estimate=cost(2, 1000),
        name="pack_lines",
    )(below_lines, above_lines, forcing_sent)
    forcing = lax.all_to_all(forcing_sent, "gx", split_axis=0, concat_axis=0, tiled=True)

    edge_lines = (2 * cells, lanes)
    code, twice, edge_x, edge_ylow, edge_yhigh, coef, table = pl.pallas_call(
        first_kernel,
        out_shape=(
            shape(brick, F32),
            shape(brick, F32),
            shape((2, rows, lanes), F32),
            shape(edge_lines, F32),
            shape(edge_lines, F32),
            shape((2, rows, lanes), F32),
            shape((cells,), I32),
        ),
        in_specs=[HBM, HBM, HBM, HBM, VMEM, VMEM, VMEM, VMEM],
        out_specs=(HBM, HBM, VMEM, VMEM, VMEM, VMEM, SMEM),
        scratch_shapes=[
            pltpu.VMEM(padded, F32),
            pltpu.VMEM(padded, F32),
            pltpu.VMEM(brick, I32),
            pltpu.VMEM(brick, F32),
            pltpu.VMEM(brick, F32),
            pltpu.VMEM(brick, F32),
            pltpu.SMEM((gx_count, EXTRA, lanes), F32),
            dma(()),
            dma((chunks,)), dma((chunks,)), dma((chunks,)), dma((chunks,)), dma((chunks,)),
        ],
        compiler_params=params(ROOMY),
        cost_estimate=cost(30, 60_000_000),
        name="two_updates",
    )(adjoint_vel, upwind_flags, brick_phi, level, v_xlow, v_xhigh, below_lines, above_lines)
    once_ylow = lax.ppermute(edge_yhigh, "gy", up_y)
    once_yhigh = lax.ppermute(edge_ylow, "gy", down_y)
    gy = lax.axis_index("gy")
    below = jnp.where(gy > 0, once_ylow[cells:, 0].astype(I32), -1)
    above = jnp.where(gy < lax.axis_size("gy") - 1, once_yhigh[cells:, 0].astype(I32), -1)

    edge_x, below, above = lax.optimization_barrier((edge_x, below, above))

    odd = (lax.axis_index("gx") % 2).astype(I32).reshape(1)
    first_slab, second_slab = pl.pallas_call(
        edge_kernel,
        out_shape=(shape((1, rows, lanes), F32), shape((1, rows, lanes), F32)),
        in_specs=[SMEM, SMEM, VMEM, VMEM],
        out_specs=(VMEM, VMEM),
        compiler_params=params(SMALL),
        cost_estimate=cost(1, 1000),
        name="edge_slabs",
    )(odd, table, edge_x, forcing)
    first_got = lax.ppermute(first_slab, "gx", swaps("gx", 0))
    second_got = lax.ppermute(second_slab, "gx", swaps("gx", 1))

    out, part = pl.pallas_call(
        last_kernel,
        out_shape=(shape(brick, F32), shape((2, rows, lanes), F32)),
        in_specs=[SMEM, SMEM, SMEM, VMEM, HBM, HBM, VMEM, VMEM],
        out_specs=(HBM, VMEM),
        scratch_shapes=[
            pltpu.VMEM(padded, F32),
            pltpu.VMEM(brick, F32),
            pltpu.VMEM(brick, F32),
            dma((chunks,)), dma((chunks,)), dma((chunks,)),
        ],
        compiler_params=params(ROOMY),
        cost_estimate=cost(30, 60_000_000),
        name="add_forcing",
    )(table, below, above, forcing, code, twice, once_ylow, once_yhigh)

    return pl.pallas_call(
        close_kernel,
        out_shape=shape(brick, F32),
        in_specs=[SMEM, VMEM, VMEM, VMEM, VMEM, HBM],
        out_specs=HBM,
        scratch_shapes=[pltpu.VMEM((2, rows, lanes), F32), dma((2,))],
        input_output_aliases={5: 0},
        compiler_params=params(SMALL),
        cost_estimate=cost(1, 1000),
        name="close_slabs",
    )(odd, part, coef, first_got, second_got, out)


def solution(mesh):
    in_specs = (
        P("gx", "gy", None),
        P("gx", "gy", None),
        P("gx", "gy"),
        P("gx", "gy"),
        P("gx", "gy", None),
        P("gx", "gy", None),
        P("gx", "gy", None),
    )
    out_specs = P("gx", "gy", None)
    return jax.shard_map(local, mesh=mesh, in_specs=in_specs, out_specs=out_specs, check_vma=False)
```

```python
import jax
import jax.numpy as jnp
from jax import lax
from jax.experimental import pallas as pl
from jax.experimental.pallas import tpu as pltpu
from jax.sharding import PartitionSpec as P

CAP = 2
REINIT = 4
REINIT_STEP = 0.4
ADV_RATE = 0.25
DIFFUSION = 0.1
AIR_DENSITY = 0.3
SMEAR_WIDTH = 1.5

F32 = jnp.float32
I32 = jnp.int32
MIB = 1 << 20
HBM = pl.BlockSpec(memory_space=pltpu.HBM)
VMEM = pl.BlockSpec(memory_space=pltpu.VMEM)
SMEM = pl.BlockSpec(memory_space=pltpu.SMEM)
EXTRA = 8
PAD = 8
CHUNK = 8
STRIP = 32
UNROLL = 4
REINIT_UNROLL = 2


BIG = 62
MEDIUM = 52
ROOMY = 50
SMALL = 4


def params(mib):
    return pltpu.CompilerParams(vmem_limit_bytes=mib * MIB)


def cost(mib, flops):
    return pl.CostEstimate(flops=flops, bytes_accessed=mib * MIB, transcendentals=0)


def by_rows(first, last, body, count=UNROLL):
    def step(i, carry):
        for j in range(count):
            body(first + i * count + j)
        return carry

    lax.fori_loop(0, (last - first) // count, step, 0)


def homes_and_ranks(owner_ref, count_ref):
    for home in range(count_ref.shape[0]):
        count_ref[home] = 0
    result = []
    for slot in range(owner_ref.shape[1]):
        home = owner_ref[0, slot]
        rank = count_ref[home]
        count_ref[home] = rank + 1
        result.append((home, rank))
    return result


def pack_level_kernel(
    owner_hbm, slab_hbm, phi_ref, out_ref, owner_ref, slab_ref, phi, tags, count_ref, load_sem, sem, tag_sem
):
    slots, rows, lanes = phi_ref.shape
    loads = [
        pltpu.make_async_copy(phi_ref.at[slot], phi.at[slot], load_sem.at[slot])
        for slot in range(slots)
    ]
    scalars = [
        pltpu.make_async_copy(owner_hbm, owner_ref, load_sem.at[slots]),
        pltpu.make_async_copy(slab_hbm, slab_ref, load_sem.at[slots + 1]),
    ]
    for load in scalars + loads:
        load.start()
    tags[...] = jnp.zeros_like(tags)
    for load in scalars:
        load.wait()
    places = homes_and_ranks(owner_ref, count_ref)
    for slot, (home, rank) in enumerate(places):
        label = (slab_ref[0, slot] + 1).astype(F32)
        tags[home, pl.ds(rank, 1), :] = jnp.full((1, lanes), label, F32)
    copies = [pltpu.make_async_copy(tags, out_ref.at[:, pl.ds(CAP * rows, EXTRA)], tag_sem)]
    copies[0].start()
    for slot, (home, rank) in enumerate(places):
        loads[slot].wait()
        copy = pltpu.make_async_copy(
            phi.at[slot],
            out_ref.at[home, pl.ds(pl.multiple_of(rank * rows, rows), rows)],
            sem.at[slot],
        )
        copy.start()
        copies.append(copy)
    for copy in copies:
        copy.wait()


def shift_rows(values, step, row):
    rows = values.shape[0]
    moved = pltpu.roll(values, step % rows, 0)
    return jnp.where(row == (0 if step == 1 else rows - 1), 0.0, moved)


def shift_lanes(values, step, lane):
    lanes = values.shape[1]
    moved = pltpu.roll(values, step % lanes, 1)
    return jnp.where(lane == (0 if step == 1 else lanes - 1), 0.0, moved)


def reinit_kernel(
    owner_ref, phi_hbm, seed_hbm, vel_hbm, out_ref, low_ref, high_ref,
    phi_ref, seed_ref, hold, vel_low, vel_high, count_ref, place_ref, load_sem, vel_sem, sem,
):
    slots, rows, lanes = phi_ref.shape

    def load(step, which):
        part = pl.ds(step * REINIT_UNROLL, REINIT_UNROLL)
        src, dst = ((phi_hbm, phi_ref), (seed_hbm, seed_ref))[which]
        return pltpu.make_async_copy(src.at[part], dst.at[part], load_sem.at[which, step])

    for step in range(slots // REINIT_UNROLL):
        load(step, 0).start()
        load(step, 1).start()
    cells = vel_hbm.shape[0]
    vel_copies = [
        pltpu.make_async_copy(vel_hbm.at[:, pl.ds(0, 8)], vel_low, vel_sem.at[0]),
        pltpu.make_async_copy(vel_hbm.at[:, pl.ds(rows - 8, 8)], vel_high, vel_sem.at[1]),
    ]
    for copy in vel_copies:
        copy.start()
    for slot, (home, rank) in enumerate(homes_and_ranks(owner_ref, count_ref)):
        place_ref[slot] = home * CAP + rank
    row = lax.broadcasted_iota(I32, (rows, lanes), 0)
    lane = lax.broadcasted_iota(I32, (rows, lanes), 1)
    low_ref[...] = jnp.zeros_like(low_ref)
    high_ref[...] = jnp.zeros_like(high_ref)

    def out_copy(slot):
        place = place_ref[slot]
        return pltpu.make_async_copy(
            hold.at[slot],
            out_ref.at[place // CAP, pl.ds(pl.multiple_of((place % CAP) * rows, rows), rows)],
            sem.at[slot],
        )

    def block(slot):
        phi = phi_ref[slot]
        up_y = jnp.where(row == rows - 1, phi, pltpu.roll(phi, rows - 1, 0))
        low_y = jnp.where(row == 0, phi, pltpu.roll(phi, 1, 0))
        up_z = jnp.where(lane == lanes - 1, phi, pltpu.roll(phi, lanes - 1, 1))
        low_z = jnp.where(lane == 0, phi, pltpu.roll(phi, 1, 1))
        grad_y = 0.5 * (up_y - low_y)
        grad_z = 0.5 * (up_z - low_z)
        normal = jnp.sqrt(grad_y * grad_y + grad_z * grad_z + 1.0)
        sign = phi / jnp.sqrt(phi * phi + 1.0)
        scale = (0.5 * REINIT_STEP) * sign / normal
        weight_y = scale * grad_y
        weight_z = scale * grad_z
        adjoint = seed_ref[slot]
        for _ in range(REINIT):
            flux_y = weight_y * adjoint
            flux_z = weight_z * adjoint
            adjoint = adjoint + (
                (shift_rows(flux_y, -1, row) - shift_rows(flux_y, 1, row))
                + (shift_lanes(flux_z, -1, lane) - shift_lanes(flux_z, 1, lane))
            )
        heaviside = jnp.tanh(phi / SMEAR_WIDTH)
        hold[slot] = adjoint * (0.5 / SMEAR_WIDTH * (1.0 - heaviside * heaviside))

    def body(step, carry):
        load(step, 0).wait()
        load(step, 1).wait()
        for j in range(REINIT_UNROLL):
            block(step * REINIT_UNROLL + j)
        for j in range(REINIT_UNROLL):
            slot = step * REINIT_UNROLL + j
            out_copy(slot).start()
            place = place_ref[slot]
            first = (place // CAP) * EXTRA + place % CAP
            high_ref[pl.ds(first, 1), :] = hold[slot, rows - 1 : rows, :]
            low_ref[pl.ds(first + CAP, 1), :] = hold[slot, 0:1, :]
        return carry

    lax.fori_loop(0, slots // REINIT_UNROLL, body, 0)
    for copy in vel_copies:
        copy.wait()
    behind = low_ref.shape[0] - cells

    def vel_lines(x):
        low_ref[pl.ds(behind + x, 1), :] = vel_low[x, 0:1, :]
        high_ref[pl.ds(behind + x, 1), :] = vel_high[x, 7:8, :]

    by_rows(0, cells, vel_lines)
    for slot in range(slots):
        out_copy(slot).wait()


def pack_lines_kernel(below_ref, above_ref, forcing_ref, out_ref, hold, sem):
    for home in range(hold.shape[0]):
        part = pl.ds(home * EXTRA, EXTRA)
        hold[home] = below_ref[part, :] + above_ref[part, :]
    copy = pltpu.make_async_copy(
        hold, out_ref.at[:, pl.ds(out_ref.shape[1] - EXTRA, EXTRA)], sem
    )
    copy.start()
    copy.wait()


def neighbours(buffer, x, first, rows, lane):
    here = buffer[x + 1, pl.ds(PAD + first, rows), :]
    low_x = buffer[x, pl.ds(PAD + first, rows), :]
    up_x = buffer[x + 2, pl.ds(PAD + first, rows), :]
    low_y = buffer[x + 1, pl.ds(PAD + first - 1, rows), :]
    up_y = buffer[x + 1, pl.ds(PAD + first + 1, rows), :]
    low_z = shift_lanes(here, 1, lane)
    up_z = shift_lanes(here, -1, lane)
    return here, low_x, up_x, low_y, up_y, low_z, up_z


def operator(fields, flags, rate, keep=1.0):
    here, low_x, up_x, low_y, up_y, low_z, up_z = fields
    upwind = (
        jnp.where((flags & 1) != 0, low_x, up_x)
        + jnp.where((flags & 2) != 0, low_y, up_y)
        + jnp.where((flags & 4) != 0, low_z, up_z)
    )
    total = (low_x + up_x) + (low_y + up_y) + (low_z + up_z)
    return (keep - 6.0 * DIFFUSION) * here + rate * (upwind - 3.0 * here) + DIFFUSION * total


def chunk_copy(src, dst, sem, c):
    part = pl.ds(c * CHUNK, CHUNK)
    return pltpu.make_async_copy(src.at[part], dst.at[part], sem.at[c])


def first_kernel(
    vel_ref, flags_ref, phi_ref, level_ref, xlow_ref, xhigh_ref, ylow_ref, yhigh_ref,
    code_out, twice_out, edge_x_ref, edge_ylow_ref, edge_yhigh_ref, coef_ref, table_ref,
    vel, once, flags, rate, code, twice, tags, sem_tags, sem_vel, sem_flags, sem_phi, sem_code, sem_twice,
):
    cells, rows, lanes = flags.shape
    chunks = cells // CHUNK

    def vel_copy(c):
        return pltpu.make_async_copy(
            vel_ref.at[pl.ds(c * CHUNK, CHUNK)],
            vel.at[pl.ds(1 + c * CHUNK, CHUNK), pl.ds(PAD, rows)],
            sem_vel.at[c],
        )

    def flags_copy(c):
        return chunk_copy(flags_ref, flags, sem_flags, c)

    def code_copy(c):
        return chunk_copy(code, code_out, sem_code, c)

    def twice_copy(c):
        return chunk_copy(twice, twice_out, sem_twice, c)

    tag_copy = pltpu.make_async_copy(level_ref.at[:, pl.ds(CAP * rows, EXTRA)], tags, sem_tags)
    tag_copy.start()

    def start_loads(c, carry):
        vel_copy(c).start()
        flags_copy(c).start()
        return carry

    lax.fori_loop(0, chunks, start_loads, 0)
    for x in range(cells):
        table_ref[x] = -1
    tag_copy.wait()
    for source in range(tags.shape[0]):
        for rank in range(CAP):
            tag = tags[source, rank, 0].astype(I32)

            @pl.when(tag > 0)
            def _():
                table_ref[tag - 1] = source * CAP + rank

    def start(c, carry):
        for j in range(CHUNK):
            x = c * CHUNK + j
            slot = table_ref[x]

            @pl.when(slot >= 0)
            def _():
                pltpu.make_async_copy(
                    block_of(level_ref, slot, rows), rate.at[x], sem_phi.at[c]
                ).start()

            @pl.when(slot < 0)
            def _():
                pltpu.make_async_copy(phi_ref.at[x], rate.at[x], sem_phi.at[c]).start()

        return carry

    lax.fori_loop(0, chunks, start, 0)

    lane = lax.broadcasted_iota(I32, (STRIP, lanes), 1)
    zeros = jnp.zeros((rows + 2 * PAD, lanes), F32)
    vel[0, pl.ds(PAD, rows), :] = xlow_ref[0]
    vel[cells + 1, pl.ds(PAD, rows), :] = xhigh_ref[0]
    once[0] = zeros
    once[cells + 1] = zeros
    line_zero = jnp.zeros((PAD, lanes), F32)

    behind = ylow_ref.shape[0] - cells

    def lines(x):
        vel[x + 1, PAD - 1 : PAD, :] = ylow_ref[pl.ds(behind + x, 1), :]
        vel[x + 1, PAD + rows : PAD + rows + 1, :] = yhigh_ref[pl.ds(behind + x, 1), :]
        once[x + 1, 0:PAD, :] = line_zero
        once[x + 1, PAD + rows : PAD + rows + PAD, :] = line_zero
        slot = jnp.full((1, lanes), table_ref[x].astype(F32), F32)
        edge_ylow_ref[pl.ds(cells + x, 1), :] = slot
        edge_yhigh_ref[pl.ds(cells + x, 1), :] = slot

    by_rows(0, cells, lines)

    def update_once(x):
        for first in range(0, rows, STRIP):
            part = pl.ds(first, STRIP)
            heaviside = jnp.tanh(rate[x, part, :] * (1.0 / SMEAR_WIDTH))
            density = (AIR_DENSITY + 0.5 * (1.0 - AIR_DENSITY)) + (0.5 * (1.0 - AIR_DENSITY)) * heaviside
            rate_here = ADV_RATE / density
            bits = flags[x, part, :]
            rate[x, part, :] = rate_here
            code[x, part, :] = bits.astype(F32) + rate_here
            once[x + 1, pl.ds(PAD + first, STRIP), :] = operator(
                neighbours(vel, x, first, STRIP, lane), bits, rate_here
            )

    def update_twice(x):
        for first in range(0, rows, STRIP):
            part = pl.ds(first, STRIP)
            twice[x, part, :] = operator(
                neighbours(once, x, first, STRIP, lane), flags[x, part, :], rate[x, part, :]
            )

    def second_pass(c):
        for j in range(CHUNK):
            update_twice(c * CHUNK + j)
        twice_copy(c).start()

    vel_copy(0).wait()

    def first_pass(c, carry):
        @pl.when(c + 1 < chunks)
        def _():
            vel_copy(c + 1).wait()

        flags_copy(c).wait()
        chunk_copy(phi_ref, rate, sem_phi, c).wait()
        for j in range(CHUNK):
            update_once(c * CHUNK + j)
        code_copy(c).start()

        @pl.when(c > 0)
        def _():
            second_pass(c - 1)

        return carry

    lax.fori_loop(0, chunks, first_pass, 0)
    second_pass(chunks - 1)
    edge_x_ref[0] = once[1, pl.ds(PAD, rows), :]
    edge_x_ref[1] = once[cells, pl.ds(PAD, rows), :]
    coef_ref[0] = DIFFUSION + jnp.where((flags[0] & 1) != 0, rate[0], 0.0)
    coef_ref[1] = DIFFUSION + jnp.where((flags[cells - 1] & 1) != 0, 0.0, rate[cells - 1])

    def edge_lines(x):
        edge_ylow_ref[pl.ds(x, 1), :] = once[x + 1, PAD : PAD + 1, :]
        edge_yhigh_ref[pl.ds(x, 1), :] = once[x + 1, PAD + rows - 1 : PAD + rows, :]

    by_rows(0, cells, edge_lines)

    for c in range(chunks):
        code_copy(c).wait()
        twice_copy(c).wait()


def block_of(ref, slot, rows):
    return ref.at[slot // CAP, pl.ds(pl.multiple_of((slot % CAP) * rows, rows), rows)]


def edge_kernel(odd_ref, table_ref, edge_ref, forcing_ref, first_out, second_out):
    rows = first_out.shape[1]
    odd = odd_ref[0]
    for side, x in enumerate((0, table_ref.shape[0] - 1)):
        slot = table_ref[x]
        safe = jnp.maximum(slot, 0)
        slab = edge_ref[side] + jnp.where(
            slot >= 0, block_of(forcing_ref, safe, rows)[...], 0.0
        )

        @pl.when(odd != side)
        def _():
            first_out[0] = slab

        @pl.when(odd == side)
        def _():
            second_out[0] = slab


def last_kernel(
    table_ref, below_ref, above_ref, forcing_ref, code_ref, twice_ref, ylow_ref, yhigh_ref,
    out_ref, part_ref, source, code, twice, sem_code, sem_twice, sem_out,
):
    cells, rows, lanes = code.shape
    chunks = cells // CHUNK
    loads = ((code_ref, code, sem_code), (twice_ref, twice, sem_twice))

    def start(c, carry):
        for load in loads:
            chunk_copy(*load, c).start()
        return carry

    lax.fori_loop(0, chunks, start, 0)
    zeros = jnp.zeros((rows, lanes), F32)
    source[0, pl.ds(PAD, rows), :] = zeros
    source[cells + 1, pl.ds(PAD, rows), :] = zeros

    def fill(x):
        slot = table_ref[x]
        safe = jnp.maximum(slot, 0)
        source[x + 1, pl.ds(PAD, rows), :] = jnp.where(
            slot >= 0, block_of(forcing_ref, safe, rows)[...], 0.0
        )
        for side, slots, halo, at in (
            (0, below_ref, ylow_ref, PAD - 1),
            (1, above_ref, yhigh_ref, PAD + rows),
        ):
            line_slot = slots[x]
            safe = jnp.maximum(line_slot, 0)
            line = forcing_ref[safe // CAP, pl.ds(CAP * rows + side * CAP + safe % CAP, 1), :]
            source[x + 1, at : at + 1, :] = halo[pl.ds(x, 1), :] + jnp.where(
                line_slot >= 0, line, 0.0
            )

    lane = lax.broadcasted_iota(I32, (STRIP, lanes), 1)

    def update(x):
        for first in range(0, rows, STRIP):
            part = pl.ds(first, STRIP)
            fields = neighbours(source, x, first, STRIP, lane)
            both = code[x, part, :]
            bits = both.astype(I32)
            twice[x, part, :] = twice[x, part, :] + operator(
                fields, bits, both - bits.astype(F32), keep=2.0
            )

    by_rows(0, cells, fill, 8)

    def work(c, carry):
        for load in loads:
            chunk_copy(*load, c).wait()
        for j in range(CHUNK):
            update(c * CHUNK + j)
        chunk_copy(twice, out_ref, sem_out, c).start()
        return carry

    lax.fori_loop(0, chunks, work, 0)
    part_ref[0] = twice[0]
    part_ref[1] = twice[cells - 1]
    for c in range(chunks):
        chunk_copy(twice, out_ref, sem_out, c).wait()


def close_kernel(odd_ref, part_ref, coef_ref, first_ref, second_ref, whole_ref, out_ref, hold, sem):
    cells = out_ref.shape[0]
    odd = odd_ref[0] == 1
    hold[0] = part_ref[0] + coef_ref[0] * jnp.where(odd, first_ref[0], second_ref[0])
    hold[1] = part_ref[1] + coef_ref[1] * jnp.where(odd, second_ref[0], first_ref[0])
    copies = [
        pltpu.make_async_copy(hold.at[0], out_ref.at[0], sem.at[0]),
        pltpu.make_async_copy(hold.at[1], out_ref.at[cells - 1], sem.at[1]),
    ]
    for copy in copies:
        copy.start()
    for copy in copies:
        copy.wait()


def neighbour_pairs(axis):
    count = lax.axis_size(axis)
    forward = [(i, i + 1) for i in range(count - 1)]
    return forward, [(target, source) for source, target in forward]


def swaps(axis, first):
    low = range(first, lax.axis_size(axis) - 1, 2)
    return [(i, i + 1) for i in low] + [(i + 1, i) for i in low]


def local(band_phi, band_seed, owner_map, active_list, brick_phi, adjoint_vel, upwind_flags):
    gx_count = lax.axis_size("gx")
    slots, rows, lanes = band_phi.shape
    cells = brick_phi.shape[0]
    chunks = cells // CHUNK
    up_x, down_x = neighbour_pairs("gx")
    up_y, down_y = neighbour_pairs("gy")
    shape = jax.ShapeDtypeStruct
    dma = pltpu.SemaphoreType.DMA
    brick = (cells, rows, lanes)
    padded = (cells + 2, rows + 2 * PAD, lanes)
    sent = (gx_count, CAP * rows + EXTRA, lanes)
    owners, slabs = owner_map.T, active_list.T

    level_sent = pl.pallas_call(
        pack_level_kernel,
        out_shape=shape(sent, F32),
        in_specs=[HBM, HBM, HBM],
        out_specs=HBM,
        scratch_shapes=[
            pltpu.SMEM((1, slots), I32),
            pltpu.SMEM((1, slots), I32),
            pltpu.VMEM((slots, rows, lanes), F32),
            pltpu.VMEM((gx_count, EXTRA, lanes), F32),
            pltpu.SMEM((gx_count,), I32),
            dma((slots + 2,)), dma((slots,)), dma(()),
        ],
        compiler_params=params(BIG),
        cost_estimate=cost(2, 1000),
        name="pack_level",
    )(owners, slabs, band_phi)
    level = lax.all_to_all(level_sent, "gx", split_axis=0, concat_axis=0, tiled=True)

    lines = (gx_count * EXTRA + cells, lanes)
    v_xlow = lax.ppermute(adjoint_vel[cells - 1 :], "gx", up_x)
    v_xhigh = lax.ppermute(adjoint_vel[:1], "gx", down_x)
    forcing_sent, low_lines, high_lines = pl.pallas_call(
        reinit_kernel,
        out_shape=(shape(sent, F32), shape(lines, F32), shape(lines, F32)),
        in_specs=[SMEM, HBM, HBM, HBM],
        out_specs=(HBM, VMEM, VMEM),
        scratch_shapes=[
            pltpu.VMEM((slots, rows, lanes), F32),
            pltpu.VMEM((slots, rows, lanes), F32),
            pltpu.VMEM((slots, rows, lanes), F32),
            pltpu.VMEM((cells, 8, lanes), F32),
            pltpu.VMEM((cells, 8, lanes), F32),
            pltpu.SMEM((gx_count,), I32),
            pltpu.SMEM((slots,), I32),
            dma((2, slots // REINIT_UNROLL)), dma((2,)), dma((slots,)),
        ],
        compiler_params=params(BIG),
        cost_estimate=cost(20, 40_000_000),
        name="reinit",
    )(owners, band_phi, band_seed, adjoint_vel)
    below_lines = lax.ppermute(high_lines, "gy", up_y)
    above_lines = lax.ppermute(low_lines, "gy", down_y)
    v_xlow, v_xhigh, below_lines, above_lines = lax.optimization_barrier(
        (v_xlow, v_xhigh, below_lines, above_lines)
    )
    forcing_sent = pl.pallas_call(
        pack_lines_kernel,
        out_shape=shape(sent, F32),
        in_specs=[VMEM, VMEM, HBM],
        out_specs=HBM,
        scratch_shapes=[pltpu.VMEM((gx_count, EXTRA, lanes), F32), dma(())],
        input_output_aliases={2: 0},
        compiler_params=params(MEDIUM),
        cost_estimate=cost(2, 1000),
        name="pack_lines",
    )(below_lines, above_lines, forcing_sent)
    forcing = lax.all_to_all(forcing_sent, "gx", split_axis=0, concat_axis=0, tiled=True)

    edge_lines = (2 * cells, lanes)
    code, twice, edge_x, edge_ylow, edge_yhigh, coef, table = pl.pallas_call(
        first_kernel,
        out_shape=(
            shape(brick, F32),
            shape(brick, F32),
            shape((2, rows, lanes), F32),
            shape(edge_lines, F32),
            shape(edge_lines, F32),
            shape((2, rows, lanes), F32),
            shape((cells,), I32),
        ),
        in_specs=[HBM, HBM, HBM, HBM, VMEM, VMEM, VMEM, VMEM],
        out_specs=(HBM, HBM, VMEM, VMEM, VMEM, VMEM, SMEM),
        scratch_shapes=[
            pltpu.VMEM(padded, F32),
            pltpu.VMEM(padded, F32),
            pltpu.VMEM(brick, I32),
            pltpu.VMEM(brick, F32),
            pltpu.VMEM(brick, F32),
            pltpu.VMEM(brick, F32),
            pltpu.SMEM((gx_count, EXTRA, lanes), F32),
            dma(()),
            dma((chunks,)), dma((chunks,)), dma((chunks,)), dma((chunks,)), dma((chunks,)),
        ],
        compiler_params=params(ROOMY),
        cost_estimate=cost(30, 60_000_000),
        name="two_updates",
    )(adjoint_vel, upwind_flags, brick_phi, level, v_xlow, v_xhigh, below_lines, above_lines)
    once_ylow = lax.ppermute(edge_yhigh, "gy", up_y)
    once_yhigh = lax.ppermute(edge_ylow, "gy", down_y)
    gy = lax.axis_index("gy")
    below = jnp.where(gy > 0, once_ylow[cells:, 0].astype(I32), -1)
    above = jnp.where(gy < lax.axis_size("gy") - 1, once_yhigh[cells:, 0].astype(I32), -1)

    edge_x, below, above = lax.optimization_barrier((edge_x, below, above))

    odd = (lax.axis_index("gx") % 2).astype(I32).reshape(1)
    first_slab, second_slab = pl.pallas_call(
        edge_kernel,
        out_shape=(shape((1, rows, lanes), F32), shape((1, rows, lanes), F32)),
        in_specs=[SMEM, SMEM, VMEM, VMEM],
        out_specs=(VMEM, VMEM),
        compiler_params=params(SMALL),
        cost_estimate=cost(1, 1000),
        name="edge_slabs",
    )(odd, table, edge_x, forcing)
    first_got = lax.ppermute(first_slab, "gx", swaps("gx", 0))
    second_got = lax.ppermute(second_slab, "gx", swaps("gx", 1))

    out, part = pl.pallas_call(
        last_kernel,
        out_shape=(shape(brick, F32), shape((2, rows, lanes), F32)),
        in_specs=[SMEM, SMEM, SMEM, VMEM, HBM, HBM, VMEM, VMEM],
        out_specs=(HBM, VMEM),
        scratch_shapes=[
            pltpu.VMEM(padded, F32),
            pltpu.VMEM(brick, F32),
            pltpu.VMEM(brick, F32),
            dma((chunks,)), dma((chunks,)), dma((chunks,)),
        ],
        compiler_params=params(ROOMY),
        cost_estimate=cost(30, 60_000_000),
        name="add_forcing",
    )(table, below, above, forcing, code, twice, once_ylow, once_yhigh)

    return pl.pallas_call(
        close_kernel,
        out_shape=shape(brick, F32),
        in_specs=[SMEM, VMEM, VMEM, VMEM, VMEM, HBM],
        out_specs=HBM,
        scratch_shapes=[pltpu.VMEM((2, rows, lanes), F32), dma((2,))],
        input_output_aliases={5: 0},
        compiler_params=params(SMALL),
        cost_estimate=cost(1, 1000),
        name="close_slabs",
    )(odd, part, coef, first_got, second_got, out)


def solution(mesh):
    in_specs = (
        P("gx", "gy", None),
        P("gx", "gy", None),
        P("gx", "gy"),
        P("gx", "gy"),
        P("gx", "gy", None),
        P("gx", "gy", None),
        P("gx", "gy", None),
    )
    out_specs = P("gx", "gy", None)
    return jax.shard_map(local, mesh=mesh, in_specs=in_specs, out_specs=out_specs, check_vma=False)
```

```python
import jax
import jax.numpy as jnp
from jax import lax
from jax.experimental import pallas as pl
from jax.experimental.pallas import tpu as pltpu
from jax.sharding import PartitionSpec as P

CAP = 2
REINIT = 4
REINIT_STEP = 0.4
ADV_RATE = 0.25
DIFFUSION = 0.1
AIR_DENSITY = 0.3
SMEAR_WIDTH = 1.5

F32 = jnp.float32
I32 = jnp.int32
MIB = 1 << 20
HBM = pl.BlockSpec(memory_space=pltpu.HBM)
VMEM = pl.BlockSpec(memory_space=pltpu.VMEM)
SMEM = pl.BlockSpec(memory_space=pltpu.SMEM)
EXTRA = 8
PAD = 8
CHUNK = 8
STRIP = 32
UNROLL = 4
REINIT_UNROLL = 2


BIG = 62
MEDIUM = 52
ROOMY = 50
SMALL = 4


def params(mib):
    return pltpu.CompilerParams(vmem_limit_bytes=mib * MIB)


def cost(mib, flops):
    return pl.CostEstimate(flops=flops, bytes_accessed=mib * MIB, transcendentals=0)


def by_rows(first, last, body, count=UNROLL):
    def step(i, carry):
        for j in range(count):
            body(first + i * count + j)
        return carry

    lax.fori_loop(0, (last - first) // count, step, 0)


def homes_and_ranks(owner_ref, count_ref):
    for home in range(count_ref.shape[0]):
        count_ref[home] = 0
    result = []
    for slot in range(owner_ref.shape[1]):
        home = owner_ref[0, slot]
        rank = count_ref[home]
        count_ref[home] = rank + 1
        result.append((home, rank))
    return result


def pack_level_kernel(
    owner_hbm, slab_hbm, phi_ref, out_ref, owner_ref, slab_ref, phi, tags, count_ref, load_sem, sem, tag_sem
):
    slots, rows, lanes = phi_ref.shape
    loads = [
        pltpu.make_async_copy(phi_ref.at[slot], phi.at[slot], load_sem.at[slot])
        for slot in range(slots)
    ]
    scalars = [
        pltpu.make_async_copy(owner_hbm, owner_ref, load_sem.at[slots]),
        pltpu.make_async_copy(slab_hbm, slab_ref, load_sem.at[slots + 1]),
    ]
    for load in scalars + loads:
        load.start()
    tags[...] = jnp.zeros_like(tags)
    for load in scalars:
        load.wait()
    places = homes_and_ranks(owner_ref, count_ref)
    for slot, (home, rank) in enumerate(places):
        label = (slab_ref[0, slot] + 1).astype(F32)
        tags[home, pl.ds(rank, 1), :] = jnp.full((1, lanes), label, F32)
    copies = [pltpu.make_async_copy(tags, out_ref.at[:, pl.ds(CAP * rows, EXTRA)], tag_sem)]
    copies[0].start()
    for slot, (home, rank) in enumerate(places):
        loads[slot].wait()
        copy = pltpu.make_async_copy(
            phi.at[slot],
            out_ref.at[home, pl.ds(pl.multiple_of(rank * rows, rows), rows)],
            sem.at[slot],
        )
        copy.start()
        copies.append(copy)
    for copy in copies:
        copy.wait()


def shift_rows(values, step, row):
    rows = values.shape[0]
    moved = pltpu.roll(values, step % rows, 0)
    return jnp.where(row == (0 if step == 1 else rows - 1), 0.0, moved)


def shift_lanes(values, step, lane):
    lanes = values.shape[1]
    moved = pltpu.roll(values, step % lanes, 1)
    return jnp.where(lane == (0 if step == 1 else lanes - 1), 0.0, moved)


def reinit_kernel(
    owner_ref, phi_hbm, seed_hbm, vel_hbm, out_ref, low_ref, high_ref,
    phi_ref, seed_ref, hold, vel_low, vel_high, count_ref, place_ref, load_sem, vel_sem, sem,
):
    slots, rows, lanes = phi_ref.shape

    def load(step, which):
        part = pl.ds(step * REINIT_UNROLL, REINIT_UNROLL)
        src, dst = ((phi_hbm, phi_ref), (seed_hbm, seed_ref))[which]
        return pltpu.make_async_copy(src.at[part], dst.at[part], load_sem.at[which, step])

    for step in range(slots // REINIT_UNROLL):
        load(step, 0).start()
        load(step, 1).start()
    cells = vel_hbm.shape[0]
    vel_copies = [
        pltpu.make_async_copy(vel_hbm.at[:, pl.ds(0, 8)], vel_low, vel_sem.at[0]),
        pltpu.make_async_copy(vel_hbm.at[:, pl.ds(rows - 8, 8)], vel_high, vel_sem.at[1]),
    ]
    for copy in vel_copies:
        copy.start()
    for slot, (home, rank) in enumerate(homes_and_ranks(owner_ref, count_ref)):
        place_ref[slot] = home * CAP + rank
    row = lax.broadcasted_iota(I32, (rows, lanes), 0)
    lane = lax.broadcasted_iota(I32, (rows, lanes), 1)
    low_ref[...] = jnp.zeros_like(low_ref)
    high_ref[...] = jnp.zeros_like(high_ref)

    def out_copy(slot):
        place = place_ref[slot]
        return pltpu.make_async_copy(
            hold.at[slot],
            out_ref.at[place // CAP, pl.ds(pl.multiple_of((place % CAP) * rows, rows), rows)],
            sem.at[slot],
        )

    def block(slot):
        phi = phi_ref[slot]
        up_y = jnp.where(row == rows - 1, phi, pltpu.roll(phi, rows - 1, 0))
        low_y = jnp.where(row == 0, phi, pltpu.roll(phi, 1, 0))
        up_z = jnp.where(lane == lanes - 1, phi, pltpu.roll(phi, lanes - 1, 1))
        low_z = jnp.where(lane == 0, phi, pltpu.roll(phi, 1, 1))
        grad_y = 0.5 * (up_y - low_y)
        grad_z = 0.5 * (up_z - low_z)
        normal = jnp.sqrt(grad_y * grad_y + grad_z * grad_z + 1.0)
        sign = phi / jnp.sqrt(phi * phi + 1.0)
        scale = (0.5 * REINIT_STEP) * sign / normal
        weight_y = scale * grad_y
        weight_z = scale * grad_z
        adjoint = seed_ref[slot]
        for _ in range(REINIT):
            flux_y = weight_y * adjoint
            flux_z = weight_z * adjoint
            adjoint = adjoint + (
                (shift_rows(flux_y, -1, row) - shift_rows(flux_y, 1, row))
                + (shift_lanes(flux_z, -1, lane) - shift_lanes(flux_z, 1, lane))
            )
        heaviside = jnp.tanh(phi / SMEAR_WIDTH)
        hold[slot] = adjoint * (0.5 / SMEAR_WIDTH * (1.0 - heaviside * heaviside))

    def body(step, carry):
        load(step, 0).wait()
        load(step, 1).wait()
        for j in range(REINIT_UNROLL):
            block(step * REINIT_UNROLL + j)
        for j in range(REINIT_UNROLL):
            slot = step * REINIT_UNROLL + j
            out_copy(slot).start()
            place = place_ref[slot]
            first = (place // CAP) * EXTRA + place % CAP
            high_ref[pl.ds(first, 1), :] = hold[slot, rows - 1 : rows, :]
            low_ref[pl.ds(first + CAP, 1), :] = hold[slot, 0:1, :]
        return carry

    lax.fori_loop(0, slots // REINIT_UNROLL, body, 0)
    for copy in vel_copies:
        copy.wait()
    behind = low_ref.shape[0] - cells

    def vel_lines(x):
        low_ref[pl.ds(behind + x, 1), :] = vel_low[x, 0:1, :]
        high_ref[pl.ds(behind + x, 1), :] = vel_high[x, 7:8, :]

    by_rows(0, cells, vel_lines)
    for slot in range(slots):
        out_copy(slot).wait()


def pack_lines_kernel(below_ref, above_ref, forcing_ref, out_ref, hold, sem):
    for home in range(hold.shape[0]):
        part = pl.ds(home * EXTRA, EXTRA)
        hold[home] = below_ref[part, :] + above_ref[part, :]
    copy = pltpu.make_async_copy(
        hold, out_ref.at[:, pl.ds(out_ref.shape[1] - EXTRA, EXTRA)], sem
    )
    copy.start()
    copy.wait()


def neighbours(buffer, x, first, rows, lane):
    here = buffer[x + 1, pl.ds(PAD + first, rows), :]
    low_x = buffer[x, pl.ds(PAD + first, rows), :]
    up_x = buffer[x + 2, pl.ds(PAD + first, rows), :]
    low_y = buffer[x + 1, pl.ds(PAD + first - 1, rows), :]
    up_y = buffer[x + 1, pl.ds(PAD + first + 1, rows), :]
    low_z = shift_lanes(here, 1, lane)
    up_z = shift_lanes(here, -1, lane)
    return here, low_x, up_x, low_y, up_y, low_z, up_z


def operator(fields, flags, rate, keep=1.0):
    here, low_x, up_x, low_y, up_y, low_z, up_z = fields
    upwind = (
        jnp.where((flags & 1) != 0, low_x, up_x)
        + jnp.where((flags & 2) != 0, low_y, up_y)
        + jnp.where((flags & 4) != 0, low_z, up_z)
    )
    total = (low_x + up_x) + (low_y + up_y) + (low_z + up_z)
    return (keep - 6.0 * DIFFUSION) * here + rate * (upwind - 3.0 * here) + DIFFUSION * total


def chunk_copy(src, dst, sem, c):
    part = pl.ds(c * CHUNK, CHUNK)
    return pltpu.make_async_copy(src.at[part], dst.at[part], sem.at[c])


def first_kernel(
    odd_ref, vel_ref, flags_ref, phi_ref, level_ref, xfirst_ref, xsecond_ref, ylow_ref, yhigh_ref,
    code_out, twice_out, edge_x_ref, edge_ylow_ref, edge_yhigh_ref, coef_ref, table_ref,
    vel, once, flags, rate, code, twice, tags, sem_tags, sem_vel, sem_flags, sem_phi, sem_code, sem_twice,
):
    cells, rows, lanes = flags.shape
    chunks = cells // CHUNK

    def vel_copy(c):
        return pltpu.make_async_copy(
            vel_ref.at[pl.ds(c * CHUNK, CHUNK)],
            vel.at[pl.ds(1 + c * CHUNK, CHUNK), pl.ds(PAD, rows)],
            sem_vel.at[c],
        )

    def flags_copy(c):
        return chunk_copy(flags_ref, flags, sem_flags, c)

    def code_copy(c):
        return chunk_copy(code, code_out, sem_code, c)

    def twice_copy(c):
        return chunk_copy(twice, twice_out, sem_twice, c)

    tag_copy = pltpu.make_async_copy(level_ref.at[:, pl.ds(CAP * rows, EXTRA)], tags, sem_tags)
    tag_copy.start()

    def start_loads(c, carry):
        vel_copy(c).start()
        flags_copy(c).start()
        return carry

    lax.fori_loop(0, chunks, start_loads, 0)
    for x in range(cells):
        table_ref[x] = -1
    tag_copy.wait()
    for source in range(tags.shape[0]):
        for rank in range(CAP):
            tag = tags[source, rank, 0].astype(I32)

            @pl.when(tag > 0)
            def _():
                table_ref[tag - 1] = source * CAP + rank

    def start(c, carry):
        for j in range(CHUNK):
            x = c * CHUNK + j
            slot = table_ref[x]

            @pl.when(slot >= 0)
            def _():
                pltpu.make_async_copy(
                    block_of(level_ref, slot, rows), rate.at[x], sem_phi.at[c]
                ).start()

            @pl.when(slot < 0)
            def _():
                pltpu.make_async_copy(phi_ref.at[x], rate.at[x], sem_phi.at[c]).start()

        return carry

    lax.fori_loop(0, chunks, start, 0)

    lane = lax.broadcasted_iota(I32, (STRIP, lanes), 1)
    zeros = jnp.zeros((rows + 2 * PAD, lanes), F32)
    odd = odd_ref[0] == 1
    vel[0, pl.ds(PAD, rows), :] = jnp.where(odd, xfirst_ref[0], xsecond_ref[0])
    vel[cells + 1, pl.ds(PAD, rows), :] = jnp.where(odd, xsecond_ref[0], xfirst_ref[0])
    once[0] = zeros
    once[cells + 1] = zeros
    line_zero = jnp.zeros((PAD, lanes), F32)

    behind = ylow_ref.shape[0] - cells

    def lines(x):
        vel[x + 1, PAD - 1 : PAD, :] = ylow_ref[pl.ds(behind + x, 1), :]
        vel[x + 1, PAD + rows : PAD + rows + 1, :] = yhigh_ref[pl.ds(behind + x, 1), :]
        once[x + 1, 0:PAD, :] = line_zero
        once[x + 1, PAD + rows : PAD + rows + PAD, :] = line_zero
        slot = jnp.full((1, lanes), table_ref[x].astype(F32), F32)
        edge_ylow_ref[pl.ds(cells + x, 1), :] = slot
        edge_yhigh_ref[pl.ds(cells + x, 1), :] = slot

    by_rows(0, cells, lines)

    def update_once(x):
        for first in range(0, rows, STRIP):
            part = pl.ds(first, STRIP)
            heaviside = jnp.tanh(rate[x, part, :] * (1.0 / SMEAR_WIDTH))
            density = (AIR_DENSITY + 0.5 * (1.0 - AIR_DENSITY)) + (0.5 * (1.0 - AIR_DENSITY)) * heaviside
            rate_here = ADV_RATE / density
            bits = flags[x, part, :]
            rate[x, part, :] = rate_here
            code[x, part, :] = bits.astype(F32) + rate_here
            once[x + 1, pl.ds(PAD + first, STRIP), :] = operator(
                neighbours(vel, x, first, STRIP, lane), bits, rate_here
            )

    def update_twice(x):
        for first in range(0, rows, STRIP):
            part = pl.ds(first, STRIP)
            twice[x, part, :] = operator(
                neighbours(once, x, first, STRIP, lane), flags[x, part, :], rate[x, part, :]
            )

    def second_pass(c):
        for j in range(CHUNK):
            update_twice(c * CHUNK + j)
        twice_copy(c).start()

    vel_copy(0).wait()

    def first_pass(c, carry):
        @pl.when(c + 1 < chunks)
        def _():
            vel_copy(c + 1).wait()

        flags_copy(c).wait()
        chunk_copy(phi_ref, rate, sem_phi, c).wait()
        for j in range(CHUNK):
            update_once(c * CHUNK + j)
        code_copy(c).start()

        @pl.when(c > 0)
        def _():
            second_pass(c - 1)

        return carry

    lax.fori_loop(0, chunks, first_pass, 0)
    second_pass(chunks - 1)
    edge_x_ref[0] = once[1, pl.ds(PAD, rows), :]
    edge_x_ref[1] = once[cells, pl.ds(PAD, rows), :]
    coef_ref[0] = DIFFUSION + jnp.where((flags[0] & 1) != 0, rate[0], 0.0)
    coef_ref[1] = DIFFUSION + jnp.where((flags[cells - 1] & 1) != 0, 0.0, rate[cells - 1])

    def edge_lines(x):
        edge_ylow_ref[pl.ds(x, 1), :] = once[x + 1, PAD : PAD + 1, :]
        edge_yhigh_ref[pl.ds(x, 1), :] = once[x + 1, PAD + rows - 1 : PAD + rows, :]

    by_rows(0, cells, edge_lines)

    for c in range(chunks):
        code_copy(c).wait()
        twice_copy(c).wait()


def block_of(ref, slot, rows):
    return ref.at[slot // CAP, pl.ds(pl.multiple_of((slot % CAP) * rows, rows), rows)]


def edge_kernel(odd_ref, table_ref, edge_ref, forcing_ref, first_out, second_out):
    rows = first_out.shape[1]
    odd = odd_ref[0]
    for side, x in enumerate((0, table_ref.shape[0] - 1)):
        slot = table_ref[x]
        safe = jnp.maximum(slot, 0)
        slab = edge_ref[side] + jnp.where(
            slot >= 0, block_of(forcing_ref, safe, rows)[...], 0.0
        )

        @pl.when(odd != side)
        def _():
            first_out[0] = slab

        @pl.when(odd == side)
        def _():
            second_out[0] = slab


def last_kernel(
    table_ref, below_ref, above_ref, forcing_ref, code_ref, twice_ref, ylow_ref, yhigh_ref,
    out_ref, part_ref, source, code, twice, sem_code, sem_twice, sem_out,
):
    cells, rows, lanes = code.shape
    chunks = cells // CHUNK
    loads = ((code_ref, code, sem_code), (twice_ref, twice, sem_twice))

    def start(c, carry):
        for load in loads:
            chunk_copy(*load, c).start()
        return carry

    lax.fori_loop(0, chunks, start, 0)
    zeros = jnp.zeros((rows, lanes), F32)
    source[0, pl.ds(PAD, rows), :] = zeros
    source[cells + 1, pl.ds(PAD, rows), :] = zeros

    def fill(x):
        slot = table_ref[x]
        safe = jnp.maximum(slot, 0)
        source[x + 1, pl.ds(PAD, rows), :] = jnp.where(
            slot >= 0, block_of(forcing_ref, safe, rows)[...], 0.0
        )
        for side, slots, halo, at in (
            (0, below_ref, ylow_ref, PAD - 1),
            (1, above_ref, yhigh_ref, PAD + rows),
        ):
            line_slot = slots[x]
            safe = jnp.maximum(line_slot, 0)
            line = forcing_ref[safe // CAP, pl.ds(CAP * rows + side * CAP + safe % CAP, 1), :]
            source[x + 1, at : at + 1, :] = halo[pl.ds(x, 1), :] + jnp.where(
                line_slot >= 0, line, 0.0
            )

    lane = lax.broadcasted_iota(I32, (STRIP, lanes), 1)

    def update(x):
        for first in range(0, rows, STRIP):
            part = pl.ds(first, STRIP)
            fields = neighbours(source, x, first, STRIP, lane)
            both = code[x, part, :]
            bits = both.astype(I32)
            twice[x, part, :] = twice[x, part, :] + operator(
                fields, bits, both - bits.astype(F32), keep=2.0
            )

    by_rows(0, cells, fill, 8)

    def work(c, carry):
        for load in loads:
            chunk_copy(*load, c).wait()
        for j in range(CHUNK):
            update(c * CHUNK + j)
        chunk_copy(twice, out_ref, sem_out, c).start()
        return carry

    lax.fori_loop(0, chunks, work, 0)
    part_ref[0] = twice[0]
    part_ref[1] = twice[cells - 1]
    for c in range(chunks):
        chunk_copy(twice, out_ref, sem_out, c).wait()


def close_kernel(odd_ref, part_ref, coef_ref, first_ref, second_ref, whole_ref, out_ref, hold, sem):
    cells = out_ref.shape[0]
    odd = odd_ref[0] == 1
    hold[0] = part_ref[0] + coef_ref[0] * jnp.where(odd, first_ref[0], second_ref[0])
    hold[1] = part_ref[1] + coef_ref[1] * jnp.where(odd, second_ref[0], first_ref[0])
    copies = [
        pltpu.make_async_copy(hold.at[0], out_ref.at[0], sem.at[0]),
        pltpu.make_async_copy(hold.at[1], out_ref.at[cells - 1], sem.at[1]),
    ]
    for copy in copies:
        copy.start()
    for copy in copies:
        copy.wait()


def neighbour_pairs(axis):
    count = lax.axis_size(axis)
    forward = [(i, i + 1) for i in range(count - 1)]
    return forward, [(target, source) for source, target in forward]


def swaps(axis, first):
    low = range(first, lax.axis_size(axis) - 1, 2)
    return [(i, i + 1) for i in low] + [(i + 1, i) for i in low]


def local(band_phi, band_seed, owner_map, active_list, brick_phi, adjoint_vel, upwind_flags):
    gx_count = lax.axis_size("gx")
    slots, rows, lanes = band_phi.shape
    cells = brick_phi.shape[0]
    chunks = cells // CHUNK
    up_x, down_x = neighbour_pairs("gx")
    up_y, down_y = neighbour_pairs("gy")
    shape = jax.ShapeDtypeStruct
    dma = pltpu.SemaphoreType.DMA
    brick = (cells, rows, lanes)
    padded = (cells + 2, rows + 2 * PAD, lanes)
    sent = (gx_count, CAP * rows + EXTRA, lanes)
    owners, slabs = owner_map.T, active_list.T

    level_sent = pl.pallas_call(
        pack_level_kernel,
        out_shape=shape(sent, F32),
        in_specs=[HBM, HBM, HBM],
        out_specs=HBM,
        scratch_shapes=[
            pltpu.SMEM((1, slots), I32),
            pltpu.SMEM((1, slots), I32),
            pltpu.VMEM((slots, rows, lanes), F32),
            pltpu.VMEM((gx_count, EXTRA, lanes), F32),
            pltpu.SMEM((gx_count,), I32),
            dma((slots + 2,)), dma((slots,)), dma(()),
        ],
        compiler_params=params(BIG),
        cost_estimate=cost(2, 1000),
        name="pack_level",
    )(owners, slabs, band_phi)
    level = lax.all_to_all(level_sent, "gx", split_axis=0, concat_axis=0, tiled=True)

    lines = (gx_count * EXTRA + cells, lanes)
    odd_x = lax.axis_index("gx") % 2
    odd = odd_x.astype(I32).reshape(1)
    v_first = lax.dynamic_slice_in_dim(adjoint_vel, jnp.where(odd_x == 1, 0, cells - 1), 1)
    v_second = lax.dynamic_slice_in_dim(adjoint_vel, jnp.where(odd_x == 1, cells - 1, 0), 1)
    v_first = lax.ppermute(v_first, "gx", swaps("gx", 0))
    v_second = lax.ppermute(v_second, "gx", swaps("gx", 1))
    forcing_sent, low_lines, high_lines = pl.pallas_call(
        reinit_kernel,
        out_shape=(shape(sent, F32), shape(lines, F32), shape(lines, F32)),
        in_specs=[SMEM, HBM, HBM, HBM],
        out_specs=(HBM, VMEM, VMEM),
        scratch_shapes=[
            pltpu.VMEM((slots, rows, lanes), F32),
            pltpu.VMEM((slots, rows, lanes), F32),
            pltpu.VMEM((slots, rows, lanes), F32),
            pltpu.VMEM((cells, 8, lanes), F32),
            pltpu.VMEM((cells, 8, lanes), F32),
            pltpu.SMEM((gx_count,), I32),
            pltpu.SMEM((slots,), I32),
            dma((2, slots // REINIT_UNROLL)), dma((2,)), dma((slots,)),
        ],
        compiler_params=params(BIG),
        cost_estimate=cost(20, 40_000_000),
        name="reinit",
    )(owners, band_phi, band_seed, adjoint_vel)
    below_lines = lax.ppermute(high_lines, "gy", up_y)
    above_lines = lax.ppermute(low_lines, "gy", down_y)
    v_first, v_second, below_lines, above_lines = lax.optimization_barrier(
        (v_first, v_second, below_lines, above_lines)
    )
    forcing_sent = pl.pallas_call(
        pack_lines_kernel,
        out_shape=shape(sent, F32),
        in_specs=[VMEM, VMEM, HBM],
        out_specs=HBM,
        scratch_shapes=[pltpu.VMEM((gx_count, EXTRA, lanes), F32), dma(())],
        input_output_aliases={2: 0},
        compiler_params=params(MEDIUM),
        cost_estimate=cost(2, 1000),
        name="pack_lines",
    )(below_lines, above_lines, forcing_sent)
    forcing = lax.all_to_all(forcing_sent, "gx", split_axis=0, concat_axis=0, tiled=True)

    edge_lines = (2 * cells, lanes)
    code, twice, edge_x, edge_ylow, edge_yhigh, coef, table = pl.pallas_call(
        first_kernel,
        out_shape=(
            shape(brick, F32),
            shape(brick, F32),
            shape((2, rows, lanes), F32),
            shape(edge_lines, F32),
            shape(edge_lines, F32),
            shape((2, rows, lanes), F32),
            shape((cells,), I32),
        ),
        in_specs=[SMEM, HBM, HBM, HBM, HBM, VMEM, VMEM, VMEM, VMEM],
        out_specs=(HBM, HBM, VMEM, VMEM, VMEM, VMEM, SMEM),
        scratch_shapes=[
            pltpu.VMEM(padded, F32),
            pltpu.VMEM(padded, F32),
            pltpu.VMEM(brick, I32),
            pltpu.VMEM(brick, F32),
            pltpu.VMEM(brick, F32),
            pltpu.VMEM(brick, F32),
            pltpu.SMEM((gx_count, EXTRA, lanes), F32),
            dma(()),
            dma((chunks,)), dma((chunks,)), dma((chunks,)), dma((chunks,)), dma((chunks,)),
        ],
        compiler_params=params(ROOMY),
        cost_estimate=cost(30, 60_000_000),
        name="two_updates",
    )(odd, adjoint_vel, upwind_flags, brick_phi, level, v_first, v_second, below_lines, above_lines)
    once_ylow = lax.ppermute(edge_yhigh, "gy", up_y)
    once_yhigh = lax.ppermute(edge_ylow, "gy", down_y)
    gy = lax.axis_index("gy")
    below = jnp.where(gy > 0, once_ylow[cells:, 0].astype(I32), -1)
    above = jnp.where(gy < lax.axis_size("gy") - 1, once_yhigh[cells:, 0].astype(I32), -1)

    edge_x, below, above = lax.optimization_barrier((edge_x, below, above))

    first_slab, second_slab = pl.pallas_call(
        edge_kernel,
        out_shape=(shape((1, rows, lanes), F32), shape((1, rows, lanes), F32)),
        in_specs=[SMEM, SMEM, VMEM, VMEM],
        out_specs=(VMEM, VMEM),
        compiler_params=params(SMALL),
        cost_estimate=cost(1, 1000),
        name="edge_slabs",
    )(odd, table, edge_x, forcing)
    first_got = lax.ppermute(first_slab, "gx", swaps("gx", 0))
    second_got = lax.ppermute(second_slab, "gx", swaps("gx", 1))

    out, part = pl.pallas_call(
        last_kernel,
        out_shape=(shape(brick, F32), shape((2, rows, lanes), F32)),
        in_specs=[SMEM, SMEM, SMEM, VMEM, HBM, HBM, VMEM, VMEM],
        out_specs=(HBM, VMEM),
        scratch_shapes=[
            pltpu.VMEM(padded, F32),
            pltpu.VMEM(brick, F32),
            pltpu.VMEM(brick, F32),
            dma((chunks,)), dma((chunks,)), dma((chunks,)),
        ],
        compiler_params=params(ROOMY),
        cost_estimate=cost(30, 60_000_000),
        name="add_forcing",
    )(table, below, above, forcing, code, twice, once_ylow, once_yhigh)

    return pl.pallas_call(
        close_kernel,
        out_shape=shape(brick, F32),
        in_specs=[SMEM, VMEM, VMEM, VMEM, VMEM, HBM],
        out_specs=HBM,
        scratch_shapes=[pltpu.VMEM((2, rows, lanes), F32), dma((2,))],
        input_output_aliases={5: 0},
        compiler_params=params(SMALL),
        cost_estimate=cost(1, 1000),
        name="close_slabs",
    )(odd, part, coef, first_got, second_got, out)


def solution(mesh):
    in_specs = (
        P("gx", "gy", None),
        P("gx", "gy", None),
        P("gx", "gy"),
        P("gx", "gy"),
        P("gx", "gy", None),
        P("gx", "gy", None),
        P("gx", "gy", None),
    )
    out_specs = P("gx", "gy", None)
    return jax.shard_map(local, mesh=mesh, in_specs=in_specs, out_specs=out_specs, check_vma=False)
```
